32 devices in a mesh: walk: 2 (over x), param: 16 (over z, y, core).
Axes of the slice: x: 2, y: 2, z: 4, core: 2. Of those that a mesh axis runs over, the one named last changes fastest.
Arguments:
- jacobian: float32 [256, 151552], P('walk', 'param'), may hold values from -0.33445946 to 0.33445946, as said below
- energies: float32 [256], P('walk'), may hold values from -6 to 6
- shifts: float32 [8], replicated, may hold values from 6.5983954e-06 to 0.00019795186
Outputs:
- update: float32 [8, 151552], P(None, 'param')
The draws below stay inside these ranges and needn't reach their ends.
Inputs may be any that keep to these rules, and one draw needn't show every extreme that they name: `jacobian`: Real-valued entries of both signs.
All inputs are finite; a program needn't handle non-finite values.
Results may differ from the reference program's by a relative error of at most 0.00028.
Values sent between devices are 32-bit elements; how exact they have to be, the bound alone decides.
No kernel may reach another device: no remote copies, remote signals or barrier semaphores. Data moves between devices by JAX's collectives and lax.ppermute only.
A program may use at most 64 MiB of HBM per device.

```python
import math
import jax
import jax.numpy as jnp
from jax import lax

SHIFTS = 8
ITERS = 3
WALKERS = 256
PARAMS = 151552


def draw_jacobian(key, part):
    key_noise, key_rows, key_cols, key_offset = jax.random.split(key, 4)
    walk_pos = jnp.arange(WALKERS, dtype=jnp.float32) / WALKERS
    param_pos = jnp.arange(PARAMS, dtype=jnp.float32) / PARAMS
    base_scale = jnp.sqrt(jnp.float32(WALKERS)) / (20.0 * PARAMS)
    col_offset = jax.random.truncated_normal(key_offset, -4.0, 4.0, (PARAMS,), jnp.float32)
    ramp_log = jnp.log(3.0)
    noise_draw = jax.random.truncated_normal(key_noise, -4.0, 4.0, (WALKERS, PARAMS), jnp.float32)
    row_scale = jnp.exp(jax.random.uniform(key_rows, (WALKERS,), jnp.float32) * jnp.log(10.0) + ramp_log * walk_pos)
    col_scale = jnp.exp(jax.random.uniform(key_cols, (PARAMS,), jnp.float32) * jnp.log(10.0) + ramp_log * param_pos)
    inner = row_scale[:, None] * noise_draw + col_offset[None, :]
    return (base_scale * col_scale[None, :] * inner).astype(jnp.float32)


def block_scale(stream_key, extent, cuts, low, high):
    loudness, own = 1.0, jax.random.fold_in(stream_key, 6)
    for dim, shards_of in cuts:
        draws = jnp.exp(jax.random.uniform(jax.random.fold_in(own, dim), (shards_of,), jnp.float32, low / len(cuts), high / len(cuts)))
        loudness = loudness * jnp.repeat(draws, extent[dim] // shards_of).reshape([-1 if axis == dim else 1 for axis in range(len(extent))])
    return loudness


def scatter_about(stream_key, extent, width, reach, shards=(), kind=jnp.bfloat16):
    entries = width * jax.random.normal(stream_key, extent, jnp.float32)
    if shards:
        entries = entries * block_scale(stream_key, extent, shards, -0.22, 0.18)
    return jnp.clip(entries, -reach, reach).astype(kind)


def setup_inputs(seed: int = 0) -> dict:
    splits = jax.random.split(jax.random.key(seed), 4)
    return {
        "jacobian": draw_jacobian(jax.random.fold_in(splits[3], 71), 0),
        "energies": scatter_about(splits[1], (WALKERS,), 1.0, 6.0, ((0, 2),), jnp.float32),
        "shifts": jnp.clip(jnp.exp(jax.random.uniform(splits[2], (SHIFTS,), jnp.float32, math.log(6.5983954300463665e-06), math.log(0.00019795186))), 6.5983954300463665e-06, 0.00019795186),
    }


highest = lax.Precision.HIGHEST

def reference(jacobian, energies, shifts):
    walkers = jacobian.shape[0]
    column_mean = lax.optimization_barrier(jnp.sum(jacobian, axis=0)) / walkers
    energy_dev = energies - jnp.sum(energies) / walkers
    gradient = (jnp.dot(energy_dev, jacobian, precision=highest) - column_mean * jnp.sum(energy_dev)) / walkers

    def operate(direction):
        projected = lax.dot_general(direction, jacobian, (((1,), (1,)), ((), ())), precision=highest)
        projected = projected - jnp.dot(direction, column_mean, precision=highest)[:, None]
        back_terms = jnp.dot(projected, jacobian, precision=highest)
        return back_terms / walkers + shifts[:, None] * direction
    residual = jnp.broadcast_to(gradient[None, :], (shifts.shape[0], jacobian.shape[1]))
    direction = residual
    solution = jnp.zeros_like(residual)
    norm_now = lax.optimization_barrier(jnp.sum(residual * residual, axis=1))
    for number in range(ITERS):
        applied = operate(direction)
        step_size = norm_now / lax.optimization_barrier(jnp.sum(direction * applied, axis=1))
        solution = solution + step_size[:, None] * direction
        residual = residual - step_size[:, None] * applied
        norm_next = lax.optimization_barrier(jnp.sum(residual * residual, axis=1))
        direction = residual + (norm_next / norm_now)[:, None] * direction
        norm_now = norm_next
    norm_scale = lax.rsqrt(lax.optimization_barrier(jnp.mean(solution * solution, axis=1)) + 1e-06)
    return solution * norm_scale[:, None]
```

```python
import functools

import jax
import jax.numpy as jnp
from jax import lax
from jax.experimental import pallas as pl
from jax.experimental.pallas import tpu as pltpu
from jax.sharding import PartitionSpec as P

LANES = 128
TINY = 1e-37
epsilon = 1e-06


def over_lanes(values):
    total = jnp.sum(values, axis=1, keepdims=True)
    return jnp.broadcast_to(total, (values.shape[0], LANES))


def tree_sum(terms):
    terms = list(terms)
    while len(terms) > 1:
        terms = [a + b for a, b in zip(terms[0::2], terms[1::2])]
    return terms[0]


def down_rows(row):
    return jnp.transpose(jnp.broadcast_to(row, (row.shape[1], row.shape[1])))


def tiles(count, step):
    def run(number, carry):
        return step(pl.multiple_of(number * LANES, LANES), carry)

    return run


def mean_and_dev(row):
    mean = over_lanes(row) / row.shape[1]
    return mean, row - mean


def first_kernel(jac_ref, energy_ref, msg_ref):
    cols = jac_ref.shape[1]
    mean, dev = mean_and_dev(energy_ref[...])
    weight = down_rows(dev)

    def step(at, carry):
        block = jac_ref[:, pl.ds(at, LANES)]
        msg_ref[0:1, pl.ds(at, LANES)] = jnp.sum(block * weight, axis=0, keepdims=True)
        msg_ref[1:2, pl.ds(at, LANES)] = jnp.sum(block, axis=0, keepdims=True)
        return carry

    lax.fori_loop(0, cols // LANES, tiles(cols, step), 0, unroll=2)
    msg_ref[0:1, cols : cols + LANES] = mean
    msg_ref[1:2, cols : cols + LANES] = mean


def back_kernel(parts, jac_ref, *refs):
    part_refs, (msg_ref, norm_ref) = refs[:parts], refs[parts:]
    cols = jac_ref.shape[1]
    total = tree_sum([ref[...] for ref in part_refs])
    mean, dev = mean_and_dev(total[0:1])
    weight = down_rows(dev)

    def step(at, carry):
        block = jac_ref[:, pl.ds(at, LANES)]
        msg_ref[:, pl.ds(at, LANES)] = jnp.sum(block * weight, axis=0, keepdims=True)
        return carry

    lax.fori_loop(0, cols // LANES, tiles(cols, step), 0, unroll=2)
    msg_ref[:, cols : cols + LANES] = mean
    msg_ref[:, cols + LANES : cols + 2 * LANES] = over_lanes(dev * dev)
    norm_ref[...] = total[1:2]


def spread(means, squares, rows):
    centre = sum(means) / len(means)
    offsets = [mean - centre for mean in means]
    total = tree_pairs(squares)
    return offsets, total + rows * tree_pairs([offset * offset for offset in offsets])


def tree_pairs(terms):
    total = terms[0]
    for term in terms[1:]:
        total = total + term
    return total


def shifted(offsets, sums):
    if len(sums) == 2:
        return offsets[0] * (sums[0] - sums[1])
    return tree_pairs([offset * term for offset, term in zip(offsets, sums)])


def load_tile(ref, row, at):
    return ref[row : row + 1, pl.ds(at, LANES)]


def combine_project(groups, jac_ref, firsts, msgs, offsets, scale, olds, vector_ref, part_ref):
    rows, cols = jac_ref.shape

    def step(at, carry):
        acc, square = carry
        value = tree_pairs([load_tile(ref, 0, at) for ref in msgs])
        value = value + shifted(offsets, [load_tile(ref, 1, at) for ref in firsts])
        value = value * scale
        for factor, ref in olds:
            value = value - factor * load_tile(ref, 0, at)
        vector_ref[:, pl.ds(at, LANES)] = value
        return acc + jac_ref[:, pl.ds(at, LANES)] * value, square + value * value

    zeros = jnp.zeros((rows, LANES), jnp.float32), jnp.zeros((1, LANES), jnp.float32)
    acc, square = lax.fori_loop(0, cols // LANES, tiles(cols, step), zeros, unroll=2)
    part_ref[0:1] = jnp.sum(jnp.transpose(acc), axis=0, keepdims=True)
    part_ref[1:2] = over_lanes(square)


def project_zero(groups, walkers, jac_ref, *refs):
    firsts, (vector_ref, part_ref) = refs[:groups], refs[groups:]
    rows, cols = jac_ref.shape
    means = [ref[0:1, cols : cols + LANES] for ref in firsts]
    offsets, _ = spread(means, means, rows)
    scale = jnp.full((1, LANES), 1.0 / walkers, jnp.float32)
    combine_project(groups, jac_ref, firsts, firsts, offsets, scale, [], vector_ref, part_ref)


def msg_spread(msgs, rows, cols):
    means = [ref[:, cols : cols + LANES] for ref in msgs]
    squares = [ref[:, cols + LANES : cols + 2 * LANES] for ref in msgs]
    return spread(means, squares, rows)


def project_one(groups, walkers, jac_ref, *refs):
    firsts, msgs, refs = refs[:groups], refs[groups : 2 * groups], refs[2 * groups :]
    norm_ref, old_ref, vector_ref, part_ref, state_ref = refs
    rows, cols = jac_ref.shape
    offsets, square = msg_spread(msgs, rows, cols)
    alpha = square / (walkers * jnp.maximum(norm_ref[...], TINY))
    scale = 1.0 / (walkers * jnp.maximum(alpha, TINY))
    state_ref[0:1] = alpha
    state_ref[1:2] = scale
    one = jnp.ones((1, LANES), jnp.float32)
    combine_project(
        groups, jac_ref, firsts, msgs, offsets, scale, [(one, old_ref)], vector_ref, part_ref
    )


def project_two(groups, walkers, jac_ref, *refs):
    firsts, msgs, refs = refs[:groups], refs[groups : 2 * groups], refs[2 * groups :]
    state_ref, norm_old, norm_now, older_ref, old_ref, vector_ref, part_ref, alpha_ref = refs
    rows, cols = jac_ref.shape
    offsets, square = msg_spread(msgs, rows, cols)
    scale = state_ref[1:2]
    norm = jnp.maximum(norm_now[...], TINY)
    alpha = square * scale / norm
    alpha_ref[...] = alpha
    beta = norm_now[...] / jnp.maximum(norm_old[...], TINY)
    combine_project(
        groups,
        jac_ref,
        firsts,
        msgs,
        offsets,
        scale,
        [(alpha, old_ref), (beta, older_ref)],
        vector_ref,
        part_ref,
    )


def final_kernel(groups, parts, params, *refs):
    part_refs, refs = refs[: groups * parts], refs[groups * parts :]
    shift_ref, state_ref, alpha_ref, norm0_ref, norm1_ref = refs[:5]
    vectors, out_ref = refs[5:8], refs[8]
    cols = out_ref.shape[1]
    totals = [
        tree_sum([ref[...] for ref in part_refs[at : at + parts]])
        for at in range(0, groups * parts, parts)
    ]
    rows = totals[0].shape[1]
    pairs = [mean_and_dev(total[0:1]) for total in totals]
    _, square = spread(
        [mean for mean, _ in pairs], [over_lanes(dev * dev) for _, dev in pairs], rows
    )
    norm2 = totals[0][1:2]
    norm0, norm1 = norm0_ref[...], norm1_ref[...]
    alpha0, scale = state_ref[0:1], state_ref[1:2]
    alpha1 = alpha_ref[...]
    alpha2 = square * scale / jnp.maximum(norm2, TINY)
    beta1 = norm1 / jnp.maximum(norm0, TINY)
    beta2 = norm2 / jnp.maximum(norm1, TINY)
    inverse = 1.0 / jnp.maximum(alpha0, TINY)
    shift = shift_ref[...] * inverse
    pivot0 = 1.0 + shift
    pivot1 = (alpha1 + shift) - beta1 / pivot0
    pivot2 = (alpha2 + shift) - beta2 / pivot1
    right1 = -1.0 / pivot0
    right2 = -right1 / pivot1
    coef2 = right2 / pivot2
    coef1 = (right1 - beta2 * coef2) / pivot1
    coef0 = (1.0 - beta1 * coef1) / pivot0
    coef0, coef1, coef2 = coef0 * inverse, coef1 * inverse, coef2 * inverse
    square = coef0 * coef0 * norm0 + coef1 * coef1 * norm1 + coef2 * coef2 * norm2
    factor = lax.rsqrt(square / params + epsilon)
    coefs = [coef0 * factor, coef1 * factor, coef2 * factor]

    def step(at, carry):
        terms = [coef * load_tile(ref, 0, at) for coef, ref in zip(coefs, vectors)]
        out_ref[:, pl.ds(at, LANES)] = terms[0] + terms[1] + terms[2]
        return carry

    lax.fori_loop(0, cols // LANES, tiles(cols, step), 0, unroll=2)


def call(kernel, outs, *args):
    shapes = [jax.ShapeDtypeStruct(shape, jnp.float32) for shape in outs]
    space = pl.BlockSpec(memory_space=pltpu.VMEM)
    return pl.pallas_call(
        kernel,
        out_shape=shapes,
        in_specs=[space] * len(args),
        out_specs=[space] * len(shapes),
        compiler_params=pltpu.CompilerParams(vmem_limit_bytes=24 * 1024 * 1024),
    )(*args)


def from_walk(array, groups):
    others = []
    for hop in range(1, groups):
        pairs = [(index, (index - hop) % groups) for index in range(groups)]
        others.append(lax.ppermute(array, "walk", pairs))
    return [array] + others


def digits(size):
    radices = []
    while size > 1:
        radix = 4 if size % 4 == 0 else 2
        radices.append(radix)
        size //= radix
    return radices


def across(array, size, stride, radix):
    out = [array]
    for mask in range(1, radix):
        pairs = [(index, index ^ (mask * stride)) for index in range(size)]
        out.append(lax.ppermute(array, "param", pairs))
    return out


def from_param(array, size):
    stride = 1
    radices = digits(size)
    for radix in radices[:-1]:
        array = tree_sum(across(array, size, stride, radix))
        stride *= radix
    return across(array, size, stride, radices[-1])


def body(jacobian, energies, shifts):
    rows, cols = jacobian.shape
    groups, shards = lax.axis_size("walk"), lax.axis_size("param")
    walkers, params = rows * groups, cols * shards
    vector, part, scalar = (1, cols), (2, LANES), (1, LANES)
    shift_rows = jnp.broadcast_to(shifts[:, None], (shifts.shape[0], LANES))

    (msg,) = call(first_kernel, [(2, cols + LANES)], jacobian, energies.reshape(1, rows))
    firsts = from_walk(msg, groups)
    vector0, sent = call(
        functools.partial(project_zero, groups, walkers), [vector, part], jacobian, *firsts
    )
    parts = from_param(sent, shards)
    back = functools.partial(back_kernel, len(parts))
    msg_shape = (1, cols + 2 * LANES)
    msg, norm0 = call(back, [msg_shape, scalar], jacobian, *parts)
    msgs = from_walk(msg, groups)
    vector1, sent, state = call(
        functools.partial(project_one, groups, walkers),
        [vector, part, (2, LANES)],
        jacobian,
        *firsts,
        *msgs,
        norm0,
        vector0,
    )
    parts = from_param(sent, shards)
    msg, norm1 = call(back, [msg_shape, scalar], jacobian, *parts)
    msgs = from_walk(msg, groups)
    vector2, sent, alpha1 = call(
        functools.partial(project_two, groups, walkers),
        [vector, part, scalar],
        jacobian,
        *firsts,
        *msgs,
        state,
        norm0,
        norm1,
        vector0,
        vector1,
    )
    parts = from_param(sent, shards)
    last = from_walk(tree_sum(parts), groups)
    (update,) = call(
        functools.partial(final_kernel, groups, 1, params),
        [(shifts.shape[0], cols)],
        *last,
        shift_rows,
        state,
        alpha1,
        norm0,
        norm1,
        vector0,
        vector1,
        vector2,
    )
    return update


def solution(mesh):
    return jax.shard_map(
        body,
        mesh=mesh,
        in_specs=(P("walk", "param"), P("walk"), P()),
        out_specs=P(None, "param"),
        check_vma=False,
    )
```

```python
import functools

import jax
import jax.numpy as jnp
from jax import lax
from jax.experimental import pallas as pl
from jax.experimental.pallas import tpu as pltpu
from jax.sharding import PartitionSpec as P

LANES = 128
TINY = 1e-37
epsilon = 1e-06


def over_lanes(values):
    total = jnp.sum(values, axis=1, keepdims=True)
    return jnp.broadcast_to(total, (values.shape[0], LANES))


def tree_sum(terms):
    terms = list(terms)
    while len(terms) > 1:
        terms = [a + b for a, b in zip(terms[0::2], terms[1::2])]
    return terms[0]


def down_rows(row):
    return jnp.transpose(jnp.broadcast_to(row, (row.shape[1], row.shape[1])))


def tiles(count, step):
    def run(number, carry):
        return step(pl.multiple_of(number * LANES, LANES), carry)

    return run


def mean_and_dev(row):
    mean = over_lanes(row) / row.shape[1]
    return mean, row - mean


def first_kernel(jac_ref, energy_ref, msg_ref):
    cols = jac_ref.shape[1]
    mean, dev = mean_and_dev(energy_ref[...])
    weight = down_rows(dev)

    def step(at, carry):
        block = jac_ref[:, pl.ds(at, LANES)]
        msg_ref[0:1, pl.ds(at, LANES)] = jnp.sum(block * weight, axis=0, keepdims=True)
        msg_ref[1:2, pl.ds(at, LANES)] = jnp.sum(block, axis=0, keepdims=True)
        return carry

    lax.fori_loop(0, cols // LANES, tiles(cols, step), 0, unroll=2)
    msg_ref[0:1, cols : cols + LANES] = mean
    msg_ref[1:2, cols : cols + LANES] = mean


def back_kernel(jac_ref, part_ref, msg_ref, norm_ref):
    cols = jac_ref.shape[1]
    total = jnp.sum(part_ref[...], axis=0)
    mean, dev = mean_and_dev(total[0:1])
    weight = down_rows(dev)

    def step(at, carry):
        block = jac_ref[:, pl.ds(at, LANES)]
        msg_ref[:, pl.ds(at, LANES)] = jnp.sum(block * weight, axis=0, keepdims=True)
        return carry

    lax.fori_loop(0, cols // LANES, tiles(cols, step), 0, unroll=2)
    msg_ref[:, cols : cols + LANES] = mean
    msg_ref[:, cols + LANES : cols + 2 * LANES] = over_lanes(dev * dev)
    norm_ref[...] = total[1:2]


def spread(means, squares, rows):
    centre = sum(means) / len(means)
    offsets = [mean - centre for mean in means]
    total = tree_pairs(squares)
    return offsets, total + rows * tree_pairs([offset * offset for offset in offsets])


def tree_pairs(terms):
    total = terms[0]
    for term in terms[1:]:
        total = total + term
    return total


def shifted(offsets, sums):
    if len(sums) == 2:
        return offsets[0] * (sums[0] - sums[1])
    return tree_pairs([offset * term for offset, term in zip(offsets, sums)])


def load_tile(ref, row, at):
    return ref[row : row + 1, pl.ds(at, LANES)]


def combine_project(groups, jac_ref, firsts, msgs, offsets, scale, olds, vector_ref, part_ref):
    rows, cols = jac_ref.shape

    def step(at, carry):
        acc, square = carry
        value = tree_pairs([load_tile(ref, 0, at) for ref in msgs])
        value = value + shifted(offsets, [load_tile(ref, 1, at) for ref in firsts])
        value = value * scale
        for factor, ref in olds:
            value = value - factor * load_tile(ref, 0, at)
        vector_ref[:, pl.ds(at, LANES)] = value
        return acc + jac_ref[:, pl.ds(at, LANES)] * value, square + value * value

    zeros = jnp.zeros((rows, LANES), jnp.float32), jnp.zeros((1, LANES), jnp.float32)
    acc, square = lax.fori_loop(0, cols // LANES, tiles(cols, step), zeros, unroll=2)
    line = jnp.sum(jnp.transpose(acc), axis=0, keepdims=True)
    lines = jnp.concatenate([line, over_lanes(square)], axis=0)
    part_ref[...] = jnp.broadcast_to(lines[None], part_ref.shape)


def project_zero(groups, walkers, jac_ref, *refs):
    firsts, (vector_ref, part_ref) = refs[:groups], refs[groups:]
    rows, cols = jac_ref.shape
    means = [ref[0:1, cols : cols + LANES] for ref in firsts]
    offsets, _ = spread(means, means, rows)
    scale = jnp.full((1, LANES), 1.0 / walkers, jnp.float32)
    combine_project(groups, jac_ref, firsts, firsts, offsets, scale, [], vector_ref, part_ref)


def msg_spread(msgs, rows, cols):
    means = [ref[:, cols : cols + LANES] for ref in msgs]
    squares = [ref[:, cols + LANES : cols + 2 * LANES] for ref in msgs]
    return spread(means, squares, rows)


def project_one(groups, walkers, jac_ref, *refs):
    firsts, msgs, refs = refs[:groups], refs[groups : 2 * groups], refs[2 * groups :]
    norm_ref, old_ref, vector_ref, part_ref, state_ref = refs
    rows, cols = jac_ref.shape
    offsets, square = msg_spread(msgs, rows, cols)
    alpha = square / (walkers * jnp.maximum(norm_ref[...], TINY))
    scale = 1.0 / (walkers * jnp.maximum(alpha, TINY))
    state_ref[0:1] = alpha
    state_ref[1:2] = scale
    one = jnp.ones((1, LANES), jnp.float32)
    combine_project(
        groups, jac_ref, firsts, msgs, offsets, scale, [(one, old_ref)], vector_ref, part_ref
    )


def project_two(groups, walkers, jac_ref, *refs):
    firsts, msgs, refs = refs[:groups], refs[groups : 2 * groups], refs[2 * groups :]
    state_ref, norm_old, norm_now, older_ref, old_ref, vector_ref, part_ref, alpha_ref = refs
    rows, cols = jac_ref.shape
    offsets, square = msg_spread(msgs, rows, cols)
    scale = state_ref[1:2]
    norm = jnp.maximum(norm_now[...], TINY)
    alpha = square * scale / norm
    alpha_ref[...] = alpha
    beta = norm_now[...] / jnp.maximum(norm_old[...], TINY)
    combine_project(
        groups,
        jac_ref,
        firsts,
        msgs,
        offsets,
        scale,
        [(alpha, old_ref), (beta, older_ref)],
        vector_ref,
        part_ref,
    )


def final_kernel(groups, parts, params, *refs):
    part_refs, refs = refs[: groups * parts], refs[groups * parts :]
    shift_ref, state_ref, alpha_ref, norm0_ref, norm1_ref = refs[:5]
    vectors, out_ref = refs[5:8], refs[8]
    cols = out_ref.shape[1]
    totals = [
        tree_sum([ref[...] for ref in part_refs[at : at + parts]])
        for at in range(0, groups * parts, parts)
    ]
    rows = totals[0].shape[1]
    pairs = [mean_and_dev(total[0:1]) for total in totals]
    _, square = spread(
        [mean for mean, _ in pairs], [over_lanes(dev * dev) for _, dev in pairs], rows
    )
    norm2 = totals[0][1:2]
    norm0, norm1 = norm0_ref[...], norm1_ref[...]
    alpha0, scale = state_ref[0:1], state_ref[1:2]
    alpha1 = alpha_ref[...]
    alpha2 = square * scale / jnp.maximum(norm2, TINY)
    beta1 = norm1 / jnp.maximum(norm0, TINY)
    beta2 = norm2 / jnp.maximum(norm1, TINY)
    inverse = 1.0 / jnp.maximum(alpha0, TINY)
    shift = shift_ref[...] * inverse
    pivot0 = 1.0 + shift
    pivot1 = (alpha1 + shift) - beta1 / pivot0
    pivot2 = (alpha2 + shift) - beta2 / pivot1
    right1 = -1.0 / pivot0
    right2 = -right1 / pivot1
    coef2 = right2 / pivot2
    coef1 = (right1 - beta2 * coef2) / pivot1
    coef0 = (1.0 - beta1 * coef1) / pivot0
    coef0, coef1, coef2 = coef0 * inverse, coef1 * inverse, coef2 * inverse
    square = coef0 * coef0 * norm0 + coef1 * coef1 * norm1 + coef2 * coef2 * norm2
    factor = lax.rsqrt(square / params + epsilon)
    coefs = [coef0 * factor, coef1 * factor, coef2 * factor]

    def step(at, carry):
        terms = [coef * load_tile(ref, 0, at) for coef, ref in zip(coefs, vectors)]
        out_ref[:, pl.ds(at, LANES)] = terms[0] + terms[1] + terms[2]
        return carry

    lax.fori_loop(0, cols // LANES, tiles(cols, step), 0, unroll=2)


def call(kernel, outs, *args):
    shapes = [jax.ShapeDtypeStruct(shape, jnp.float32) for shape in outs]
    space = pl.BlockSpec(memory_space=pltpu.VMEM)
    return pl.pallas_call(
        kernel,
        out_shape=shapes,
        in_specs=[space] * len(args),
        out_specs=[space] * len(shapes),
        compiler_params=pltpu.CompilerParams(vmem_limit_bytes=24 * 1024 * 1024),
    )(*args)


def from_walk(array, groups):
    others = []
    for hop in range(1, groups):
        pairs = [(index, (index - hop) % groups) for index in range(groups)]
        others.append(lax.ppermute(array, "walk", pairs))
    return [array] + others


def from_param(array, shards):
    return lax.all_to_all(array, "param", 0, 0, tiled=True)


def body(jacobian, energies, shifts):
    rows, cols = jacobian.shape
    groups, shards = lax.axis_size("walk"), lax.axis_size("param")
    walkers, params = rows * groups, cols * shards
    vector, part, scalar = (1, cols), (shards, 2, LANES), (1, LANES)
    shift_rows = jnp.broadcast_to(shifts[:, None], (shifts.shape[0], LANES))

    (msg,) = call(first_kernel, [(2, cols + LANES)], jacobian, energies.reshape(1, rows))
    firsts = from_walk(msg, groups)
    vector0, sent = call(
        functools.partial(project_zero, groups, walkers), [vector, part], jacobian, *firsts
    )
    parts = from_param(sent, shards)
    msg_shape = (1, cols + 2 * LANES)
    msg, norm0 = call(back_kernel, [msg_shape, scalar], jacobian, parts)
    msgs = from_walk(msg, groups)
    vector1, sent, state = call(
        functools.partial(project_one, groups, walkers),
        [vector, part, (2, LANES)],
        jacobian,
        *firsts,
        *msgs,
        norm0,
        vector0,
    )
    parts = from_param(sent, shards)
    msg, norm1 = call(back_kernel, [msg_shape, scalar], jacobian, parts)
    msgs = from_walk(msg, groups)
    vector2, sent, alpha1 = call(
        functools.partial(project_two, groups, walkers),
        [vector, part, scalar],
        jacobian,
        *firsts,
        *msgs,
        state,
        norm0,
        norm1,
        vector0,
        vector1,
    )
    parts = from_param(sent, shards)
    last = from_walk(jnp.sum(parts, axis=0), groups)
    (update,) = call(
        functools.partial(final_kernel, groups, 1, params),
        [(shifts.shape[0], cols)],
        *last,
        shift_rows,
        state,
        alpha1,
        norm0,
        norm1,
        vector0,
        vector1,
        vector2,
    )
    return update


def solution(mesh):
    return jax.shard_map(
        body,
        mesh=mesh,
        in_specs=(P("walk", "param"), P("walk"), P()),
        out_specs=P(None, "param"),
        check_vma=False,
    )
```

```python
import functools

import jax
import jax.numpy as jnp
from jax import lax
from jax.experimental import pallas as pl
from jax.experimental.pallas import tpu as pltpu
from jax.sharding import PartitionSpec as P

LANES = 128
TINY = 1e-37
CHUNKS = 8
FLIGHT = 4
epsilon = 1e-06


def over_lanes(values):
    total = jnp.sum(values, axis=1, keepdims=True)
    return jnp.broadcast_to(total, (values.shape[0], LANES))


def tree_sum(terms):
    terms = list(terms)
    while len(terms) > 1:
        terms = [a + b for a, b in zip(terms[0::2], terms[1::2])]
    return terms[0]


def down_rows(row):
    return jnp.transpose(jnp.broadcast_to(row, (row.shape[1], row.shape[1])))


def tiles(count, step):
    def run(number, carry):
        return step(pl.multiple_of(number * LANES, LANES), carry)

    return run


def mean_and_dev(row):
    mean = over_lanes(row) / row.shape[1]
    return mean, row - mean


def cut(count, pieces):
    edges = [count * number // pieces for number in range(pieces + 1)]
    return [(low * LANES, high * LANES) for low, high in zip(edges, edges[1:]) if high > low]


def first_kernel(jac_hbm, energy_hbm, jac_ref, msg_ref, energy_ref, sems, energy_sem):
    cols = jac_ref.shape[1]
    pieces = cut(cols // LANES, CHUNKS)
    copies = [
        pltpu.make_async_copy(
            jac_hbm.at[:, low:high], jac_ref.at[:, low:high], sems.at[number]
        )
        for number, (low, high) in enumerate(pieces)
    ]
    energy_copy = pltpu.make_async_copy(energy_hbm, energy_ref, energy_sem)
    energy_copy.start()
    for copy in copies[:FLIGHT]:
        copy.start()
    energy_copy.wait()
    mean, dev = mean_and_dev(energy_ref[...])
    weight = down_rows(dev)
    msg_ref[0:1, cols : cols + LANES] = mean
    msg_ref[1:2, cols : cols + LANES] = mean
    for number, (low, high) in enumerate(pieces):
        copies[number].wait()
        if number + FLIGHT < len(copies):
            copies[number + FLIGHT].start()
        for at in range(low, high, LANES):
            block = jac_ref[:, at : at + LANES]
            msg_ref[0:1, at : at + LANES] = jnp.sum(block * weight, axis=0, keepdims=True)
            msg_ref[1:2, at : at + LANES] = jnp.sum(block, axis=0, keepdims=True)


def back_kernel(jac_ref, part_ref, msg_ref, norm_ref):
    cols = jac_ref.shape[1]
    total = jnp.sum(part_ref[...], axis=0)
    mean, dev = mean_and_dev(total[0:1])
    weight = down_rows(dev)

    def step(at, carry):
        block = jac_ref[:, pl.ds(at, LANES)]
        msg_ref[:, pl.ds(at, LANES)] = jnp.sum(block * weight, axis=0, keepdims=True)
        return carry

    lax.fori_loop(0, cols // LANES, tiles(cols, step), 0, unroll=2)
    msg_ref[:, cols : cols + LANES] = mean
    msg_ref[:, cols + LANES : cols + 2 * LANES] = over_lanes(dev * dev)
    norm_ref[...] = total[1:2]


def spread(means, squares, rows):
    centre = sum(means) / len(means)
    offsets = [mean - centre for mean in means]
    total = tree_pairs(squares)
    return offsets, total + rows * tree_pairs([offset * offset for offset in offsets])


def tree_pairs(terms):
    total = terms[0]
    for term in terms[1:]:
        total = total + term
    return total


def shifted(offsets, sums):
    if len(sums) == 2:
        return offsets[0] * (sums[0] - sums[1])
    return tree_pairs([offset * term for offset, term in zip(offsets, sums)])


def load_tile(ref, row, at):
    return ref[row : row + 1, pl.ds(at, LANES)]


def combine_project(groups, jac_ref, firsts, msgs, offsets, scale, olds, vector_ref, part_ref):
    rows, cols = jac_ref.shape

    def step(at, carry):
        acc, square = carry
        value = tree_pairs([load_tile(ref, 0, at) for ref in msgs])
        value = value + shifted(offsets, [load_tile(ref, 1, at) for ref in firsts])
        value = value * scale
        for factor, ref in olds:
            value = value - factor * load_tile(ref, 0, at)
        vector_ref[:, pl.ds(at, LANES)] = value
        return acc + jac_ref[:, pl.ds(at, LANES)] * value, square + value * value

    zeros = jnp.zeros((rows, LANES), jnp.float32), jnp.zeros((1, LANES), jnp.float32)
    acc, square = lax.fori_loop(0, cols // LANES, tiles(cols, step), zeros, unroll=2)
    line = jnp.sum(jnp.transpose(acc), axis=0, keepdims=True)
    part_ref[...] = jnp.concatenate([line, over_lanes(square)], axis=0)


def project_zero(groups, walkers, jac_ref, *refs):
    firsts, (vector_ref, part_ref) = refs[:groups], refs[groups:]
    rows, cols = jac_ref.shape
    means = [ref[0:1, cols : cols + LANES] for ref in firsts]
    offsets, _ = spread(means, means, rows)
    scale = jnp.full((1, LANES), 1.0 / walkers, jnp.float32)
    combine_project(groups, jac_ref, firsts, firsts, offsets, scale, [], vector_ref, part_ref)


def msg_spread(msgs, rows, cols):
    means = [ref[:, cols : cols + LANES] for ref in msgs]
    squares = [ref[:, cols + LANES : cols + 2 * LANES] for ref in msgs]
    return spread(means, squares, rows)


def project_one(groups, walkers, jac_ref, *refs):
    firsts, msgs, refs = refs[:groups], refs[groups : 2 * groups], refs[2 * groups :]
    norm_ref, old_ref, vector_ref, part_ref, state_ref = refs
    rows, cols = jac_ref.shape
    offsets, square = msg_spread(msgs, rows, cols)
    alpha = square / (walkers * jnp.maximum(norm_ref[...], TINY))
    scale = 1.0 / (walkers * jnp.maximum(alpha, TINY))
    state_ref[0:1] = alpha
    state_ref[1:2] = scale
    one = jnp.ones((1, LANES), jnp.float32)
    combine_project(
        groups, jac_ref, firsts, msgs, offsets, scale, [(one, old_ref)], vector_ref, part_ref
    )


def project_two(groups, walkers, jac_ref, *refs):
    firsts, msgs, refs = refs[:groups], refs[groups : 2 * groups], refs[2 * groups :]
    state_ref, norm_old, norm_now, older_ref, old_ref, vector_ref, part_ref, alpha_ref = refs
    rows, cols = jac_ref.shape
    offsets, square = msg_spread(msgs, rows, cols)
    scale = state_ref[1:2]
    norm = jnp.maximum(norm_now[...], TINY)
    alpha = square * scale / norm
    alpha_ref[...] = alpha
    beta = norm_now[...] / jnp.maximum(norm_old[...], TINY)
    combine_project(
        groups,
        jac_ref,
        firsts,
        msgs,
        offsets,
        scale,
        [(alpha, old_ref), (beta, older_ref)],
        vector_ref,
        part_ref,
    )


def final_kernel(groups, params, part_ref, *refs):
    shift_ref, state_ref, alpha_ref, norm0_ref, norm1_ref = refs[:5]
    vectors, out_ref = refs[5:8], refs[8]
    cols = out_ref.shape[1]
    parts = part_ref.shape[0] // groups
    totals = [
        jnp.sum(part_ref[at * parts : (at + 1) * parts], axis=0) for at in range(groups)
    ]
    rows = totals[0].shape[1]
    pairs = [mean_and_dev(total[0:1]) for total in totals]
    _, square = spread(
        [mean for mean, _ in pairs], [over_lanes(dev * dev) for _, dev in pairs], rows
    )
    norm2 = totals[0][1:2]
    norm0, norm1 = norm0_ref[...], norm1_ref[...]
    alpha0, scale = state_ref[0:1], state_ref[1:2]
    alpha1 = alpha_ref[...]
    alpha2 = square * scale / jnp.maximum(norm2, TINY)
    beta1 = norm1 / jnp.maximum(norm0, TINY)
    beta2 = norm2 / jnp.maximum(norm1, TINY)
    inverse = 1.0 / jnp.maximum(alpha0, TINY)
    shift = shift_ref[...] * inverse
    pivot0 = 1.0 + shift
    pivot1 = (alpha1 + shift) - beta1 / pivot0
    pivot2 = (alpha2 + shift) - beta2 / pivot1
    right1 = -1.0 / pivot0
    right2 = -right1 / pivot1
    coef2 = right2 / pivot2
    coef1 = (right1 - beta2 * coef2) / pivot1
    coef0 = (1.0 - beta1 * coef1) / pivot0
    coef0, coef1, coef2 = coef0 * inverse, coef1 * inverse, coef2 * inverse
    square = coef0 * coef0 * norm0 + coef1 * coef1 * norm1 + coef2 * coef2 * norm2
    factor = lax.rsqrt(square / params + epsilon)
    coefs = [coef0 * factor, coef1 * factor, coef2 * factor]

    def step(at, carry):
        terms = [coef * load_tile(ref, 0, at) for coef, ref in zip(coefs, vectors)]
        out_ref[:, pl.ds(at, LANES)] = terms[0] + terms[1] + terms[2]
        return carry

    lax.fori_loop(0, cols // LANES, tiles(cols, step), 0, unroll=2)


def call(kernel, outs, *args, spaces=None, scratch=()):
    shapes = [jax.ShapeDtypeStruct(shape, jnp.float32) for shape in outs]
    space = pl.BlockSpec(memory_space=pltpu.VMEM)
    return pl.pallas_call(
        kernel,
        out_shape=shapes,
        in_specs=spaces or [space] * len(args),
        out_specs=[space] * len(shapes),
        scratch_shapes=scratch,
        compiler_params=pltpu.CompilerParams(vmem_limit_bytes=24 * 1024 * 1024),
    )(*args)


def from_walk(array, groups):
    others = []
    for hop in range(1, groups):
        pairs = [(index, (index - hop) % groups) for index in range(groups)]
        others.append(lax.ppermute(array, "walk", pairs))
    return [array] + others


def radices_of(size):
    radices = []
    while size > 1:
        radices.append(4 if size % 4 == 0 else 2)
        size //= radices[-1]
    return radices or [1]


def squads(groups, size, stride, radix):
    squad = []
    for start in range(size):
        if start // stride % radix == 0:
            members = [start + stride * step for step in range(radix)]
            squad.append([size * group + index for group in groups for index in members])
    return squad


def swap(array, names, squad):
    copies = jnp.broadcast_to(array[None], (len(squad[0]),) + array.shape)
    return lax.all_to_all(copies, names, 0, 0, axis_index_groups=squad, tiled=True)


def from_param(array, shards):
    radices = radices_of(shards)
    stride = 1
    for radix in radices[:-1]:
        array = jnp.sum(swap(array, "param", squads([0], shards, stride, radix)), axis=0)
        stride *= radix
    return array, stride, radices[-1]


def by_param(array, shards):
    array, stride, radix = from_param(array, shards)
    return swap(array, "param", squads([0], shards, stride, radix))


def by_both(array, groups, shards):
    array, stride, radix = from_param(array, shards)
    squad = squads(range(groups), shards, stride, radix)
    return swap(array, ("walk", "param"), squad)


def body(jacobian, energies, shifts):
    rows, cols = jacobian.shape
    groups, shards = lax.axis_size("walk"), lax.axis_size("param")
    walkers, params = rows * groups, cols * shards
    vector, part, scalar = (1, cols), (2, LANES), (1, LANES)
    shift_rows = jnp.broadcast_to(shifts[:, None], (shifts.shape[0], LANES))

    jacobian, msg = call(
        first_kernel,
        [(rows, cols), (2, cols + LANES)],
        pltpu.with_memory_space_constraint(jacobian, pltpu.HBM),
        pltpu.with_memory_space_constraint(energies.reshape(1, rows), pltpu.HBM),
        spaces=[pl.BlockSpec(memory_space=pltpu.HBM)] * 2,
        scratch=[
            pltpu.VMEM((1, rows), jnp.float32),
            pltpu.SemaphoreType.DMA((CHUNKS,)),
            pltpu.SemaphoreType.DMA(()),
        ],
    )
    firsts = from_walk(msg, groups)
    vector0, sent = call(
        functools.partial(project_zero, groups, walkers), [vector, part], jacobian, *firsts
    )
    parts = by_param(sent, shards)
    msg_shape = (1, cols + 2 * LANES)
    msg, norm0 = call(back_kernel, [msg_shape, scalar], jacobian, parts)
    msgs = from_walk(msg, groups)
    vector1, sent, state = call(
        functools.partial(project_one, groups, walkers),
        [vector, part, (2, LANES)],
        jacobian,
        *firsts,
        *msgs,
        norm0,
        vector0,
    )
    parts = by_param(sent, shards)
    msg, norm1 = call(back_kernel, [msg_shape, scalar], jacobian, parts)
    msgs = from_walk(msg, groups)
    vector2, sent, alpha1 = call(
        functools.partial(project_two, groups, walkers),
        [vector, part, scalar],
        jacobian,
        *firsts,
        *msgs,
        state,
        norm0,
        norm1,
        vector0,
        vector1,
    )
    parts = by_both(sent, groups, shards)
    (update,) = call(
        functools.partial(final_kernel, groups, params),
        [(shifts.shape[0], cols)],
        parts,
        shift_rows,
        state,
        alpha1,
        norm0,
        norm1,
        vector0,
        vector1,
        vector2,
    )
    return update


def solution(mesh):
    return jax.shard_map(
        body,
        mesh=mesh,
        in_specs=(P("walk", "param"), P("walk"), P()),
        out_specs=P(None, "param"),
        check_vma=False,
    )
```

```python
import functools

import jax
import jax.numpy as jnp
from jax import lax
from jax.experimental import pallas as pl
from jax.experimental.pallas import tpu as pltpu
from jax.sharding import PartitionSpec as P

LANES = 128
TINY = 1e-37
CHUNKS = 8
FLIGHT = 8
epsilon = 1e-06


def over_lanes(values):
    total = jnp.sum(values, axis=1, keepdims=True)
    return jnp.broadcast_to(total, (values.shape[0], LANES))


def tree_sum(terms):
    terms = list(terms)
    while len(terms) > 1:
        odd = terms[len(terms) // 2 * 2 :]
        terms = [a + b for a, b in zip(terms[0::2], terms[1::2])] + odd
    return terms[0]


def down_rows(row):
    return jnp.transpose(jnp.broadcast_to(row, (row.shape[1], row.shape[1])))


def tiles(count, step):
    def run(number, carry):
        return step(pl.multiple_of(number * LANES, LANES), carry)

    return run


def mean_and_dev(row):
    mean = over_lanes(row) / row.shape[1]
    return mean, row - mean


def cut(count, pieces):
    edges = [count * number // pieces for number in range(pieces + 1)]
    return [(low * LANES, high * LANES) for low, high in zip(edges, edges[1:]) if high > low]


def first_kernel(jac_hbm, energy_hbm, jac_ref, msg_ref, energy_ref, sems, energy_sem):
    cols = jac_ref.shape[1]
    pieces = cut(cols // LANES, CHUNKS)
    copies = [
        pltpu.make_async_copy(
            jac_hbm.at[:, low:high], jac_ref.at[:, low:high], sems.at[number]
        )
        for number, (low, high) in enumerate(pieces)
    ]
    energy_copy = pltpu.make_async_copy(energy_hbm, energy_ref, energy_sem)
    energy_copy.start()
    for copy in copies[:FLIGHT]:
        copy.start()
    energy_copy.wait()
    mean, dev = mean_and_dev(energy_ref[...])
    weight = down_rows(dev)
    msg_ref[0:1, cols : cols + LANES] = mean
    msg_ref[1:2, cols : cols + LANES] = mean
    for number, (low, high) in enumerate(pieces):
        copies[number].wait()
        if number + FLIGHT < len(copies):
            copies[number + FLIGHT].start()
        for at in range(low, high, LANES):
            block = jac_ref[:, at : at + LANES]
            msg_ref[0:1, at : at + LANES] = jnp.sum(block * weight, axis=0, keepdims=True)
            msg_ref[1:2, at : at + LANES] = jnp.sum(block, axis=0, keepdims=True)


def back_kernel(jac_ref, total_ref, msg_ref, norm_ref):
    cols = jac_ref.shape[1]
    weight = down_rows(total_ref[0, 0:1])
    mean = jnp.sum(weight, axis=0, keepdims=True) / jac_ref.shape[0]
    weight = weight - mean

    def step(at, carry):
        block = jac_ref[:, pl.ds(at, LANES)]
        msg_ref[:, pl.ds(at, LANES)] = jnp.sum(block * weight, axis=0, keepdims=True)
        return carry

    lax.fori_loop(0, cols // LANES, tiles(cols, step), 0, unroll=2)
    msg_ref[:, cols : cols + LANES] = mean
    msg_ref[:, cols + LANES : cols + 2 * LANES] = jnp.sum(weight * weight, axis=0, keepdims=True)
    norm_ref[...] = total_ref[0, 1:2]


def spread(means, squares, rows):
    centre = sum(means) / len(means)
    offsets = [mean - centre for mean in means]
    total = tree_pairs(squares)
    return offsets, total + rows * tree_pairs([offset * offset for offset in offsets])


def tree_pairs(terms):
    total = terms[0]
    for term in terms[1:]:
        total = total + term
    return total


def shifted(offsets, sums):
    if len(sums) == 2:
        return offsets[0] * (sums[0] - sums[1])
    return tree_pairs([offset * term for offset, term in zip(offsets, sums)])


def load_tile(ref, row, at):
    return ref[row : row + 1, pl.ds(at, LANES)]


def combine_project(groups, jac_ref, firsts, msgs, offsets, scale, olds, vector_ref, part_ref):
    rows, cols = jac_ref.shape

    def step(at, carry):
        acc, square = carry
        value = tree_pairs([load_tile(ref, 0, at) for ref in msgs])
        value = value + shifted(offsets, [load_tile(ref, 1, at) for ref in firsts])
        value = value * scale
        for factor, ref in olds:
            value = value - factor * load_tile(ref, 0, at)
        vector_ref[:, pl.ds(at, LANES)] = value
        return acc + jac_ref[:, pl.ds(at, LANES)] * value, square + value * value

    zeros = jnp.zeros((rows, LANES), jnp.float32), jnp.zeros((1, LANES), jnp.float32)
    acc, square = lax.fori_loop(0, cols // LANES, tiles(cols, step), zeros, unroll=2)
    line = jnp.sum(jnp.transpose(acc), axis=0, keepdims=True)
    part_ref[...] = jnp.concatenate([line, over_lanes(square)], axis=0)


def project_zero(groups, walkers, jac_ref, *refs):
    firsts, (vector_ref, part_ref) = refs[:groups], refs[groups:]
    rows, cols = jac_ref.shape
    means = [ref[0:1, cols : cols + LANES] for ref in firsts]
    offsets, _ = spread(means, means, rows)
    scale = jnp.full((1, LANES), 1.0 / walkers, jnp.float32)
    combine_project(groups, jac_ref, firsts, firsts, offsets, scale, [], vector_ref, part_ref)


def msg_spread(msgs, rows, cols):
    means = [ref[:, cols : cols + LANES] for ref in msgs]
    squares = [ref[:, cols + LANES : cols + 2 * LANES] for ref in msgs]
    return spread(means, squares, rows)


def project_one(groups, walkers, jac_ref, *refs):
    firsts, msgs, refs = refs[:groups], refs[groups : 2 * groups], refs[2 * groups :]
    norm_ref, old_ref, vector_ref, part_ref, state_ref = refs
    rows, cols = jac_ref.shape
    offsets, square = msg_spread(msgs, rows, cols)
    alpha = square / (walkers * jnp.maximum(norm_ref[...], TINY))
    scale = 1.0 / (walkers * jnp.maximum(alpha, TINY))
    state_ref[0:1] = alpha
    state_ref[1:2] = scale
    one = jnp.ones((1, LANES), jnp.float32)
    combine_project(
        groups, jac_ref, firsts, msgs, offsets, scale, [(one, old_ref)], vector_ref, part_ref
    )


def project_two(groups, walkers, jac_ref, *refs):
    firsts, msgs, refs = refs[:groups], refs[groups : 2 * groups], refs[2 * groups :]
    state_ref, norm_old, norm_now, older_ref, old_ref, vector_ref, part_ref, alpha_ref = refs
    rows, cols = jac_ref.shape
    offsets, square = msg_spread(msgs, rows, cols)
    scale = state_ref[1:2]
    norm = jnp.maximum(norm_now[...], TINY)
    alpha = square * scale / norm
    alpha_ref[...] = alpha
    beta = norm_now[...] / jnp.maximum(norm_old[...], TINY)
    combine_project(
        groups,
        jac_ref,
        firsts,
        msgs,
        offsets,
        scale,
        [(alpha, old_ref), (beta, older_ref)],
        vector_ref,
        part_ref,
    )


def final_kernel(groups, params, total_ref, *refs):
    shift_ref, state_ref, alpha_ref, norm0_ref, norm1_ref = refs[:5]
    vectors, out_ref = refs[5:8], refs[8]
    cols = out_ref.shape[1]
    totals = [total_ref[at] for at in range(groups)]
    rows = totals[0].shape[1]
    pairs = [mean_and_dev(total[0:1]) for total in totals]
    _, square = spread(
        [mean for mean, _ in pairs], [over_lanes(dev * dev) for _, dev in pairs], rows
    )
    norm2 = totals[0][1:2]
    norm0, norm1 = norm0_ref[...], norm1_ref[...]
    alpha0, scale = state_ref[0:1], state_ref[1:2]
    alpha1 = alpha_ref[...]
    alpha2 = square * scale / jnp.maximum(norm2, TINY)
    beta1 = norm1 / jnp.maximum(norm0, TINY)
    beta2 = norm2 / jnp.maximum(norm1, TINY)
    inverse = 1.0 / jnp.maximum(alpha0, TINY)
    shift = shift_ref[...] * inverse
    pivot0 = 1.0 + shift
    pivot1 = (alpha1 + shift) - beta1 / pivot0
    pivot2 = (alpha2 + shift) - beta2 / pivot1
    right1 = -1.0 / pivot0
    right2 = -right1 / pivot1
    coef2 = right2 / pivot2
    coef1 = (right1 - beta2 * coef2) / pivot1
    coef0 = (1.0 - beta1 * coef1) / pivot0
    coef0, coef1, coef2 = coef0 * inverse, coef1 * inverse, coef2 * inverse
    square = coef0 * coef0 * norm0 + coef1 * coef1 * norm1 + coef2 * coef2 * norm2
    factor = lax.rsqrt(square / params + epsilon)
    coefs = [coef0 * factor, coef1 * factor, coef2 * factor]

    def step(at, carry):
        terms = [coef * load_tile(ref, 0, at) for coef, ref in zip(coefs, vectors)]
        out_ref[:, pl.ds(at, LANES)] = terms[0] + terms[1] + terms[2]
        return carry

    lax.fori_loop(0, cols // LANES, tiles(cols, step), 0, unroll=2)


def call(kernel, outs, *args, spaces=None, scratch=()):
    shapes = [jax.ShapeDtypeStruct(shape, jnp.float32) for shape in outs]
    space = pl.BlockSpec(memory_space=pltpu.VMEM)
    return pl.pallas_call(
        kernel,
        out_shape=shapes,
        in_specs=spaces or [space] * len(args),
        out_specs=[space] * len(shapes),
        scratch_shapes=scratch,
        compiler_params=pltpu.CompilerParams(vmem_limit_bytes=24 * 1024 * 1024),
    )(*args)


def from_walk(array, groups):
    others = []
    for hop in range(1, groups):
        pairs = [(index, (index - hop) % groups) for index in range(groups)]
        others.append(lax.ppermute(array, "walk", pairs))
    return [array] + others


def send(array, pairs):
    return lax.ppermute(array, ("walk", "param"), pairs)


def climb(array, groups, shards):
    root = shards // 2 - 1
    bases = [shards * group for group in range(groups)]
    pairs = [(base + at, base + at + 1) for base in bases for at in range(0, shards, 2)]
    array = array + send(array, pairs)
    terms = [array]
    for at in range(1, shards, 2):
        if at != root:
            terms.append(send(array, [(base + at, base + root) for base in bases]))
    return tree_sum(terms)


def descend(array, groups, shards, hops):
    root = shards // 2 - 1
    bases = [shards * group for group in range(groups)]
    index = lax.axis_index("param")
    totals = []
    for hop in range(hops):
        terms = []
        for at in range(1, shards, 2):
            if hop or at != root:
                pairs = [
                    (shards * group + root, shards * ((group + hop) % groups) + at)
                    for group in range(groups)
                ]
                terms.append(send(array, pairs))
            else:
                terms.append(jnp.where(index == root, array, 0.0))
        totals.append(tree_sum(terms))
    total = jnp.stack(totals)
    pairs = [(base + at + 1, base + at) for base in bases for at in range(0, shards, 2)]
    return jnp.where(index % 2 == 1, total, send(total, pairs))


def body(jacobian, energies, shifts):
    rows, cols = jacobian.shape
    groups, shards = lax.axis_size("walk"), lax.axis_size("param")
    walkers, params = rows * groups, cols * shards
    vector, part, scalar = (1, cols), (2, LANES), (1, LANES)
    shift_rows = jnp.broadcast_to(shifts[:, None], (shifts.shape[0], LANES))

    jacobian, msg = call(
        first_kernel,
        [(rows, cols), (2, cols + LANES)],
        pltpu.with_memory_space_constraint(jacobian, pltpu.HBM),
        pltpu.with_memory_space_constraint(energies.reshape(1, rows), pltpu.HBM),
        spaces=[pl.BlockSpec(memory_space=pltpu.HBM)] * 2,
        scratch=[
            pltpu.VMEM((1, rows), jnp.float32),
            pltpu.SemaphoreType.DMA((CHUNKS,)),
            pltpu.SemaphoreType.DMA(()),
        ],
    )
    firsts = from_walk(msg, groups)
    vector0, sent = call(
        functools.partial(project_zero, groups, walkers), [vector, part], jacobian, *firsts
    )
    total = descend(climb(sent, groups, shards), groups, shards, 1)
    msg_shape = (1, cols + 2 * LANES)
    msg, norm0 = call(back_kernel, [msg_shape, scalar], jacobian, total)
    msgs = from_walk(msg, groups)
    vector1, sent, state = call(
        functools.partial(project_one, groups, walkers),
        [vector, part, (2, LANES)],
        jacobian,
        *firsts,
        *msgs,
        norm0,
        vector0,
    )
    total = descend(climb(sent, groups, shards), groups, shards, 1)
    msg, norm1 = call(back_kernel, [msg_shape, scalar], jacobian, total)
    msgs = from_walk(msg, groups)
    vector2, sent, alpha1 = call(
        functools.partial(project_two, groups, walkers),
        [vector, part, scalar],
        jacobian,
        *firsts,
        *msgs,
        state,
        norm0,
        norm1,
        vector0,
        vector1,
    )
    total = descend(climb(sent, groups, shards), groups, shards, groups)
    (update,) = call(
        functools.partial(final_kernel, groups, params),
        [(shifts.shape[0], cols)],
        total,
        shift_rows,
        state,
        alpha1,
        norm0,
        norm1,
        vector0,
        vector1,
        vector2,
    )
    return update


def solution(mesh):
    return jax.shard_map(
        body,
        mesh=mesh,
        in_specs=(P("walk", "param"), P("walk"), P()),
        out_specs=P(None, "param"),
        check_vma=False,
    )
```

```python
import functools

import jax
import jax.numpy as jnp
from jax import lax
from jax.experimental import pallas as pl
from jax.experimental.pallas import tpu as pltpu
from jax.sharding import PartitionSpec as P

LANES = 128
TINY = 1e-37
CHUNKS = 8
FLIGHT = 8
epsilon = 1e-06


def over_lanes(values):
    total = jnp.sum(values, axis=1, keepdims=True)
    return jnp.broadcast_to(total, (values.shape[0], LANES))


def tree_sum(terms):
    terms = list(terms)
    while len(terms) > 1:
        odd = terms[len(terms) // 2 * 2 :]
        terms = [a + b for a, b in zip(terms[0::2], terms[1::2])] + odd
    return terms[0]


def down_rows(row):
    return jnp.transpose(jnp.broadcast_to(row, (row.shape[1], row.shape[1])))


def tiles(count, step):
    def run(number, carry):
        return step(pl.multiple_of(number * LANES, LANES), carry)

    return run


def mean_and_dev(row):
    mean = over_lanes(row) / row.shape[1]
    return mean, row - mean


def cut(count, pieces):
    edges = [count * number // pieces for number in range(pieces + 1)]
    return [(low * LANES, high * LANES) for low, high in zip(edges, edges[1:]) if high > low]


def first_kernel(jac_hbm, energy_hbm, msg_ref, jac_ref, energy_ref, sems, energy_sem):
    cols = jac_ref.shape[1]
    pieces = cut(cols // LANES, CHUNKS)
    copies = [
        pltpu.make_async_copy(
            jac_hbm.at[:, low:high], jac_ref.at[:, low:high], sems.at[number]
        )
        for number, (low, high) in enumerate(pieces)
    ]
    energy_copy = pltpu.make_async_copy(energy_hbm, energy_ref, energy_sem)
    energy_copy.start()
    for copy in copies[:FLIGHT]:
        copy.start()
    energy_copy.wait()
    mean, dev = mean_and_dev(energy_ref[...])
    weight = down_rows(dev)
    msg_ref[0:1, cols : cols + LANES] = mean
    msg_ref[1:2, cols : cols + LANES] = mean
    for number, (low, high) in enumerate(pieces):
        copies[number].wait()
        if number + FLIGHT < len(copies):
            copies[number + FLIGHT].start()
        for at in range(low, high, LANES):
            block = jac_ref[:, at : at + LANES]
            msg_ref[0:1, at : at + LANES] = jnp.sum(block * weight, axis=0, keepdims=True)
            msg_ref[1:2, at : at + LANES] = jnp.sum(block, axis=0, keepdims=True)


def back_kernel(jac_ref, total_ref, msg_ref, norm_ref):
    cols = jac_ref.shape[1]
    weight = down_rows(total_ref[0, 0:1])
    mean = jnp.sum(weight, axis=0, keepdims=True) / jac_ref.shape[0]
    weight = weight - mean

    def step(at, carry):
        block = jac_ref[:, pl.ds(at, LANES)]
        msg_ref[:, pl.ds(at, LANES)] = jnp.sum(block * weight, axis=0, keepdims=True)
        return carry

    lax.fori_loop(0, cols // LANES, tiles(cols, step), 0, unroll=2)
    msg_ref[:, cols : cols + LANES] = mean
    msg_ref[:, cols + LANES : cols + 2 * LANES] = jnp.sum(weight * weight, axis=0, keepdims=True)
    norm_ref[...] = total_ref[0, 1:2]


def spread(means, squares, rows):
    centre = sum(means) / len(means)
    offsets = [mean - centre for mean in means]
    total = tree_pairs(squares)
    return offsets, total + rows * tree_pairs([offset * offset for offset in offsets])


def tree_pairs(terms):
    total = terms[0]
    for term in terms[1:]:
        total = total + term
    return total


def shifted(offsets, sums):
    if len(sums) == 2:
        return offsets[0] * (sums[0] - sums[1])
    return tree_pairs([offset * term for offset, term in zip(offsets, sums)])


def load_tile(ref, row, at):
    return ref[row : row + 1, pl.ds(at, LANES)]


def combine_project(groups, jac_ref, firsts, msgs, offsets, scale, olds, vector_ref, part_ref):
    rows, cols = jac_ref.shape

    def step(at, carry):
        acc, square = carry
        value = tree_pairs([load_tile(ref, 0, at) for ref in msgs])
        value = value + shifted(offsets, [load_tile(ref, 1, at) for ref in firsts])
        value = value * scale
        for factor, ref in olds:
            value = value - factor * load_tile(ref, 0, at)
        vector_ref[:, pl.ds(at, LANES)] = value
        return acc + jac_ref[:, pl.ds(at, LANES)] * value, square + value * value

    zeros = jnp.zeros((rows, LANES), jnp.float32), jnp.zeros((1, LANES), jnp.float32)
    acc, square = lax.fori_loop(0, cols // LANES, tiles(cols, step), zeros, unroll=2)
    line = jnp.sum(jnp.transpose(acc), axis=0, keepdims=True)
    part_ref[...] = jnp.concatenate([line, over_lanes(square)], axis=0)


def project_zero(groups, walkers, jac_ref, *refs):
    firsts, (vector_ref, part_ref) = refs[:groups], refs[groups:]
    rows, cols = jac_ref.shape
    means = [ref[0:1, cols : cols + LANES] for ref in firsts]
    offsets, _ = spread(means, means, rows)
    scale = jnp.full((1, LANES), 1.0 / walkers, jnp.float32)
    combine_project(groups, jac_ref, firsts, firsts, offsets, scale, [], vector_ref, part_ref)


def msg_spread(msgs, rows, cols):
    means = [ref[:, cols : cols + LANES] for ref in msgs]
    squares = [ref[:, cols + LANES : cols + 2 * LANES] for ref in msgs]
    return spread(means, squares, rows)


def project_one(groups, walkers, jac_ref, *refs):
    firsts, msgs, refs = refs[:groups], refs[groups : 2 * groups], refs[2 * groups :]
    norm_ref, old_ref, vector_ref, part_ref, state_ref = refs
    rows, cols = jac_ref.shape
    offsets, square = msg_spread(msgs, rows, cols)
    alpha = square / (walkers * jnp.maximum(norm_ref[...], TINY))
    scale = 1.0 / (walkers * jnp.maximum(alpha, TINY))
    state_ref[0:1] = alpha
    state_ref[1:2] = scale
    one = jnp.ones((1, LANES), jnp.float32)
    combine_project(
        groups, jac_ref, firsts, msgs, offsets, scale, [(one, old_ref)], vector_ref, part_ref
    )


def project_two(groups, walkers, jac_ref, *refs):
    firsts, msgs, refs = refs[:groups], refs[groups : 2 * groups], refs[2 * groups :]
    state_ref, norm_old, norm_now, older_ref, old_ref, vector_ref, part_ref, alpha_ref = refs
    rows, cols = jac_ref.shape
    offsets, square = msg_spread(msgs, rows, cols)
    scale = state_ref[1:2]
    norm = jnp.maximum(norm_now[...], TINY)
    alpha = square * scale / norm
    alpha_ref[...] = alpha
    beta = norm_now[...] / jnp.maximum(norm_old[...], TINY)
    combine_project(
        groups,
        jac_ref,
        firsts,
        msgs,
        offsets,
        scale,
        [(alpha, old_ref), (beta, older_ref)],
        vector_ref,
        part_ref,
    )


def final_kernel(groups, params, total_ref, *refs):
    shift_ref, state_ref, alpha_ref, norm0_ref, norm1_ref = refs[:5]
    vectors, out_ref = refs[5:8], refs[8]
    cols = out_ref.shape[1]
    totals = [total_ref[at] for at in range(groups)]
    rows = totals[0].shape[1]
    pairs = [mean_and_dev(total[0:1]) for total in totals]
    _, square = spread(
        [mean for mean, _ in pairs], [over_lanes(dev * dev) for _, dev in pairs], rows
    )
    norm2 = totals[0][1:2]
    norm0, norm1 = norm0_ref[...], norm1_ref[...]
    alpha0, scale = state_ref[0:1], state_ref[1:2]
    alpha1 = alpha_ref[...]
    alpha2 = square * scale / jnp.maximum(norm2, TINY)
    beta1 = norm1 / jnp.maximum(norm0, TINY)
    beta2 = norm2 / jnp.maximum(norm1, TINY)
    inverse = 1.0 / jnp.maximum(alpha0, TINY)
    shift = shift_ref[...] * inverse
    pivot0 = 1.0 + shift
    pivot1 = (alpha1 + shift) - beta1 / pivot0
    pivot2 = (alpha2 + shift) - beta2 / pivot1
    right1 = -1.0 / pivot0
    right2 = -right1 / pivot1
    coef2 = right2 / pivot2
    coef1 = (right1 - beta2 * coef2) / pivot1
    coef0 = (1.0 - beta1 * coef1) / pivot0
    coef0, coef1, coef2 = coef0 * inverse, coef1 * inverse, coef2 * inverse
    square = coef0 * coef0 * norm0 + coef1 * coef1 * norm1 + coef2 * coef2 * norm2
    factor = lax.rsqrt(square / params + epsilon)
    coefs = [coef0 * factor, coef1 * factor, coef2 * factor]

    def step(at, carry):
        terms = [coef * load_tile(ref, 0, at) for coef, ref in zip(coefs, vectors)]
        out_ref[:, pl.ds(at, LANES)] = terms[0] + terms[1] + terms[2]
        return carry

    lax.fori_loop(0, cols // LANES, tiles(cols, step), 0, unroll=2)


def call(kernel, outs, *args, spaces=None, scratch=()):
    shapes = [jax.ShapeDtypeStruct(shape, jnp.float32) for shape in outs]
    space = pl.BlockSpec(memory_space=pltpu.VMEM)
    return pl.pallas_call(
        kernel,
        out_shape=shapes,
        in_specs=spaces or [space] * len(args),
        out_specs=[space] * len(shapes),
        scratch_shapes=scratch,
        compiler_params=pltpu.CompilerParams(vmem_limit_bytes=24 * 1024 * 1024),
    )(*args)


def from_walk(array, groups):
    others = []
    for hop in range(1, groups):
        pairs = [(index, (index - hop) % groups) for index in range(groups)]
        others.append(lax.ppermute(array, "walk", pairs))
    return [array] + others


def radices_of(size):
    radices = []
    while size > 1:
        radices.append(4 if size in (4, 16, 64, 256) else 2)
        size //= radices[-1]
    return radices


def send(array, groups, shards, target, odd_only):
    pairs = []
    for group in range(groups):
        for at in range(shards):
            to = (group, at) if odd_only and at % 2 == 0 else target(group, at)
            pairs.append((group * shards + at, to[0] * shards + to[1]))
    return lax.ppermute(array, ("walk", "param"), pairs)


def total_over_param(array, groups, shards, both):
    def swap(value):
        return send(value, groups, shards, lambda group, at: (group, at ^ 1), False)

    array = array + swap(array)
    stride = 2
    for radix in radices_of(shards // 2):
        terms = [array]
        for mask in range(1, radix):
            jump = mask * stride
            terms.append(
                send(array, groups, shards, lambda group, at: (group, at ^ jump), True)
            )
        array = tree_sum(terms)
        stride *= radix
    totals = [array]
    for hop in range(1, groups if both else 1):
        totals.append(
            send(array, groups, shards, lambda group, at: ((group - hop) % groups, at), True)
        )
    total = jnp.stack(totals)
    odd = lax.axis_index("param") & 1
    return jnp.where(odd == 1, total, swap(total))


def body(jacobian, energies, shifts):
    rows, cols = jacobian.shape
    groups, shards = lax.axis_size("walk"), lax.axis_size("param")
    walkers, params = rows * groups, cols * shards
    vector, part, scalar = (1, cols), (2, LANES), (1, LANES)
    shift_rows = jnp.broadcast_to(shifts[:, None], (shifts.shape[0], LANES))

    (msg,) = call(
        first_kernel,
        [(2, cols + LANES)],
        pltpu.with_memory_space_constraint(jacobian, pltpu.HBM),
        pltpu.with_memory_space_constraint(energies.reshape(1, rows), pltpu.HBM),
        spaces=[pl.BlockSpec(memory_space=pltpu.HBM)] * 2,
        scratch=[
            pltpu.VMEM((rows, cols), jnp.float32),
            pltpu.VMEM((1, rows), jnp.float32),
            pltpu.SemaphoreType.DMA((CHUNKS,)),
            pltpu.SemaphoreType.DMA(()),
        ],
    )
    firsts = from_walk(msg, groups)
    vector0, sent = call(
        functools.partial(project_zero, groups, walkers), [vector, part], jacobian, *firsts
    )
    total = total_over_param(sent, groups, shards, False)
    msg_shape = (1, cols + 2 * LANES)
    msg, norm0 = call(back_kernel, [msg_shape, scalar], jacobian, total)
    msgs = from_walk(msg, groups)
    vector1, sent, state = call(
        functools.partial(project_one, groups, walkers),
        [vector, part, (2, LANES)],
        jacobian,
        *firsts,
        *msgs,
        norm0,
        vector0,
    )
    total = total_over_param(sent, groups, shards, False)
    msg, norm1 = call(back_kernel, [msg_shape, scalar], jacobian, total)
    msgs = from_walk(msg, groups)
    vector2, sent, alpha1 = call(
        functools.partial(project_two, groups, walkers),
        [vector, part, scalar],
        jacobian,
        *firsts,
        *msgs,
        state,
        norm0,
        norm1,
        vector0,
        vector1,
    )
    total = total_over_param(sent, groups, shards, True)
    (update,) = call(
        functools.partial(final_kernel, groups, params),
        [(shifts.shape[0], cols)],
        total,
        shift_rows,
        state,
        alpha1,
        norm0,
        norm1,
        vector0,
        vector1,
        vector2,
    )
    return update


def solution(mesh):
    return jax.shard_map(
        body,
        mesh=mesh,
        in_specs=(P("walk", "param"), P("walk"), P()),
        out_specs=P(None, "param"),
        check_vma=False,
    )
```

```python
import functools

import jax
import jax.numpy as jnp
from jax import lax
from jax.experimental import pallas as pl
from jax.experimental.pallas import tpu as pltpu
from jax.sharding import PartitionSpec as P

LANES = 128
TINY = 1e-37
CHUNKS = 8
GROUP = 8
epsilon = 1e-06


def tree_sum(terms):
    terms = list(terms)
    while len(terms) > 1:
        odd = terms[len(terms) // 2 * 2 :]
        terms = [a + b for a, b in zip(terms[0::2], terms[1::2])] + odd
    return terms[0]


def over_lanes(values):
    total = jnp.sum(values, axis=1, keepdims=True)
    return jnp.broadcast_to(total, (values.shape[0], LANES))


def over_rows(values):
    return jnp.sum(values, axis=0, keepdims=True)


def down_rows(row):
    return jnp.transpose(jnp.broadcast_to(row, (row.shape[1], row.shape[1])))


def centred_weight(row):
    weight = down_rows(row)
    mean = over_rows(weight) / row.shape[1]
    return weight - mean, mean


def each_tile(cols, step, carry):
    count = cols // LANES

    def run(number, carry):
        for part in range(GROUP):
            at = pl.multiple_of((number * GROUP + part) * LANES, LANES)
            carry = step(at, carry)
        return carry

    carry = lax.fori_loop(0, count // GROUP, run, carry)
    for number in range(count // GROUP * GROUP, count):
        carry = step(number * LANES, carry)
    return carry


def cut(count, pieces):
    edges = [count * number // pieces for number in range(pieces + 1)]
    return [(low * LANES, high * LANES) for low, high in zip(edges, edges[1:]) if high > low]


def load_tile(ref, row, at):
    return ref[row : row + 1, pl.ds(at, LANES)]


def first_kernel(jac_hbm, energy_hbm, jac_ref, msg_ref, energy_ref, sems, energy_sem):
    cols = jac_ref.shape[1]
    pieces = cut(cols // LANES, CHUNKS)
    energy_copy = pltpu.make_async_copy(energy_hbm, energy_ref, energy_sem)
    energy_copy.start()
    copies = [
        pltpu.make_async_copy(
            jac_hbm.at[:, low:high], jac_ref.at[:, low:high], sems.at[number]
        )
        for number, (low, high) in enumerate(pieces)
    ]
    for copy in copies:
        copy.start()
    energy_copy.wait()
    weight, mean = centred_weight(energy_ref[...])
    msg_ref[0:1, cols : cols + LANES] = mean
    msg_ref[1:2, cols : cols + LANES] = mean
    for copy, (low, high) in zip(copies, pieces):
        copy.wait()
        for at in range(low, high, LANES):
            block = jac_ref[:, at : at + LANES]
            msg_ref[0:1, at : at + LANES] = over_rows(block * weight)
            msg_ref[1:2, at : at + LANES] = over_rows(block)


def back_kernel(jac_ref, *refs):
    part_refs, (msg_ref, norm_ref) = refs[:-2], refs[-2:]
    cols = jac_ref.shape[1]
    total = tree_sum([ref[...] for ref in part_refs])
    norm_ref[...] = total[1:2]
    weight, mean = centred_weight(total[0:1])

    def step(at, carry):
        msg_ref[:, pl.ds(at, LANES)] = over_rows(jac_ref[:, pl.ds(at, LANES)] * weight)
        return carry

    each_tile(cols, step, 0)
    msg_ref[:, cols : cols + LANES] = mean
    msg_ref[:, cols + LANES : cols + 2 * LANES] = over_rows(weight * weight)


def mean_offsets(means):
    centre = sum(means) / len(means)
    return [mean - centre for mean in means]


def square_total(offsets, squares, rows):
    return sum(squares) + rows * sum([offset * offset for offset in offsets])


def offset_term(offsets, sums):
    if len(sums) == 2:
        return offsets[0] * (sums[0] - sums[1])
    return sum([offset * term for offset, term in zip(offsets, sums)])


def project(jac_ref, firsts, msgs, offsets, scale, olds, vector_ref, part_ref):
    rows, cols = jac_ref.shape

    def step(at, carry):
        acc, square = carry
        value = sum([load_tile(ref, 0, at) for ref in msgs])
        value = value + offset_term(offsets, [load_tile(ref, 1, at) for ref in firsts])
        value = value * scale
        for factor, ref in olds:
            value = value - factor * load_tile(ref, 0, at)
        vector_ref[:, pl.ds(at, LANES)] = value
        return acc + jac_ref[:, pl.ds(at, LANES)] * value, square + value * value

    zeros = jnp.zeros((rows, LANES), jnp.float32), jnp.zeros((1, LANES), jnp.float32)
    acc, square = each_tile(cols, step, zeros)
    part_ref[0:1] = over_rows(jnp.transpose(acc))
    part_ref[1:2] = over_lanes(square)


def project_zero(walkers, jac_ref, *refs):
    firsts, (vector_ref, part_ref) = refs[:-2], refs[-2:]
    cols = jac_ref.shape[1]
    offsets = mean_offsets([ref[0:1, cols : cols + LANES] for ref in firsts])
    scale = jnp.full((1, LANES), 1.0 / walkers, jnp.float32)
    project(jac_ref, firsts, firsts, offsets, scale, [], vector_ref, part_ref)


def message_scalars(msgs, rows, cols):
    offsets = mean_offsets([ref[:, cols : cols + LANES] for ref in msgs])
    squares = [ref[:, cols + LANES : cols + 2 * LANES] for ref in msgs]
    return offsets, square_total(offsets, squares, rows)


def project_one(groups, walkers, jac_ref, *refs):
    firsts, msgs, refs = refs[:groups], refs[groups : 2 * groups], refs[2 * groups :]
    norm_ref, old_ref, vector_ref, part_ref, state_ref = refs
    offsets, square = message_scalars(msgs, *jac_ref.shape)
    alpha = square / (walkers * jnp.maximum(norm_ref[...], TINY))
    scale = 1.0 / (walkers * jnp.maximum(alpha, TINY))
    state_ref[0:1] = alpha
    state_ref[1:2] = scale
    one = jnp.ones((1, LANES), jnp.float32)
    project(jac_ref, firsts, msgs, offsets, scale, [(one, old_ref)], vector_ref, part_ref)


def project_two(groups, jac_ref, *refs):
    firsts, msgs, refs = refs[:groups], refs[groups : 2 * groups], refs[2 * groups :]
    state_ref, norm_old, norm_now, older_ref, old_ref, vector_ref, part_ref, alpha_ref = refs
    offsets, square = message_scalars(msgs, *jac_ref.shape)
    scale = state_ref[1:2]
    alpha = square * scale / jnp.maximum(norm_now[...], TINY)
    alpha_ref[...] = alpha
    beta = norm_now[...] / jnp.maximum(norm_old[...], TINY)
    olds = [(alpha, old_ref), (beta, older_ref)]
    project(jac_ref, firsts, msgs, offsets, scale, olds, vector_ref, part_ref)


def final_kernel(params, *refs):
    refs, vectors, out_ref = refs[:-4], refs[-4:-1], refs[-1]
    part_refs, (shift_ref, state_ref, alpha_ref, norm0_ref, norm1_ref) = refs[:-5], refs[-5:]
    cols = out_ref.shape[1]
    total = tree_sum([ref[...] for ref in part_refs])
    rows = total.shape[2]
    means = [over_lanes(slot[0:1]) / rows for slot in total]
    devs = [slot[0:1] - mean for slot, mean in zip(total, means)]
    squares = [over_lanes(dev * dev) for dev in devs]
    square = square_total(mean_offsets(means), squares, rows)
    norm0, norm1, norm2 = norm0_ref[...], norm1_ref[...], total[0, 1:2]
    alpha0, scale, alpha1 = state_ref[0:1], state_ref[1:2], alpha_ref[...]
    alpha2 = square * scale / jnp.maximum(norm2, TINY)
    beta1 = norm1 / jnp.maximum(norm0, TINY)
    beta2 = norm2 / jnp.maximum(norm1, TINY)
    inverse = 1.0 / jnp.maximum(alpha0, TINY)
    shift = shift_ref[...] * inverse
    pivot0 = 1.0 + shift
    pivot1 = (alpha1 + shift) - beta1 / pivot0
    pivot2 = (alpha2 + shift) - beta2 / pivot1
    right1 = -1.0 / pivot0
    right2 = -right1 / pivot1
    coef2 = right2 / pivot2
    coef1 = (right1 - beta2 * coef2) / pivot1
    coef0 = (1.0 - beta1 * coef1) / pivot0
    coefs = [coef0 * inverse, coef1 * inverse, coef2 * inverse]
    square = sum([coef * coef * norm for coef, norm in zip(coefs, (norm0, norm1, norm2))])
    factor = lax.rsqrt(square / params + epsilon)
    coefs = [coef * factor for coef in coefs]

    def step(at, carry):
        terms = [coef * load_tile(ref, 0, at) for coef, ref in zip(coefs, vectors)]
        out_ref[:, pl.ds(at, LANES)] = terms[0] + terms[1] + terms[2]
        return carry

    each_tile(cols, step, 0)


def call(kernel, outs, *args, spaces=None, scratch=()):
    shapes = [
        jax.ShapeDtypeStruct(out, jnp.float32) if isinstance(out, tuple) else out for out in outs
    ]
    space = pl.BlockSpec(memory_space=pltpu.VMEM)
    return pl.pallas_call(
        kernel,
        out_shape=shapes,
        in_specs=spaces or [space] * len(args),
        out_specs=[space] * len(shapes),
        scratch_shapes=scratch,
        compiler_params=pltpu.CompilerParams(vmem_limit_bytes=24 * 1024 * 1024),
    )(*args)


def from_walk(array, groups):
    others = []
    for hop in range(1, groups):
        pairs = [(index, (index - hop) % groups) for index in range(groups)]
        others.append(lax.ppermute(array, "walk", pairs))
    return [array] + others


def across(array, size, stride, radix):
    out = [array]
    for mask in range(1, radix):
        pairs = [(index, index ^ (mask * stride)) for index in range(size)]
        out.append(lax.ppermute(array, "param", pairs))
    return out


def param_parts(array, size, stride):
    while size > stride:
        radix = 4 if size // stride % 4 == 0 else 2
        parts = across(array, size, stride, radix)
        stride *= radix
        if stride == size:
            return parts
        array = tree_sum(parts)
    return [array]


def other_group(array, size, jump):
    pairs = [
        (group * size + index, (1 - group) * size + (index ^ jump))
        for group in range(2)
        for index in range(size)
    ]
    return lax.ppermute(array, ("walk", "param"), pairs)


def last_parts(array, groups, size):
    if groups == 2 and size % 4 == 0:
        array = tree_sum(across(array, size, 1, 2))
        others = [other_group(array, size, jump) for jump in (0, 2)]
        array = jnp.stack([tree_sum(across(array, size, 2, 2)), tree_sum(others)])
        return param_parts(array, size, 4)
    total = tree_sum(param_parts(array, size, 1))
    return [jnp.stack(from_walk(total, groups))]


def body(jacobian, energies, shifts):
    rows, cols = jacobian.shape
    groups, shards = lax.axis_size("walk"), lax.axis_size("param")
    walkers, params = rows * groups, cols * shards
    vector, part, scalar = (1, cols), (2, LANES), (1, LANES)
    msg_shape = (1, cols + 2 * LANES)
    shift_rows = jnp.broadcast_to(shifts[:, None], (shifts.shape[0], LANES))

    jacobian, msg = call(
        first_kernel,
        [pltpu.VMEM((rows, cols), jnp.float32), (2, cols + LANES)],
        pltpu.with_memory_space_constraint(jacobian, pltpu.HBM),
        pltpu.with_memory_space_constraint(energies.reshape(1, rows), pltpu.HBM),
        spaces=[pl.BlockSpec(memory_space=pltpu.HBM)] * 2,
        scratch=[
            pltpu.VMEM((1, rows), jnp.float32),
            pltpu.SemaphoreType.DMA((CHUNKS,)),
            pltpu.SemaphoreType.DMA(()),
        ],
    )
    firsts = from_walk(msg, groups)
    vector0, sent = call(
        functools.partial(project_zero, walkers), [vector, part], jacobian, *firsts
    )
    parts = param_parts(sent, shards, 1)
    msg, norm0 = call(back_kernel, [msg_shape, scalar], jacobian, *parts)
    msgs = from_walk(msg, groups)
    vector1, sent, state = call(
        functools.partial(project_one, groups, walkers),
        [vector, part, (2, LANES)],
        jacobian,
        *firsts,
        *msgs,
        norm0,
        vector0,
    )
    parts = param_parts(sent, shards, 1)
    msg, norm1 = call(back_kernel, [msg_shape, scalar], jacobian, *parts)
    msgs = from_walk(msg, groups)
    vector2, sent, alpha1 = call(
        functools.partial(project_two, groups),
        [vector, part, scalar],
        jacobian,
        *firsts,
        *msgs,
        state,
        norm0,
        norm1,
        vector0,
        vector1,
    )
    (update,) = call(
        functools.partial(final_kernel, params),
        [(shifts.shape[0], cols)],
        *last_parts(sent, groups, shards),
        shift_rows,
        state,
        alpha1,
        norm0,
        norm1,
        vector0,
        vector1,
        vector2,
    )
    return update


def solution(mesh):
    return jax.shard_map(
        body,
        mesh=mesh,
        in_specs=(P("walk", "param"), P("walk"), P()),
        out_specs=P(None, "param"),
        check_vma=False,
    )
```

```python
import functools

import jax
import jax.numpy as jnp
from jax import lax
from jax.experimental import pallas as pl
from jax.experimental.pallas import tpu as pltpu
from jax.sharding import PartitionSpec as P

LANES = 128
TINY = 1e-37
CHUNKS = 8
GROUP = 8
epsilon = 1e-06


def tree_sum(terms):
    terms = list(terms)
    while len(terms) > 1:
        odd = terms[len(terms) // 2 * 2 :]
        terms = [a + b for a, b in zip(terms[0::2], terms[1::2])] + odd
    return terms[0]


def over_lanes(values):
    total = jnp.sum(values, axis=1, keepdims=True)
    return jnp.broadcast_to(total, (values.shape[0], LANES))


def over_rows(values):
    return jnp.sum(values, axis=0, keepdims=True)


def down_rows(row):
    return jnp.transpose(jnp.broadcast_to(row, (row.shape[1], row.shape[1])))


def centred_weight(row):
    weight = down_rows(row)
    mean = over_rows(weight) / row.shape[1]
    return weight - mean, mean


def each_tile(cols, step, carry):
    count = cols // LANES

    def run(number, carry):
        for part in range(GROUP):
            at = pl.multiple_of((number * GROUP + part) * LANES, LANES)
            carry = step(at, carry)
        return carry

    carry = lax.fori_loop(0, count // GROUP, run, carry)
    for number in range(count // GROUP * GROUP, count):
        carry = step(number * LANES, carry)
    return carry


def cut(count, pieces):
    edges = [count * number // pieces for number in range(pieces + 1)]
    return [(low * LANES, high * LANES) for low, high in zip(edges, edges[1:]) if high > low]


def load_tile(ref, row, at):
    return ref[row : row + 1, pl.ds(at, LANES)]


def first_kernel(jac_hbm, energy_hbm, jac_ref, msg_ref, energy_ref, sems, energy_sem):
    cols = jac_ref.shape[1]
    pieces = cut(cols // LANES, CHUNKS)
    energy_copy = pltpu.make_async_copy(energy_hbm, energy_ref, energy_sem)
    energy_copy.start()
    copies = [
        pltpu.make_async_copy(
            jac_hbm.at[:, low:high], jac_ref.at[:, low:high], sems.at[number]
        )
        for number, (low, high) in enumerate(pieces)
    ]
    for copy in copies:
        copy.start()
    energy_copy.wait()
    weight, mean = centred_weight(energy_ref[...])
    msg_ref[0:1, cols : cols + LANES] = mean
    msg_ref[1:2, cols : cols + LANES] = mean
    for copy, (low, high) in zip(copies, pieces):
        copy.wait()
        for at in range(low, high, LANES):
            block = jac_ref[:, at : at + LANES]
            msg_ref[0:1, at : at + LANES] = over_rows(block * weight)
            msg_ref[1:2, at : at + LANES] = over_rows(block)


def back_kernel(jac_ref, *refs):
    part_refs, (msg_ref, norm_ref) = refs[:-2], refs[-2:]
    cols = jac_ref.shape[1]
    total = tree_sum([ref[...] for ref in part_refs])
    norm_ref[...] = total[1:2]
    weight, mean = centred_weight(total[0:1])

    def step(at, carry):
        msg_ref[:, pl.ds(at, LANES)] = over_rows(jac_ref[:, pl.ds(at, LANES)] * weight)
        return carry

    each_tile(cols, step, 0)
    msg_ref[:, cols : cols + LANES] = mean
    msg_ref[:, cols + LANES : cols + 2 * LANES] = over_rows(weight * weight)


def mean_offsets(means):
    centre = sum(means) / len(means)
    return [mean - centre for mean in means]


def square_total(offsets, squares, rows):
    return sum(squares) + rows * sum([offset * offset for offset in offsets])


def offset_term(offsets, sums):
    if len(sums) == 2:
        return offsets[0] * (sums[0] - sums[1])
    return sum([offset * term for offset, term in zip(offsets, sums)])


def project(jac_ref, firsts, msgs, offsets, scale, olds, vector_ref, part_ref):
    rows, cols = jac_ref.shape

    def step(at, carry):
        acc, square = carry
        value = sum([load_tile(ref, 0, at) for ref in msgs])
        value = value + offset_term(offsets, [load_tile(ref, 1, at) for ref in firsts])
        value = value * scale
        for factor, ref in olds:
            value = value - factor * load_tile(ref, 0, at)
        vector_ref[:, pl.ds(at, LANES)] = value
        return acc + jac_ref[:, pl.ds(at, LANES)] * value, square + value * value

    zeros = jnp.zeros((rows, LANES), jnp.float32), jnp.zeros((1, LANES), jnp.float32)
    acc, square = each_tile(cols, step, zeros)
    part_ref[0:1] = over_rows(jnp.transpose(acc))
    part_ref[1:2] = over_lanes(square)


def project_zero(walkers, jac_ref, *refs):
    firsts, (vector_ref, part_ref) = refs[:-2], refs[-2:]
    cols = jac_ref.shape[1]
    offsets = mean_offsets([ref[0:1, cols : cols + LANES] for ref in firsts])
    scale = jnp.full((1, LANES), 1.0 / walkers, jnp.float32)
    project(jac_ref, firsts, firsts, offsets, scale, [], vector_ref, part_ref)


def message_scalars(msgs, rows, cols):
    offsets = mean_offsets([ref[:, cols : cols + LANES] for ref in msgs])
    squares = [ref[:, cols + LANES : cols + 2 * LANES] for ref in msgs]
    return offsets, square_total(offsets, squares, rows)


def project_one(groups, walkers, jac_ref, *refs):
    firsts, msgs, refs = refs[:groups], refs[groups : 2 * groups], refs[2 * groups :]
    norm_ref, old_ref, vector_ref, part_ref, state_ref = refs
    offsets, square = message_scalars(msgs, *jac_ref.shape)
    alpha = square / (walkers * jnp.maximum(norm_ref[...], TINY))
    scale = 1.0 / (walkers * jnp.maximum(alpha, TINY))
    state_ref[0:1] = alpha
    state_ref[1:2] = scale
    one = jnp.ones((1, LANES), jnp.float32)
    project(jac_ref, firsts, msgs, offsets, scale, [(one, old_ref)], vector_ref, part_ref)


def project_two(groups, jac_ref, *refs):
    firsts, msgs, refs = refs[:groups], refs[groups : 2 * groups], refs[2 * groups :]
    state_ref, norm_old, norm_now, older_ref, old_ref, vector_ref, part_ref, alpha_ref = refs
    offsets, square = message_scalars(msgs, *jac_ref.shape)
    scale = state_ref[1:2]
    alpha = square * scale / jnp.maximum(norm_now[...], TINY)
    alpha_ref[...] = alpha
    beta = norm_now[...] / jnp.maximum(norm_old[...], TINY)
    olds = [(alpha, old_ref), (beta, older_ref)]
    project(jac_ref, firsts, msgs, offsets, scale, olds, vector_ref, part_ref)


def final_kernel(params, *refs):
    refs, vectors, out_ref = refs[:-4], refs[-4:-1], refs[-1]
    part_refs, (shift_ref, state_ref, alpha_ref, norm0_ref, norm1_ref) = refs[:-5], refs[-5:]
    cols = out_ref.shape[1]
    total = tree_sum([ref[...] for ref in part_refs])
    rows = total.shape[2]
    means = [over_lanes(slot[0:1]) / rows for slot in total]
    devs = [slot[0:1] - mean for slot, mean in zip(total, means)]
    squares = [over_lanes(dev * dev) for dev in devs]
    square = square_total(mean_offsets(means), squares, rows)
    norm0, norm1, norm2 = norm0_ref[...], norm1_ref[...], total[0, 1:2]
    alpha0, scale, alpha1 = state_ref[0:1], state_ref[1:2], alpha_ref[...]
    alpha2 = square * scale / jnp.maximum(norm2, TINY)
    beta1 = norm1 / jnp.maximum(norm0, TINY)
    beta2 = norm2 / jnp.maximum(norm1, TINY)
    inverse = 1.0 / jnp.maximum(alpha0, TINY)
    shift = shift_ref[...] * inverse
    pivot0 = 1.0 + shift
    pivot1 = (alpha1 + shift) - beta1 / pivot0
    pivot2 = (alpha2 + shift) - beta2 / pivot1
    right1 = -1.0 / pivot0
    right2 = -right1 / pivot1
    coef2 = right2 / pivot2
    coef1 = (right1 - beta2 * coef2) / pivot1
    coef0 = (1.0 - beta1 * coef1) / pivot0
    coefs = [coef0 * inverse, coef1 * inverse, coef2 * inverse]
    square = sum([coef * coef * norm for coef, norm in zip(coefs, (norm0, norm1, norm2))])
    factor = lax.rsqrt(square / params + epsilon)
    coefs = [coef * factor for coef in coefs]

    def step(at, carry):
        terms = [coef * load_tile(ref, 0, at) for coef, ref in zip(coefs, vectors)]
        out_ref[:, pl.ds(at, LANES)] = terms[0] + terms[1] + terms[2]
        return carry

    each_tile(cols, step, 0)


def call(kernel, outs, *args, spaces=None, scratch=()):
    shapes = [
        jax.ShapeDtypeStruct(out, jnp.float32) if isinstance(out, tuple) else out for out in outs
    ]
    space = pl.BlockSpec(memory_space=pltpu.VMEM)
    return pl.pallas_call(
        kernel,
        out_shape=shapes,
        in_specs=spaces or [space] * len(args),
        out_specs=[space] * len(shapes),
        scratch_shapes=scratch,
        compiler_params=pltpu.CompilerParams(vmem_limit_bytes=24 * 1024 * 1024),
    )(*args)


def from_walk(array, groups):
    others = []
    for hop in range(1, groups):
        pairs = [(index, (index - hop) % groups) for index in range(groups)]
        others.append(lax.ppermute(array, "walk", pairs))
    return [array] + others


def across(array, size, stride, radix):
    out = [array]
    for mask in range(radix - 1, 0, -1):
        pairs = [(index, index ^ (mask * stride)) for index in range(size)]
        out.append(lax.ppermute(array, "param", pairs))
    return out


def param_parts(array, size, stride):
    while size > stride:
        radix = 4 if size // stride % 4 == 0 else 2
        parts = across(array, size, stride, radix)
        stride *= radix
        if stride == size:
            return parts
        array = tree_sum(parts)
    return [array]


def other_group(array, size, jump):
    pairs = [
        (group * size + index, (1 - group) * size + (index ^ jump))
        for group in range(2)
        for index in range(size)
    ]
    return lax.ppermute(array, ("walk", "param"), pairs)


def last_parts(array, groups, size):
    if groups == 2 and size % 4 == 0:
        array = tree_sum(across(array, size, 1, 2))
        others = [other_group(array, size, jump) for jump in (2, 0)]
        own = tree_sum(across(array, size, 2, 2))
        array = jnp.stack([own, tree_sum(others)])
        return param_parts(array, size, 4)
    total = tree_sum(param_parts(array, size, 1))
    return [jnp.stack(from_walk(total, groups))]


def body(jacobian, energies, shifts):
    rows, cols = jacobian.shape
    groups, shards = lax.axis_size("walk"), lax.axis_size("param")
    walkers, params = rows * groups, cols * shards
    vector, part, scalar = (1, cols), (2, LANES), (1, LANES)
    msg_shape = (1, cols + 2 * LANES)
    shift_rows = jnp.broadcast_to(shifts[:, None], (shifts.shape[0], LANES))

    jacobian, msg = call(
        first_kernel,
        [pltpu.VMEM((rows, cols), jnp.float32), (2, cols + LANES)],
        pltpu.with_memory_space_constraint(jacobian, pltpu.HBM),
        pltpu.with_memory_space_constraint(energies.reshape(1, rows), pltpu.HBM),
        spaces=[pl.BlockSpec(memory_space=pltpu.HBM)] * 2,
        scratch=[
            pltpu.VMEM((1, rows), jnp.float32),
            pltpu.SemaphoreType.DMA((CHUNKS,)),
            pltpu.SemaphoreType.DMA(()),
        ],
    )
    firsts = from_walk(msg, groups)
    vector0, sent = call(
        functools.partial(project_zero, walkers), [vector, part], jacobian, *firsts
    )
    parts = param_parts(sent, shards, 1)
    msg, norm0 = call(back_kernel, [msg_shape, scalar], jacobian, *parts)
    msgs = from_walk(msg, groups)
    vector1, sent, state = call(
        functools.partial(project_one, groups, walkers),
        [vector, part, (2, LANES)],
        jacobian,
        *firsts,
        *msgs,
        norm0,
        vector0,
    )
    parts = param_parts(sent, shards, 1)
    msg, norm1 = call(back_kernel, [msg_shape, scalar], jacobian, *parts)
    msgs = from_walk(msg, groups)
    vector2, sent, alpha1 = call(
        functools.partial(project_two, groups),
        [vector, part, scalar],
        jacobian,
        *firsts,
        *msgs,
        state,
        norm0,
        norm1,
        vector0,
        vector1,
    )
    (update,) = call(
        functools.partial(final_kernel, params),
        [(shifts.shape[0], cols)],
        *last_parts(sent, groups, shards),
        shift_rows,
        state,
        alpha1,
        norm0,
        norm1,
        vector0,
        vector1,
        vector2,
    )
    return update


def solution(mesh):
    return jax.shard_map(
        body,
        mesh=mesh,
        in_specs=(P("walk", "param"), P("walk"), P()),
        out_specs=P(None, "param"),
        check_vma=False,
    )
```

```python
import functools

import jax
import jax.numpy as jnp
from jax import lax
from jax.experimental import pallas as pl
from jax.experimental.pallas import tpu as pltpu
from jax.sharding import PartitionSpec as P

LANES = 128
TINY = 1e-37
CHUNKS = 8
GROUP = 8
epsilon = 1e-06


def tree_sum(terms):
    terms = list(terms)
    while len(terms) > 1:
        odd = terms[len(terms) // 2 * 2 :]
        terms = [a + b for a, b in zip(terms[0::2], terms[1::2])] + odd
    return terms[0]


def over_lanes(values):
    total = jnp.sum(values, axis=1, keepdims=True)
    return jnp.broadcast_to(total, (values.shape[0], LANES))


def over_rows(values):
    return jnp.sum(values, axis=0, keepdims=True)


def down_rows(row):
    return jnp.transpose(jnp.broadcast_to(row, (row.shape[1], row.shape[1])))


def centred_weight(row):
    weight = down_rows(row)
    mean = over_rows(weight) / row.shape[1]
    return weight - mean, mean


def each_tile(cols, step, carry):
    count = cols // LANES

    def run(number, carry):
        for part in range(GROUP):
            at = pl.multiple_of((number * GROUP + part) * LANES, LANES)
            carry = step(at, carry)
        return carry

    carry = lax.fori_loop(0, count // GROUP, run, carry)
    for number in range(count // GROUP * GROUP, count):
        carry = step(number * LANES, carry)
    return carry


def cut(count, pieces):
    edges = [count * number // pieces for number in range(pieces + 1)]
    return [(low * LANES, high * LANES) for low, high in zip(edges, edges[1:]) if high > low]


def load_tile(ref, row, at):
    return ref[row : row + 1, pl.ds(at, LANES)]


def first_kernel(jac_hbm, energy_hbm, jac_ref, msg_ref, energy_ref, sems, energy_sem):
    cols = jac_ref.shape[1]
    pieces = cut(cols // LANES, CHUNKS)
    energy_copy = pltpu.make_async_copy(energy_hbm, energy_ref, energy_sem)
    energy_copy.start()
    copies = [
        pltpu.make_async_copy(
            jac_hbm.at[:, low:high], jac_ref.at[:, low:high], sems.at[number]
        )
        for number, (low, high) in enumerate(pieces)
    ]
    for copy in copies:
        copy.start()
    energy_copy.wait()
    weight, mean = centred_weight(energy_ref[...])
    msg_ref[0:1, cols : cols + LANES] = mean
    msg_ref[1:2, cols : cols + LANES] = mean
    for copy, (low, high) in zip(copies, pieces):
        copy.wait()
        for at in range(low, high, LANES):
            block = jac_ref[:, at : at + LANES]
            msg_ref[0:1, at : at + LANES] = over_rows(block * weight)
            msg_ref[1:2, at : at + LANES] = over_rows(block)


def back_kernel(jac_ref, *refs):
    part_refs, (msg_ref, norm_ref) = refs[:-2], refs[-2:]
    cols = jac_ref.shape[1]
    total = tree_sum([ref[...] for ref in part_refs])
    norm_ref[...] = total[1:2]
    weight, mean = centred_weight(total[0:1])

    def step(at, carry):
        msg_ref[:, pl.ds(at, LANES)] = over_rows(jac_ref[:, pl.ds(at, LANES)] * weight)
        return carry

    each_tile(cols, step, 0)
    msg_ref[:, cols : cols + LANES] = mean
    msg_ref[:, cols + LANES : cols + 2 * LANES] = over_rows(weight * weight)


def mean_offsets(means):
    centre = sum(means) / len(means)
    return [mean - centre for mean in means]


def square_total(offsets, squares, rows):
    return sum(squares) + rows * sum([offset * offset for offset in offsets])


def offset_term(offsets, sums):
    if len(sums) == 2:
        return offsets[0] * (sums[0] - sums[1])
    return sum([offset * term for offset, term in zip(offsets, sums)])


def project(jac_ref, firsts, msgs, offsets, scale, olds, vector_ref, part_ref):
    rows, cols = jac_ref.shape

    def step(at, carry):
        acc, square = carry
        value = sum([load_tile(ref, 0, at) for ref in msgs])
        value = value + offset_term(offsets, [load_tile(ref, 1, at) for ref in firsts])
        value = value * scale
        for factor, ref in olds:
            value = value - factor * load_tile(ref, 0, at)
        vector_ref[:, pl.ds(at, LANES)] = value
        return acc + jac_ref[:, pl.ds(at, LANES)] * value, square + value * value

    zeros = jnp.zeros((rows, LANES), jnp.float32), jnp.zeros((1, LANES), jnp.float32)
    acc, square = each_tile(cols, step, zeros)
    part_ref[0:1] = over_rows(jnp.transpose(acc))
    part_ref[1:2] = over_lanes(square)


def project_zero(walkers, jac_ref, *refs):
    firsts, (vector_ref, part_ref) = refs[:-2], refs[-2:]
    cols = jac_ref.shape[1]
    offsets = mean_offsets([ref[0:1, cols : cols + LANES] for ref in firsts])
    scale = jnp.full((1, LANES), 1.0 / walkers, jnp.float32)
    project(jac_ref, firsts, firsts, offsets, scale, [], vector_ref, part_ref)


def message_scalars(msgs, rows, cols):
    offsets = mean_offsets([ref[:, cols : cols + LANES] for ref in msgs])
    squares = [ref[:, cols + LANES : cols + 2 * LANES] for ref in msgs]
    return offsets, square_total(offsets, squares, rows)


def project_one(groups, walkers, jac_ref, *refs):
    firsts, msgs, refs = refs[:groups], refs[groups : 2 * groups], refs[2 * groups :]
    norm_ref, old_ref, vector_ref, part_ref, state_ref = refs
    offsets, square = message_scalars(msgs, *jac_ref.shape)
    alpha = square / (walkers * jnp.maximum(norm_ref[...], TINY))
    scale = 1.0 / (walkers * jnp.maximum(alpha, TINY))
    state_ref[0:1] = alpha
    state_ref[1:2] = scale
    one = jnp.ones((1, LANES), jnp.float32)
    project(jac_ref, firsts, msgs, offsets, scale, [(one, old_ref)], vector_ref, part_ref)


def project_two(groups, jac_ref, *refs):
    firsts, msgs, refs = refs[:groups], refs[groups : 2 * groups], refs[2 * groups :]
    state_ref, norm_old, norm_now, older_ref, old_ref, vector_ref, part_ref, alpha_ref = refs
    offsets, square = message_scalars(msgs, *jac_ref.shape)
    scale = state_ref[1:2]
    alpha = square * scale / jnp.maximum(norm_now[...], TINY)
    alpha_ref[...] = alpha
    beta = norm_now[...] / jnp.maximum(norm_old[...], TINY)
    olds = [(alpha, old_ref), (beta, older_ref)]
    project(jac_ref, firsts, msgs, offsets, scale, olds, vector_ref, part_ref)


def final_kernel(params, *refs):
    refs, vectors, out_ref = refs[:-4], refs[-4:-1], refs[-1]
    part_refs, (shift_ref, state_ref, alpha_ref, norm0_ref, norm1_ref) = refs[:-5], refs[-5:]
    cols = out_ref.shape[1]
    total = tree_sum([ref[...] for ref in part_refs])
    rows = total.shape[2]
    means = [over_lanes(slot[0:1]) / rows for slot in total]
    devs = [slot[0:1] - mean for slot, mean in zip(total, means)]
    squares = [over_lanes(dev * dev) for dev in devs]
    square = square_total(mean_offsets(means), squares, rows)
    norm0, norm1, norm2 = norm0_ref[...], norm1_ref[...], total[0, 1:2]
    alpha0, scale, alpha1 = state_ref[0:1], state_ref[1:2], alpha_ref[...]
    alpha2 = square * scale / jnp.maximum(norm2, TINY)
    beta1 = norm1 / jnp.maximum(norm0, TINY)
    beta2 = norm2 / jnp.maximum(norm1, TINY)
    inverse = 1.0 / jnp.maximum(alpha0, TINY)
    shift = shift_ref[...] * inverse
    pivot0 = 1.0 + shift
    pivot1 = (alpha1 + shift) - beta1 / pivot0
    pivot2 = (alpha2 + shift) - beta2 / pivot1
    right1 = -1.0 / pivot0
    right2 = -right1 / pivot1
    coef2 = right2 / pivot2
    coef1 = (right1 - beta2 * coef2) / pivot1
    coef0 = (1.0 - beta1 * coef1) / pivot0
    coefs = [coef0 * inverse, coef1 * inverse, coef2 * inverse]
    square = sum([coef * coef * norm for coef, norm in zip(coefs, (norm0, norm1, norm2))])
    factor = lax.rsqrt(square / params + epsilon)
    coefs = [coef * factor for coef in coefs]

    def step(at, carry):
        terms = [coef * load_tile(ref, 0, at) for coef, ref in zip(coefs, vectors)]
        out_ref[:, pl.ds(at, LANES)] = terms[0] + terms[1] + terms[2]
        return carry

    each_tile(cols, step, 0)


def call(kernel, outs, *args, spaces=None, scratch=()):
    shapes = [
        jax.ShapeDtypeStruct(out, jnp.float32) if isinstance(out, tuple) else out for out in outs
    ]
    space = pl.BlockSpec(memory_space=pltpu.VMEM)
    return pl.pallas_call(
        kernel,
        out_shape=shapes,
        in_specs=spaces or [space] * len(args),
        out_specs=[space] * len(shapes),
        scratch_shapes=scratch,
        compiler_params=pltpu.CompilerParams(vmem_limit_bytes=24 * 1024 * 1024),
    )(*args)


def from_walk(array, groups):
    others = []
    for hop in range(1, groups):
        pairs = [(index, (index - hop) % groups) for index in range(groups)]
        others.append(lax.ppermute(array, "walk", pairs))
    return [array] + others


def slot_sums(array, groups):
    slot = jnp.arange(groups)[:, None, None] == lax.axis_index("walk")
    return lax.psum(jnp.where(slot, array[None], 0.0), ("walk", "param"))


def own_sum(array, groups):
    sums = slot_sums(array, groups)
    own = lax.dynamic_index_in_dim(sums, lax.axis_index("walk"), 0, keepdims=False)
    return jnp.where(jnp.arange(2)[:, None] == 0, own, sums[0])


def body(jacobian, energies, shifts):
    rows, cols = jacobian.shape
    groups, shards = lax.axis_size("walk"), lax.axis_size("param")
    walkers, params = rows * groups, cols * shards
    vector, part, scalar = (1, cols), (2, LANES), (1, LANES)
    msg_shape = (1, cols + 2 * LANES)
    shift_rows = jnp.broadcast_to(shifts[:, None], (shifts.shape[0], LANES))

    jacobian, msg = call(
        first_kernel,
        [pltpu.VMEM((rows, cols), jnp.float32), (2, cols + LANES)],
        pltpu.with_memory_space_constraint(jacobian, pltpu.HBM),
        pltpu.with_memory_space_constraint(energies.reshape(1, rows), pltpu.HBM),
        spaces=[pl.BlockSpec(memory_space=pltpu.HBM)] * 2,
        scratch=[
            pltpu.VMEM((1, rows), jnp.float32),
            pltpu.SemaphoreType.DMA((CHUNKS,)),
            pltpu.SemaphoreType.DMA(()),
        ],
    )
    firsts = from_walk(msg, groups)
    vector0, sent = call(
        functools.partial(project_zero, walkers), [vector, part], jacobian, *firsts
    )
    parts = [own_sum(sent, groups)]
    msg, norm0 = call(back_kernel, [msg_shape, scalar], jacobian, *parts)
    msgs = from_walk(msg, groups)
    vector1, sent, state = call(
        functools.partial(project_one, groups, walkers),
        [vector, part, (2, LANES)],
        jacobian,
        *firsts,
        *msgs,
        norm0,
        vector0,
    )
    parts = [own_sum(sent, groups)]
    msg, norm1 = call(back_kernel, [msg_shape, scalar], jacobian, *parts)
    msgs = from_walk(msg, groups)
    vector2, sent, alpha1 = call(
        functools.partial(project_two, groups),
        [vector, part, scalar],
        jacobian,
        *firsts,
        *msgs,
        state,
        norm0,
        norm1,
        vector0,
        vector1,
    )
    (update,) = call(
        functools.partial(final_kernel, params),
        [(shifts.shape[0], cols)],
        slot_sums(sent, groups),
        shift_rows,
        state,
        alpha1,
        norm0,
        norm1,
        vector0,
        vector1,
        vector2,
    )
    return update


def solution(mesh):
    return jax.shard_map(
        body,
        mesh=mesh,
        in_specs=(P("walk", "param"), P("walk"), P()),
        out_specs=P(None, "param"),
        check_vma=False,
    )
```

```python
import functools

import jax
import jax.numpy as jnp
from jax import lax
from jax.experimental import pallas as pl
from jax.experimental.pallas import tpu as pltpu
from jax.sharding import PartitionSpec as P

LANES = 128
TINY = 1e-37
CHUNKS = 8
GROUP = 8
epsilon = 1e-06


def tree_sum(terms):
    terms = list(terms)
    while len(terms) > 1:
        odd = terms[len(terms) // 2 * 2 :]
        terms = [a + b for a, b in zip(terms[0::2], terms[1::2])] + odd
    return terms[0]


def over_lanes(values):
    total = jnp.sum(values, axis=1, keepdims=True)
    return jnp.broadcast_to(total, (values.shape[0], LANES))


def over_rows(values):
    return jnp.sum(values, axis=0, keepdims=True)


def down_rows(row):
    return jnp.transpose(jnp.broadcast_to(row, (row.shape[1], row.shape[1])))


def centred_weight(row):
    weight = down_rows(row)
    mean = over_rows(weight) / row.shape[1]
    return weight - mean, mean


def each_tile(cols, step, carry):
    count = cols // LANES

    def run(number, carry):
        for part in range(GROUP):
            at = pl.multiple_of((number * GROUP + part) * LANES, LANES)
            carry = step(at, carry)
        return carry

    carry = lax.fori_loop(0, count // GROUP, run, carry)
    for number in range(count // GROUP * GROUP, count):
        carry = step(number * LANES, carry)
    return carry


def cut(count, pieces):
    edges = [count * number // pieces for number in range(pieces + 1)]
    return [(low * LANES, high * LANES) for low, high in zip(edges, edges[1:]) if high > low]


def load_tile(ref, row, at):
    return ref[row : row + 1, pl.ds(at, LANES)]


def first_kernel(jac_hbm, energy_hbm, jac_ref, msg_ref, energy_ref, sems, energy_sem):
    cols = jac_ref.shape[1]
    pieces = cut(cols // LANES, CHUNKS)
    energy_copy = pltpu.make_async_copy(energy_hbm, energy_ref, energy_sem)
    energy_copy.start()
    copies = [
        pltpu.make_async_copy(
            jac_hbm.at[:, low:high], jac_ref.at[:, low:high], sems.at[number]
        )
        for number, (low, high) in enumerate(pieces)
    ]
    for number, copy in enumerate(copies):
        copy.start(priority=number % 2)
    energy_copy.wait()
    weight, mean = centred_weight(energy_ref[...])
    msg_ref[0:1, cols : cols + LANES] = mean
    msg_ref[1:2, cols : cols + LANES] = mean
    for copy, (low, high) in zip(copies, pieces):
        copy.wait()
        for at in range(low, high, LANES):
            block = jac_ref[:, at : at + LANES]
            msg_ref[0:1, at : at + LANES] = over_rows(block * weight)
            msg_ref[1:2, at : at + LANES] = over_rows(block)


def back_kernel(jac_ref, *refs):
    part_refs, (msg_ref, norm_ref) = refs[:-2], refs[-2:]
    cols = jac_ref.shape[1]
    total = tree_sum([ref[...] for ref in part_refs])
    norm_ref[...] = total[1:2]
    weight, mean = centred_weight(total[0:1])

    def step(at, carry):
        msg_ref[:, pl.ds(at, LANES)] = over_rows(jac_ref[:, pl.ds(at, LANES)] * weight)
        return carry

    each_tile(cols, step, 0)
    msg_ref[:, cols : cols + LANES] = mean
    msg_ref[:, cols + LANES : cols + 2 * LANES] = over_rows(weight * weight)


def mean_offsets(means):
    centre = sum(means) / len(means)
    return [mean - centre for mean in means]


def square_total(offsets, squares, rows):
    return sum(squares) + rows * sum([offset * offset for offset in offsets])


def offset_term(offsets, sums):
    if len(sums) == 2:
        return offsets[0] * (sums[0] - sums[1])
    return sum([offset * term for offset, term in zip(offsets, sums)])


def project(jac_ref, firsts, msgs, offsets, scale, olds, vector_ref, part_ref):
    rows, cols = jac_ref.shape

    def step(at, carry):
        acc, square = carry
        value = sum([load_tile(ref, 0, at) for ref in msgs])
        value = value + offset_term(offsets, [load_tile(ref, 1, at) for ref in firsts])
        value = value * scale
        for factor, ref in olds:
            value = value - factor * load_tile(ref, 0, at)
        vector_ref[:, pl.ds(at, LANES)] = value
        return acc + jac_ref[:, pl.ds(at, LANES)] * value, square + value * value

    zeros = jnp.zeros((rows, LANES), jnp.float32), jnp.zeros((1, LANES), jnp.float32)
    acc, square = each_tile(cols, step, zeros)
    part_ref[0:1] = over_rows(jnp.transpose(acc))
    part_ref[1:2] = over_lanes(square)


def project_zero(walkers, jac_ref, *refs):
    firsts, (vector_ref, part_ref) = refs[:-2], refs[-2:]
    cols = jac_ref.shape[1]
    offsets = mean_offsets([ref[0:1, cols : cols + LANES] for ref in firsts])
    scale = jnp.full((1, LANES), 1.0 / walkers, jnp.float32)
    project(jac_ref, firsts, firsts, offsets, scale, [], vector_ref, part_ref)


def message_scalars(msgs, rows, cols):
    offsets = mean_offsets([ref[:, cols : cols + LANES] for ref in msgs])
    squares = [ref[:, cols + LANES : cols + 2 * LANES] for ref in msgs]
    return offsets, square_total(offsets, squares, rows)


def project_one(groups, walkers, jac_ref, *refs):
    firsts, msgs, refs = refs[:groups], refs[groups : 2 * groups], refs[2 * groups :]
    norm_ref, old_ref, vector_ref, part_ref, state_ref = refs
    offsets, square = message_scalars(msgs, *jac_ref.shape)
    alpha = square / (walkers * jnp.maximum(norm_ref[...], TINY))
    scale = 1.0 / (walkers * jnp.maximum(alpha, TINY))
    state_ref[0:1] = alpha
    state_ref[1:2] = scale
    one = jnp.ones((1, LANES), jnp.float32)
    project(jac_ref, firsts, msgs, offsets, scale, [(one, old_ref)], vector_ref, part_ref)


def project_two(groups, jac_ref, *refs):
    firsts, msgs, refs = refs[:groups], refs[groups : 2 * groups], refs[2 * groups :]
    state_ref, norm_old, norm_now, older_ref, old_ref, vector_ref, part_ref, alpha_ref = refs
    offsets, square = message_scalars(msgs, *jac_ref.shape)
    scale = state_ref[1:2]
    alpha = square * scale / jnp.maximum(norm_now[...], TINY)
    alpha_ref[...] = alpha
    beta = norm_now[...] / jnp.maximum(norm_old[...], TINY)
    olds = [(alpha, old_ref), (beta, older_ref)]
    project(jac_ref, firsts, msgs, offsets, scale, olds, vector_ref, part_ref)


def final_kernel(params, *refs):
    refs, vectors, out_ref = refs[:-4], refs[-4:-1], refs[-1]
    sum_refs, (shift_ref, state_ref, alpha_ref, norm0_ref, norm1_ref) = refs[:-5], refs[-5:]
    cols = out_ref.shape[1]
    lines = [ref[0:1] for ref in sum_refs]
    rows = lines[0].shape[1]
    means = [over_lanes(line) / rows for line in lines]
    devs = [line - mean for line, mean in zip(lines, means)]
    squares = [over_lanes(dev * dev) for dev in devs]
    square = square_total(mean_offsets(means), squares, rows)
    norm0, norm1, norm2 = norm0_ref[...], norm1_ref[...], sum_refs[0][1:2]
    alpha0, scale, alpha1 = state_ref[0:1], state_ref[1:2], alpha_ref[...]
    alpha2 = square * scale / jnp.maximum(norm2, TINY)
    beta1 = norm1 / jnp.maximum(norm0, TINY)
    beta2 = norm2 / jnp.maximum(norm1, TINY)
    inverse = 1.0 / jnp.maximum(alpha0, TINY)
    shift = shift_ref[...] * inverse
    pivot0 = 1.0 + shift
    pivot1 = (alpha1 + shift) - beta1 / pivot0
    pivot2 = (alpha2 + shift) - beta2 / pivot1
    right1 = -1.0 / pivot0
    right2 = -right1 / pivot1
    coef2 = right2 / pivot2
    coef1 = (right1 - beta2 * coef2) / pivot1
    coef0 = (1.0 - beta1 * coef1) / pivot0
    coefs = [coef0 * inverse, coef1 * inverse, coef2 * inverse]
    square = sum([coef * coef * norm for coef, norm in zip(coefs, (norm0, norm1, norm2))])
    factor = lax.rsqrt(square / params + epsilon)
    coefs = [coef * factor for coef in coefs]

    def step(at, carry):
        terms = [coef * load_tile(ref, 0, at) for coef, ref in zip(coefs, vectors)]
        out_ref[:, pl.ds(at, LANES)] = terms[0] + terms[1] + terms[2]
        return carry

    each_tile(cols, step, 0)


def call(kernel, outs, *args, spaces=None, scratch=()):
    shapes = [
        jax.ShapeDtypeStruct(out, jnp.float32) if isinstance(out, tuple) else out for out in outs
    ]
    space = pl.BlockSpec(memory_space=pltpu.VMEM)
    return pl.pallas_call(
        kernel,
        out_shape=shapes,
        in_specs=spaces or [space] * len(args),
        out_specs=[space] * len(shapes),
        scratch_shapes=scratch,
        compiler_params=pltpu.CompilerParams(vmem_limit_bytes=24 * 1024 * 1024),
    )(*args)


def from_walk(array, groups):
    others = []
    for hop in range(1, groups):
        pairs = [(index, (index - hop) % groups) for index in range(groups)]
        others.append(lax.ppermute(array, "walk", pairs))
    return [array] + others


def across(array, size, masks):
    out = [array]
    for mask in masks:
        pairs = [(index, index ^ mask) for index in range(size)]
        out.append(lax.ppermute(array, "param", pairs))
    return out


def masks_of(stride, radix, order):
    flip = 1 if stride > 1 else 0
    masks = [step * stride ^ flip for step in range(radix - 1, 0, -1)]
    return [masks[at] for at in order] if radix == 4 else masks


def param_parts(array, size, order=(0, 1, 2)):
    stride = 1
    while size > stride:
        radix = 4 if size // stride % 4 == 0 else 2
        parts = across(array, size, masks_of(stride, radix, order if stride == 1 else (0, 1, 2)))
        stride *= radix
        if stride == size:
            return parts
        array = tree_sum(parts)
    return [array]


def last_parts(array, groups, size):
    total = tree_sum(param_parts(array, size))
    others = []
    for hop in range(1, groups):
        pairs = [
            (group * size + index, (group - hop) % groups * size + (index ^ 1))
            for group in range(groups)
            for index in range(size)
        ]
        others.append(lax.ppermute(total, ("walk", "param"), pairs))
    return [total] + others


def body(jacobian, energies, shifts):
    rows, cols = jacobian.shape
    groups, shards = lax.axis_size("walk"), lax.axis_size("param")
    walkers, params = rows * groups, cols * shards
    vector, part, scalar = (1, cols), (2, LANES), (1, LANES)
    msg_shape = (1, cols + 2 * LANES)
    shift_rows = jnp.broadcast_to(shifts[:, None], (shifts.shape[0], LANES))

    jacobian, msg = call(
        first_kernel,
        [pltpu.VMEM((rows, cols), jnp.float32), (2, cols + LANES)],
        pltpu.with_memory_space_constraint(jacobian, pltpu.HBM),
        pltpu.with_memory_space_constraint(energies.reshape(1, rows), pltpu.HBM),
        spaces=[pl.BlockSpec(memory_space=pltpu.HBM)] * 2,
        scratch=[
            pltpu.VMEM((1, rows), jnp.float32),
            pltpu.SemaphoreType.DMA((CHUNKS,)),
            pltpu.SemaphoreType.DMA(()),
        ],
    )
    firsts = from_walk(msg, groups)
    vector0, sent = call(
        functools.partial(project_zero, walkers), [vector, part], jacobian, *firsts
    )
    parts = param_parts(sent, shards)
    msg, norm0 = call(back_kernel, [msg_shape, scalar], jacobian, *parts)
    msgs = from_walk(msg, groups)
    vector1, sent, state = call(
        functools.partial(project_one, groups, walkers),
        [vector, part, (2, LANES)],
        jacobian,
        *firsts,
        *msgs,
        norm0,
        vector0,
    )
    parts = param_parts(sent, shards, (1, 2, 0))
    msg, norm1 = call(back_kernel, [msg_shape, scalar], jacobian, *parts)
    msgs = from_walk(msg, groups)
    vector2, sent, alpha1 = call(
        functools.partial(project_two, groups),
        [vector, part, scalar],
        jacobian,
        *firsts,
        *msgs,
        state,
        norm0,
        norm1,
        vector0,
        vector1,
    )
    (update,) = call(
        functools.partial(final_kernel, params),
        [(shifts.shape[0], cols)],
        *last_parts(sent, groups, shards),
        shift_rows,
        state,
        alpha1,
        norm0,
        norm1,
        vector0,
        vector1,
        vector2,
    )
    return update


def solution(mesh):
    return jax.shard_map(
        body,
        mesh=mesh,
        in_specs=(P("walk", "param"), P("walk"), P()),
        out_specs=P(None, "param"),
        check_vma=False,
    )
```

```python
import functools

import jax
import jax.numpy as jnp
from jax import lax
from jax.experimental import pallas as pl
from jax.experimental.pallas import tpu as pltpu
from jax.sharding import PartitionSpec as P

LANES = 128
TINY = 1e-37
CHUNKS = 8
GROUP = 8
epsilon = 1e-06


def tree_sum(terms):
    terms = list(terms)
    while len(terms) > 1:
        odd = terms[len(terms) // 2 * 2 :]
        terms = [a + b for a, b in zip(terms[0::2], terms[1::2])] + odd
    return terms[0]


def over_lanes(values):
    total = jnp.sum(values, axis=1, keepdims=True)
    return jnp.broadcast_to(total, (values.shape[0], LANES))


def over_rows(values):
    return jnp.sum(values, axis=0, keepdims=True)


def down_rows(row):
    return jnp.transpose(jnp.broadcast_to(row, (row.shape[1], row.shape[1])))


def centred_weight(row):
    weight = down_rows(row)
    mean = over_rows(weight) / row.shape[1]
    return weight - mean, mean


def each_tile(cols, step, carry):
    count = cols // LANES

    def run(number, carry):
        for part in range(GROUP):
            at = pl.multiple_of((number * GROUP + part) * LANES, LANES)
            carry = step(at, carry)
        return carry

    carry = lax.fori_loop(0, count // GROUP, run, carry)
    for number in range(count // GROUP * GROUP, count):
        carry = step(number * LANES, carry)
    return carry


def cut(count, pieces):
    edges = [count * number // pieces for number in range(pieces + 1)]
    return [(low * LANES, high * LANES) for low, high in zip(edges, edges[1:]) if high > low]


def load_tile(ref, row, at):
    return ref[row : row + 1, pl.ds(at, LANES)]


def first_kernel(jac_hbm, energy_hbm, jac_ref, msg_ref, energy_ref, sems, energy_sem):
    cols = jac_ref.shape[1]
    pieces = cut(cols // LANES, CHUNKS)
    energy_copy = pltpu.make_async_copy(energy_hbm, energy_ref, energy_sem)
    energy_copy.start()
    copies = [
        pltpu.make_async_copy(
            jac_hbm.at[:, low:high], jac_ref.at[:, low:high], sems.at[number]
        )
        for number, (low, high) in enumerate(pieces)
    ]
    for number, copy in enumerate(copies):
        copy.start(priority=number % 2)
    energy_copy.wait()
    weight, mean = centred_weight(energy_ref[...])
    msg_ref[0:1, cols : cols + LANES] = mean
    msg_ref[1:2, cols : cols + LANES] = mean
    for copy, (low, high) in zip(copies, pieces):
        copy.wait()
        for at in range(low, high, LANES):
            block = jac_ref[:, at : at + LANES]
            msg_ref[0:1, at : at + LANES] = over_rows(block * weight)
            msg_ref[1:2, at : at + LANES] = over_rows(block)


def back_kernel(jac_ref, *refs):
    part_refs, (msg_ref, norm_ref) = refs[:-2], refs[-2:]
    cols = jac_ref.shape[1]
    total = tree_sum([ref[...] for ref in part_refs])
    norm_ref[...] = total[1:2]
    weight, mean = centred_weight(total[0:1])

    def step(at, carry):
        msg_ref[:, pl.ds(at, LANES)] = over_rows(jac_ref[:, pl.ds(at, LANES)] * weight)
        return carry

    each_tile(cols, step, 0)
    msg_ref[:, cols : cols + LANES] = mean
    msg_ref[:, cols + LANES : cols + 2 * LANES] = over_rows(weight * weight)


def mean_offsets(means):
    centre = sum(means) / len(means)
    return [mean - centre for mean in means]


def square_total(offsets, squares, rows):
    return sum(squares) + rows * sum([offset * offset for offset in offsets])


def offset_term(offsets, sums):
    if len(sums) == 2:
        return offsets[0] * (sums[0] - sums[1])
    return sum([offset * term for offset, term in zip(offsets, sums)])


def project(jac_ref, firsts, msgs, offsets, scale, olds, vector_ref, part_ref):
    rows, cols = jac_ref.shape

    def step(at, carry):
        acc, square = carry
        value = sum([load_tile(ref, 0, at) for ref in msgs])
        value = value + offset_term(offsets, [load_tile(ref, 1, at) for ref in firsts])
        value = value * scale
        for factor, ref in olds:
            value = value - factor * load_tile(ref, 0, at)
        vector_ref[:, pl.ds(at, LANES)] = value
        return acc + jac_ref[:, pl.ds(at, LANES)] * value, square + value * value

    zeros = jnp.zeros((rows, LANES), jnp.float32), jnp.zeros((1, LANES), jnp.float32)
    acc, square = each_tile(cols, step, zeros)
    part_ref[0:1] = over_rows(jnp.transpose(acc))
    part_ref[1:2] = over_lanes(square)


def project_zero(walkers, jac_ref, *refs):
    firsts, (vector_ref, part_ref) = refs[:-2], refs[-2:]
    cols = jac_ref.shape[1]
    offsets = mean_offsets([ref[0:1, cols : cols + LANES] for ref in firsts])
    scale = jnp.full((1, LANES), 1.0 / walkers, jnp.float32)
    project(jac_ref, firsts, firsts, offsets, scale, [], vector_ref, part_ref)


def message_scalars(msgs, rows, cols):
    offsets = mean_offsets([ref[:, cols : cols + LANES] for ref in msgs])
    squares = [ref[:, cols + LANES : cols + 2 * LANES] for ref in msgs]
    return offsets, square_total(offsets, squares, rows)


def project_one(groups, walkers, jac_ref, *refs):
    firsts, msgs, refs = refs[:groups], refs[groups : 2 * groups], refs[2 * groups :]
    norm_ref, old_ref, vector_ref, part_ref, state_ref = refs
    offsets, square = message_scalars(msgs, *jac_ref.shape)
    alpha = square / (walkers * jnp.maximum(norm_ref[...], TINY))
    scale = 1.0 / (walkers * jnp.maximum(alpha, TINY))
    state_ref[0:1] = alpha
    state_ref[1:2] = scale
    one = jnp.ones((1, LANES), jnp.float32)
    project(jac_ref, firsts, msgs, offsets, scale, [(one, old_ref)], vector_ref, part_ref)


def project_two(groups, jac_ref, *refs):
    firsts, msgs, refs = refs[:groups], refs[groups : 2 * groups], refs[2 * groups :]
    state_ref, norm_old, norm_now, older_ref, old_ref, vector_ref, part_ref, alpha_ref = refs
    offsets, square = message_scalars(msgs, *jac_ref.shape)
    scale = state_ref[1:2]
    alpha = square * scale / jnp.maximum(norm_now[...], TINY)
    alpha_ref[...] = alpha
    beta = norm_now[...] / jnp.maximum(norm_old[...], TINY)
    olds = [(alpha, old_ref), (beta, older_ref)]
    project(jac_ref, firsts, msgs, offsets, scale, olds, vector_ref, part_ref)


def final_kernel(params, *refs):
    refs, vectors, out_ref = refs[:-4], refs[-4:-1], refs[-1]
    sum_refs, (shift_ref, state_ref, alpha_ref, norm0_ref, norm1_ref) = refs[:-5], refs[-5:]
    cols = out_ref.shape[1]
    lines = [ref[0:1] for ref in sum_refs]
    rows = lines[0].shape[1]
    means = [over_lanes(line) / rows for line in lines]
    devs = [line - mean for line, mean in zip(lines, means)]
    squares = [over_lanes(dev * dev) for dev in devs]
    square = square_total(mean_offsets(means), squares, rows)
    norm0, norm1, norm2 = norm0_ref[...], norm1_ref[...], sum_refs[0][1:2]
    alpha0, scale, alpha1 = state_ref[0:1], state_ref[1:2], alpha_ref[...]
    alpha2 = square * scale / jnp.maximum(norm2, TINY)
    beta1 = norm1 / jnp.maximum(norm0, TINY)
    beta2 = norm2 / jnp.maximum(norm1, TINY)
    inverse = 1.0 / jnp.maximum(alpha0, TINY)
    shift = shift_ref[...] * inverse
    pivot0 = 1.0 + shift
    pivot1 = (alpha1 + shift) - beta1 / pivot0
    pivot2 = (alpha2 + shift) - beta2 / pivot1
    right1 = -1.0 / pivot0
    right2 = -right1 / pivot1
    coef2 = right2 / pivot2
    coef1 = (right1 - beta2 * coef2) / pivot1
    coef0 = (1.0 - beta1 * coef1) / pivot0
    coefs = [coef0 * inverse, coef1 * inverse, coef2 * inverse]
    square = sum([coef * coef * norm for coef, norm in zip(coefs, (norm0, norm1, norm2))])
    factor = lax.rsqrt(square / params + epsilon)
    coefs = [coef * factor for coef in coefs]

    def step(at, carry):
        terms = [coef * load_tile(ref, 0, at) for coef, ref in zip(coefs, vectors)]
        out_ref[:, pl.ds(at, LANES)] = terms[0] + terms[1] + terms[2]
        return carry

    each_tile(cols, step, 0)


def call(kernel, outs, *args, spaces=None, scratch=()):
    shapes = [
        jax.ShapeDtypeStruct(out, jnp.float32) if isinstance(out, tuple) else out for out in outs
    ]
    space = pl.BlockSpec(memory_space=pltpu.VMEM)
    return pl.pallas_call(
        kernel,
        out_shape=shapes,
        in_specs=spaces or [space] * len(args),
        out_specs=[space] * len(shapes),
        scratch_shapes=scratch,
        compiler_params=pltpu.CompilerParams(vmem_limit_bytes=24 * 1024 * 1024),
    )(*args)


def from_walk(array, groups):
    others = []
    for hop in range(1, groups):
        pairs = [(index, (index - hop) % groups) for index in range(groups)]
        others.append(lax.ppermute(array, "walk", pairs))
    return [array] + others


def across(array, size, masks):
    out = [array]
    for mask in masks:
        pairs = [(index, index ^ mask) for index in range(size)]
        out.append(lax.ppermute(array, "param", pairs))
    return out


def masks_of(stride, radix, order):
    flip = 1 if stride > 1 else 0
    masks = [step * stride ^ flip for step in range(radix - 1, 0, -1)]
    return [masks[at] for at in order] if radix == 4 else masks


def param_parts(array, size, order=(0, 1, 2)):
    stride = 1
    while size > stride:
        radix = 4 if size // stride % 4 == 0 else 2
        parts = across(array, size, masks_of(stride, radix, order if stride == 1 else (0, 1, 2)))
        stride *= radix
        if stride == size:
            return parts
        array = tree_sum(parts)
    return [array]


def send(array, groups, size, target):
    pairs = []
    for group in range(groups):
        for index in range(size):
            to_group, to_index = target(group, index)
            pairs.append((group * size + index, to_group * size + to_index))
    return lax.ppermute(array, ("walk", "param"), pairs)


def swap_cores(array, groups, size):
    return send(array, groups, size, lambda group, index: (group, index ^ 1))


def is_odd():
    return lax.axis_index("param") & 1 == 1


def shared_parts(array, groups, size, order):
    if size != 16:
        return param_parts(array, size)
    array = array + swap_cores(array, groups, size)

    def fetch(step):
        def target(group, index):
            far = 4 if index & 1 or step == 0 else 0
            return group, index ^ (2 * (step ^ far))

        return send(array, groups, size, target)

    three, two, zero, one = [fetch(step) for step in (3, 2, 0, 1)]
    zero = jnp.where(is_odd(), zero, array)
    terms = [zero, one, two, three]
    half = tree_sum([terms[step] for step in order])
    return [half, swap_cores(half, groups, size)]


def last_sums(array, groups, size):
    if groups != 2 or size != 16:
        total = tree_sum(param_parts(array, size))
        hops = [
            send(total, groups, size, lambda group, index: ((group - hop) % groups, index))
            for hop in range(1, groups)
        ]
        return [total] + hops
    array = tree_sum(across(array, size, masks_of(1, 4, (0, 1, 2))))

    def fetch(step):
        def target(group, index):
            other = group ^ 1 if index & 1 or step == 0 else group
            return other, index ^ (4 * step)

        return send(array, groups, size, target)

    three, two, zero, one = [fetch(step) for step in (3, 2, 0, 1)]
    odd = is_odd()
    zero = jnp.where(odd, zero, array)
    mine = tree_sum([three, two, zero, one])
    theirs = swap_cores(mine, groups, size)
    return [jnp.where(odd, theirs, mine), jnp.where(odd, mine, theirs)]


def body(jacobian, energies, shifts):
    rows, cols = jacobian.shape
    groups, shards = lax.axis_size("walk"), lax.axis_size("param")
    walkers, params = rows * groups, cols * shards
    vector, part, scalar = (1, cols), (2, LANES), (1, LANES)
    msg_shape = (1, cols + 2 * LANES)
    shift_rows = jnp.broadcast_to(shifts[:, None], (shifts.shape[0], LANES))

    jacobian, msg = call(
        first_kernel,
        [pltpu.VMEM((rows, cols), jnp.float32), (2, cols + LANES)],
        pltpu.with_memory_space_constraint(jacobian, pltpu.HBM),
        pltpu.with_memory_space_constraint(energies.reshape(1, rows), pltpu.HBM),
        spaces=[pl.BlockSpec(memory_space=pltpu.HBM)] * 2,
        scratch=[
            pltpu.VMEM((1, rows), jnp.float32),
            pltpu.SemaphoreType.DMA((CHUNKS,)),
            pltpu.SemaphoreType.DMA(()),
        ],
    )
    firsts = from_walk(msg, groups)
    vector0, sent = call(
        functools.partial(project_zero, walkers), [vector, part], jacobian, *firsts
    )
    parts = shared_parts(sent, groups, shards, (3, 2, 0, 1))
    msg, norm0 = call(back_kernel, [msg_shape, scalar], jacobian, *parts)
    msgs = from_walk(msg, groups)
    vector1, sent, state = call(
        functools.partial(project_one, groups, walkers),
        [vector, part, (2, LANES)],
        jacobian,
        *firsts,
        *msgs,
        norm0,
        vector0,
    )
    parts = shared_parts(sent, groups, shards, (1, 3, 2, 0))
    msg, norm1 = call(back_kernel, [msg_shape, scalar], jacobian, *parts)
    msgs = from_walk(msg, groups)
    vector2, sent, alpha1 = call(
        functools.partial(project_two, groups),
        [vector, part, scalar],
        jacobian,
        *firsts,
        *msgs,
        state,
        norm0,
        norm1,
        vector0,
        vector1,
    )
    (update,) = call(
        functools.partial(final_kernel, params),
        [(shifts.shape[0], cols)],
        *last_sums(sent, groups, shards),
        shift_rows,
        state,
        alpha1,
        norm0,
        norm1,
        vector0,
        vector1,
        vector2,
    )
    return update


def solution(mesh):
    return jax.shard_map(
        body,
        mesh=mesh,
        in_specs=(P("walk", "param"), P("walk"), P()),
        out_specs=P(None, "param"),
        check_vma=False,
    )
```

```python
import functools

import jax
import jax.numpy as jnp
from jax import lax
from jax.experimental import pallas as pl
from jax.experimental.pallas import tpu as pltpu
from jax.sharding import PartitionSpec as P

LANES = 128
TINY = 1e-37
CHUNKS = 8
PIECES = 3
GROUP = 8
epsilon = 1e-06


def tree_sum(terms):
    terms = list(terms)
    while len(terms) > 1:
        odd = terms[len(terms) // 2 * 2 :]
        terms = [a + b for a, b in zip(terms[0::2], terms[1::2])] + odd
    return terms[0]


def over_lanes(values):
    total = jnp.sum(values, axis=1, keepdims=True)
    return jnp.broadcast_to(total, (values.shape[0], LANES))


def over_rows(values):
    return jnp.sum(values, axis=0, keepdims=True)


def down_rows(row):
    return jnp.transpose(jnp.broadcast_to(row, (row.shape[1], row.shape[1])))


def centred_weight(row):
    weight = down_rows(row)
    mean = over_rows(weight) / row.shape[1]
    return weight - mean, mean


def each_tile(cols, step, carry):
    count = cols // LANES

    def run(number, carry):
        for part in range(GROUP):
            at = pl.multiple_of((number * GROUP + part) * LANES, LANES)
            carry = step(at, carry)
        return carry

    carry = lax.fori_loop(0, count // GROUP, run, carry)
    for number in range(count // GROUP * GROUP, count):
        carry = step(number * LANES, carry)
    return carry


def cut(count, pieces):
    edges = [count * number // pieces for number in range(pieces + 1)]
    return [(low * LANES, high * LANES) for low, high in zip(edges, edges[1:]) if high > low]


def load_tile(ref, row, at):
    return ref[row : row + 1, pl.ds(at, LANES)]


def first_kernel(jac_hbm, energy_hbm, jac_ref, msg_ref, energy_ref, sems, energy_sem):
    cols = jac_ref.shape[1]
    pieces = cut(cols // LANES, CHUNKS)
    energy_copy = pltpu.make_async_copy(energy_hbm, energy_ref, energy_sem)
    energy_copy.start()
    copies = [
        pltpu.make_async_copy(
            jac_hbm.at[:, low:high], jac_ref.at[:, low:high], sems.at[number]
        )
        for number, (low, high) in enumerate(pieces)
    ]
    for number, copy in enumerate(copies):
        copy.start(priority=number % 2)
    energy_copy.wait()
    weight, mean = centred_weight(energy_ref[...])
    msg_ref[0:1, cols : cols + LANES] = mean
    msg_ref[1:2, cols : cols + LANES] = mean
    for copy, (low, high) in zip(copies, pieces):
        copy.wait()
        for at in range(low, high, LANES):
            block = jac_ref[:, at : at + LANES]
            msg_ref[0:1, at : at + LANES] = over_rows(block * weight)
            msg_ref[1:2, at : at + LANES] = over_rows(block)


def back_kernel(jac_ref, *refs):
    part_refs, (msg_ref, norm_ref) = refs[:-2], refs[-2:]
    cols = jac_ref.shape[1]
    total = tree_sum([ref[...] for ref in part_refs])
    norm_ref[...] = total[1:2]
    weight, mean = centred_weight(total[0:1])

    def step(at, carry):
        msg_ref[:, pl.ds(at, LANES)] = over_rows(jac_ref[:, pl.ds(at, LANES)] * weight)
        return carry

    each_tile(cols, step, 0)
    msg_ref[:, cols : cols + LANES] = mean
    msg_ref[:, cols + LANES : cols + 2 * LANES] = over_rows(weight * weight)


def mean_offsets(means):
    centre = sum(means) / len(means)
    return [mean - centre for mean in means]


def square_total(offsets, squares, rows):
    return sum(squares) + rows * sum([offset * offset for offset in offsets])


def offset_term(offsets, sums):
    if len(sums) == 2:
        return offsets[0] * (sums[0] - sums[1])
    return sum([offset * term for offset, term in zip(offsets, sums)])


def project(jac_ref, firsts, msgs, offsets, scale, olds, vector_ref, part_ref):
    rows, cols = jac_ref.shape

    def step(at, carry):
        acc, square = carry
        value = sum([load_tile(ref, 0, at) for ref in msgs])
        value = value + offset_term(offsets, [load_tile(ref, 1, at) for ref in firsts])
        value = value * scale
        for factor, ref in olds:
            value = value - factor * load_tile(ref, 0, at)
        vector_ref[:, pl.ds(at, LANES)] = value
        return acc + jac_ref[:, pl.ds(at, LANES)] * value, square + value * value

    zeros = jnp.zeros((rows, LANES), jnp.float32), jnp.zeros((1, LANES), jnp.float32)
    acc, square = each_tile(cols, step, zeros)
    part_ref[0:1] = over_rows(jnp.transpose(acc))
    part_ref[1:2] = over_lanes(square)


def project_zero(walkers, jac_ref, *refs):
    firsts, (vector_ref, part_ref) = refs[:-2], refs[-2:]
    cols = jac_ref.shape[1]
    offsets = mean_offsets([ref[0:1, cols : cols + LANES] for ref in firsts])
    scale = jnp.full((1, LANES), 1.0 / walkers, jnp.float32)
    project(jac_ref, firsts, firsts, offsets, scale, [], vector_ref, part_ref)


def message_scalars(msgs, rows, cols):
    offsets = mean_offsets([ref[:, cols : cols + LANES] for ref in msgs])
    squares = [ref[:, cols + LANES : cols + 2 * LANES] for ref in msgs]
    return offsets, square_total(offsets, squares, rows)


def project_one(groups, walkers, jac_ref, *refs):
    firsts, msgs, refs = refs[:groups], refs[groups : 2 * groups], refs[2 * groups :]
    norm_ref, old_ref, vector_ref, part_ref, state_ref = refs
    offsets, square = message_scalars(msgs, *jac_ref.shape)
    alpha = square / (walkers * jnp.maximum(norm_ref[...], TINY))
    scale = 1.0 / (walkers * jnp.maximum(alpha, TINY))
    state_ref[0:1] = alpha
    state_ref[1:2] = scale
    one = jnp.ones((1, LANES), jnp.float32)
    project(jac_ref, firsts, msgs, offsets, scale, [(one, old_ref)], vector_ref, part_ref)


def project_two(groups, jac_ref, *refs):
    firsts, msgs, refs = refs[:groups], refs[groups : 2 * groups], refs[2 * groups :]
    state_ref, norm_old, norm_now, older_ref, old_ref, vector_ref, part_ref, alpha_ref = refs
    offsets, square = message_scalars(msgs, *jac_ref.shape)
    scale = state_ref[1:2]
    alpha = square * scale / jnp.maximum(norm_now[...], TINY)
    alpha_ref[...] = alpha
    beta = norm_now[...] / jnp.maximum(norm_old[...], TINY)
    olds = [(alpha, old_ref), (beta, older_ref)]
    project(jac_ref, firsts, msgs, offsets, scale, olds, vector_ref, part_ref)


def final_kernel(params, *refs):
    refs, vectors, (out_ref, held_ref, sems) = refs[:-6], refs[-6:-3], refs[-3:]
    part_refs, (shift_ref, state_ref, alpha_ref, norm0_ref, norm1_ref) = refs[:-5], refs[-5:]
    cols = out_ref.shape[1]
    total = tree_sum([ref[...] for ref in part_refs])
    lines = [slot[0:1] for slot in total]
    rows = lines[0].shape[1]
    means = [over_lanes(line) / rows for line in lines]
    devs = [line - mean for line, mean in zip(lines, means)]
    squares = [over_lanes(dev * dev) for dev in devs]
    square = square_total(mean_offsets(means), squares, rows)
    norm0, norm1, norm2 = norm0_ref[...], norm1_ref[...], total[0, 1:2]
    alpha0, scale, alpha1 = state_ref[0:1], state_ref[1:2], alpha_ref[...]
    alpha2 = square * (scale / jnp.maximum(norm2, TINY))
    beta1 = norm1 / jnp.maximum(norm0, TINY)
    beta2 = norm2 / jnp.maximum(norm1, TINY)
    inverse = 1.0 / jnp.maximum(alpha0, TINY)
    shift = shift_ref[...] * inverse
    over0 = 1.0 / (1.0 + shift)
    over1 = 1.0 / ((alpha1 + shift) - beta1 * over0)
    over2 = 1.0 / ((alpha2 + shift) - beta2 * over1)
    coef2 = over0 * over1 * over2
    coef1 = -(over0 + beta2 * coef2) * over1
    coef0 = (1.0 - beta1 * coef1) * over0
    coefs = [coef0 * inverse, coef1 * inverse, coef2 * inverse]
    square = sum([coef * coef * norm for coef, norm in zip(coefs, (norm0, norm1, norm2))])
    factor = lax.rsqrt(square / params + epsilon)
    coefs = [coef * factor for coef in coefs]

    pieces = cut(cols // LANES, PIECES)
    copies = []
    for number, (low, high) in enumerate(pieces):
        for at in range(low, high, LANES):
            terms = [coef * load_tile(ref, 0, at) for coef, ref in zip(coefs, vectors)]
            held_ref[:, at : at + LANES] = terms[0] + terms[1] + terms[2]
        copies.append(
            pltpu.make_async_copy(
                held_ref.at[:, low:high], out_ref.at[:, low:high], sems.at[number]
            )
        )
        copies[-1].start()
    for copy in copies:
        copy.wait()


def call(kernel, outs, *args, spaces=None, out_space=pltpu.VMEM, scratch=()):
    shapes = [
        jax.ShapeDtypeStruct(out, jnp.float32) if isinstance(out, tuple) else out for out in outs
    ]
    space = pl.BlockSpec(memory_space=pltpu.VMEM)
    return pl.pallas_call(
        kernel,
        out_shape=shapes,
        in_specs=spaces or [space] * len(args),
        out_specs=[pl.BlockSpec(memory_space=out_space)] * len(shapes),
        scratch_shapes=scratch,
        compiler_params=pltpu.CompilerParams(vmem_limit_bytes=24 * 1024 * 1024),
    )(*args)


def from_walk(array, groups):
    others = []
    for hop in range(1, groups):
        pairs = [(index, (index - hop) % groups) for index in range(groups)]
        others.append(lax.ppermute(array, "walk", pairs))
    return [array] + others


def across(array, size, masks):
    out = [array]
    for mask in masks:
        pairs = [(index, index ^ mask) for index in range(size)]
        out.append(lax.ppermute(array, "param", pairs))
    return out


def masks_of(stride, radix, order):
    flip = 1 if stride > 1 else 0
    masks = [step * stride ^ flip for step in range(radix - 1, 0, -1)]
    return [masks[at] for at in order] if radix == 4 else masks


def param_parts(array, size, order=(1, 0, 2), stride=1):
    while size > stride:
        radix = 4 if size // stride % 4 == 0 else 2
        parts = across(array, size, masks_of(stride, radix, order if stride == 1 else (0, 1, 2)))
        stride *= radix
        if stride == size:
            return parts
        array = tree_sum(parts)
    return [array]


def send(array, groups, size, target):
    pairs = []
    for group in range(groups):
        for index in range(size):
            to_group, to_index = target(group, index)
            pairs.append((group * size + index, to_group * size + to_index))
    return lax.ppermute(array, ("walk", "param"), pairs)


def last_parts(array, groups, size):
    if groups != 2 or size < 8:
        total = tree_sum(param_parts(array, size))
        hops = [
            send(total, groups, size, lambda group, index: ((group - hop) % groups, index))
            for hop in range(1, groups)
        ]
        return [jnp.stack([total] + hops)]
    array = tree_sum(across(array, size, [1]))
    both = send(array, groups, size, lambda group, index: (group ^ 1, index ^ 3))
    beside = across(array, size, [3])[1]
    facing = send(array, groups, size, lambda group, index: (group ^ 1, index ^ 1))
    array = jnp.stack([array + beside, both + facing])
    return param_parts(array, size, stride=4)


def body(jacobian, energies, shifts):
    rows, cols = jacobian.shape
    groups, shards = lax.axis_size("walk"), lax.axis_size("param")
    walkers, params = rows * groups, cols * shards
    vector, part, scalar = (1, cols), (2, LANES), (1, LANES)
    msg_shape = (1, cols + 2 * LANES)
    shift_rows = jnp.broadcast_to(shifts[:, None], (shifts.shape[0], LANES))

    jacobian, msg = call(
        first_kernel,
        [pltpu.VMEM((rows, cols), jnp.float32), (2, cols + LANES)],
        pltpu.with_memory_space_constraint(jacobian, pltpu.HBM),
        pltpu.with_memory_space_constraint(energies.reshape(1, rows), pltpu.HBM),
        spaces=[pl.BlockSpec(memory_space=pltpu.HBM)] * 2,
        scratch=[
            pltpu.VMEM((1, rows), jnp.float32),
            pltpu.SemaphoreType.DMA((CHUNKS,)),
            pltpu.SemaphoreType.DMA(()),
        ],
    )
    firsts = from_walk(msg, groups)
    vector0, sent = call(
        functools.partial(project_zero, walkers), [vector, part], jacobian, *firsts
    )
    parts = param_parts(sent, shards)
    msg, norm0 = call(back_kernel, [msg_shape, scalar], jacobian, *parts)
    msgs = from_walk(msg, groups)
    vector1, sent, state = call(
        functools.partial(project_one, groups, walkers),
        [vector, part, (2, LANES)],
        jacobian,
        *firsts,
        *msgs,
        norm0,
        vector0,
    )
    parts = param_parts(sent, shards, (0, 2, 1))
    msg, norm1 = call(back_kernel, [msg_shape, scalar], jacobian, *parts)
    msgs = from_walk(msg, groups)
    vector2, sent, alpha1 = call(
        functools.partial(project_two, groups),
        [vector, part, scalar],
        jacobian,
        *firsts,
        *msgs,
        state,
        norm0,
        norm1,
        vector0,
        vector1,
    )
    (update,) = call(
        functools.partial(final_kernel, params),
        [(shifts.shape[0], cols)],
        *last_parts(sent, groups, shards),
        shift_rows,
        state,
        alpha1,
        norm0,
        norm1,
        vector0,
        vector1,
        vector2,
        out_space=pltpu.HBM,
        scratch=[
            pltpu.VMEM((shifts.shape[0], cols), jnp.float32),
            pltpu.SemaphoreType.DMA((PIECES,)),
        ],
    )
    return update


def solution(mesh):
    return jax.shard_map(
        body,
        mesh=mesh,
        in_specs=(P("walk", "param"), P("walk"), P()),
        out_specs=P(None, "param"),
        check_vma=False,
    )
```

```python
import functools

import jax
import jax.numpy as jnp
from jax import lax
from jax.experimental import pallas as pl
from jax.experimental.pallas import tpu as pltpu
from jax.sharding import PartitionSpec as P

LANES = 128
TINY = 1e-37
CHUNKS = 8
PIECES = 3
GROUP = 8
epsilon = 1e-06


def tree_sum(terms):
    terms = list(terms)
    while len(terms) > 1:
        odd = terms[len(terms) // 2 * 2 :]
        terms = [a + b for a, b in zip(terms[0::2], terms[1::2])] + odd
    return terms[0]


def over_lanes(values):
    total = jnp.sum(values, axis=1, keepdims=True)
    return jnp.broadcast_to(total, (values.shape[0], LANES))


def over_rows(values):
    return jnp.sum(values, axis=0, keepdims=True)


def down_rows(row):
    return jnp.transpose(jnp.broadcast_to(row, (row.shape[1], row.shape[1])))


def centred_weight(row):
    weight = down_rows(row)
    mean = over_rows(weight) / row.shape[1]
    return weight - mean, mean


def each_tile(cols, step, carry):
    count = cols // LANES

    def run(number, carry):
        for part in range(GROUP):
            at = pl.multiple_of((number * GROUP + part) * LANES, LANES)
            carry = step(at, carry)
        return carry

    carry = lax.fori_loop(0, count // GROUP, run, carry)
    for number in range(count // GROUP * GROUP, count):
        carry = step(number * LANES, carry)
    return carry


def cut(count, pieces):
    edges = [count * number // pieces for number in range(pieces + 1)]
    return [(low * LANES, high * LANES) for low, high in zip(edges, edges[1:]) if high > low]


def load_tile(ref, row, at):
    return ref[row : row + 1, pl.ds(at, LANES)]


def first_kernel(jac_hbm, energy_hbm, jac_ref, msg_ref, energy_ref, sems, energy_sem):
    cols = jac_ref.shape[1]
    pieces = cut(cols // LANES, CHUNKS)
    energy_copy = pltpu.make_async_copy(energy_hbm, energy_ref, energy_sem)
    energy_copy.start()
    copies = [
        pltpu.make_async_copy(
            jac_hbm.at[:, low:high], jac_ref.at[:, low:high], sems.at[number]
        )
        for number, (low, high) in enumerate(pieces)
    ]
    for number, copy in enumerate(copies):
        copy.start(priority=number % 2)
    energy_copy.wait()
    weight, mean = centred_weight(energy_ref[...])
    msg_ref[0:1, cols : cols + LANES] = mean
    msg_ref[1:2, cols : cols + LANES] = mean
    for copy, (low, high) in zip(copies, pieces):
        copy.wait()
        for at in range(low, high, LANES):
            block = jac_ref[:, at : at + LANES]
            msg_ref[0:1, at : at + LANES] = over_rows(block * weight)
            msg_ref[1:2, at : at + LANES] = over_rows(block)


def back_kernel(jac_ref, *refs):
    part_refs, (msg_ref, norm_ref) = refs[:-2], refs[-2:]
    cols = jac_ref.shape[1]
    total = tree_sum([ref[...] for ref in part_refs])
    norm_ref[...] = total[1:2]
    weight, mean = centred_weight(total[0:1])

    def step(at, carry):
        msg_ref[:, pl.ds(at, LANES)] = over_rows(jac_ref[:, pl.ds(at, LANES)] * weight)
        return carry

    each_tile(cols, step, 0)
    msg_ref[:, cols : cols + LANES] = mean
    msg_ref[:, cols + LANES : cols + 2 * LANES] = over_rows(weight * weight)


def mean_offsets(means):
    centre = sum(means) / len(means)
    return [mean - centre for mean in means]


def square_total(offsets, squares, rows):
    return sum(squares) + rows * sum([offset * offset for offset in offsets])


def offset_term(offsets, sums):
    if len(sums) == 2:
        return offsets[0] * (sums[0] - sums[1])
    return sum([offset * term for offset, term in zip(offsets, sums)])


def project(jac_ref, firsts, msgs, offsets, scale, olds, vector_ref, part_ref):
    rows, cols = jac_ref.shape

    def step(at, carry):
        acc, square = carry
        value = sum([load_tile(ref, 0, at) for ref in msgs])
        value = value + offset_term(offsets, [load_tile(ref, 1, at) for ref in firsts])
        value = value * scale
        for factor, ref in olds:
            value = value - factor * load_tile(ref, 0, at)
        vector_ref[:, pl.ds(at, LANES)] = value
        return acc + jac_ref[:, pl.ds(at, LANES)] * value, square + value * value

    zeros = jnp.zeros((rows, LANES), jnp.float32), jnp.zeros((1, LANES), jnp.float32)
    acc, square = each_tile(cols, step, zeros)
    part_ref[0:1] = over_rows(jnp.transpose(acc))
    part_ref[1:2] = over_lanes(square)


def project_zero(walkers, jac_ref, *refs):
    firsts, (vector_ref, part_ref) = refs[:-2], refs[-2:]
    cols = jac_ref.shape[1]
    offsets = mean_offsets([ref[0:1, cols : cols + LANES] for ref in firsts])
    scale = jnp.full((1, LANES), 1.0 / walkers, jnp.float32)
    project(jac_ref, firsts, firsts, offsets, scale, [], vector_ref, part_ref)


def message_scalars(msgs, rows, cols):
    offsets = mean_offsets([ref[:, cols : cols + LANES] for ref in msgs])
    squares = [ref[:, cols + LANES : cols + 2 * LANES] for ref in msgs]
    return offsets, square_total(offsets, squares, rows)


def project_one(groups, walkers, jac_ref, *refs):
    firsts, msgs, refs = refs[:groups], refs[groups : 2 * groups], refs[2 * groups :]
    norm_ref, old_ref, vector_ref, part_ref, state_ref = refs
    offsets, square = message_scalars(msgs, *jac_ref.shape)
    alpha = square / (walkers * jnp.maximum(norm_ref[...], TINY))
    scale = 1.0 / (walkers * jnp.maximum(alpha, TINY))
    state_ref[0:1] = alpha
    state_ref[1:2] = scale
    one = jnp.ones((1, LANES), jnp.float32)
    project(jac_ref, firsts, msgs, offsets, scale, [(one, old_ref)], vector_ref, part_ref)


def project_two(groups, jac_ref, *refs):
    firsts, msgs, refs = refs[:groups], refs[groups : 2 * groups], refs[2 * groups :]
    state_ref, norm_old, norm_now, older_ref, old_ref, vector_ref, part_ref, alpha_ref = refs
    offsets, square = message_scalars(msgs, *jac_ref.shape)
    scale = state_ref[1:2]
    alpha = square * scale / jnp.maximum(norm_now[...], TINY)
    alpha_ref[...] = alpha
    beta = norm_now[...] / jnp.maximum(norm_old[...], TINY)
    olds = [(alpha, old_ref), (beta, older_ref)]
    project(jac_ref, firsts, msgs, offsets, scale, olds, vector_ref, part_ref)


def final_kernel(params, *refs):
    refs, vectors, (out_ref, held_ref, sems) = refs[:-6], refs[-6:-3], refs[-3:]
    sum_refs, (shift_ref, state_ref, alpha_ref, norm0_ref, norm1_ref) = refs[:-5], refs[-5:]
    cols = out_ref.shape[1]
    lines = [ref[0:1] for ref in sum_refs]
    rows = lines[0].shape[1]
    means = [over_lanes(line) / rows for line in lines]
    devs = [line - mean for line, mean in zip(lines, means)]
    squares = [over_lanes(dev * dev) for dev in devs]
    square = square_total(mean_offsets(means), squares, rows)
    norm0, norm1, norm2 = norm0_ref[...], norm1_ref[...], sum_refs[0][1:2]
    alpha0, scale, alpha1 = state_ref[0:1], state_ref[1:2], alpha_ref[...]
    alpha2 = square * (scale / jnp.maximum(norm2, TINY))
    beta1 = norm1 / jnp.maximum(norm0, TINY)
    beta2 = norm2 / jnp.maximum(norm1, TINY)
    inverse = 1.0 / jnp.maximum(alpha0, TINY)
    shift = shift_ref[...] * inverse
    over0 = 1.0 / (1.0 + shift)
    over1 = 1.0 / ((alpha1 + shift) - beta1 * over0)
    over2 = 1.0 / ((alpha2 + shift) - beta2 * over1)
    coef2 = over0 * over1 * over2
    coef1 = -(over0 + beta2 * coef2) * over1
    coef0 = (1.0 - beta1 * coef1) * over0
    coefs = [coef0 * inverse, coef1 * inverse, coef2 * inverse]
    square = sum([coef * coef * norm for coef, norm in zip(coefs, (norm0, norm1, norm2))])
    factor = lax.rsqrt(square / params + epsilon)
    coefs = [coef * factor for coef in coefs]

    pieces = cut(cols // LANES, PIECES)
    copies = []
    for number, (low, high) in enumerate(pieces):
        for at in range(low, high, LANES):
            terms = [coef * load_tile(ref, 0, at) for coef, ref in zip(coefs, vectors)]
            held_ref[:, at : at + LANES] = terms[0] + terms[1] + terms[2]
        copies.append(
            pltpu.make_async_copy(
                held_ref.at[:, low:high], out_ref.at[:, low:high], sems.at[number]
            )
        )
        copies[-1].start()
    for copy in copies:
        copy.wait()


def call(kernel, outs, *args, spaces=None, out_space=pltpu.VMEM, scratch=()):
    shapes = [
        jax.ShapeDtypeStruct(out, jnp.float32) if isinstance(out, tuple) else out for out in outs
    ]
    space = pl.BlockSpec(memory_space=pltpu.VMEM)
    return pl.pallas_call(
        kernel,
        out_shape=shapes,
        in_specs=spaces or [space] * len(args),
        out_specs=[pl.BlockSpec(memory_space=out_space)] * len(shapes),
        scratch_shapes=scratch,
        compiler_params=pltpu.CompilerParams(vmem_limit_bytes=24 * 1024 * 1024),
    )(*args)


def from_walk(array, groups):
    others = []
    for hop in range(1, groups):
        pairs = [(index, (index - hop) % groups) for index in range(groups)]
        others.append(lax.ppermute(array, "walk", pairs))
    return [array] + others


def across(array, size, masks):
    out = [array]
    for mask in masks:
        pairs = [(index, index ^ mask) for index in range(size)]
        out.append(lax.ppermute(array, "param", pairs))
    return out


def param_parts(array, size, turn=0):
    stride = 1
    if size % 4 == 0:
        for mask in (3, 1):
            array = tree_sum(across(array, size, [mask]))
        stride = 4
    while size > stride:
        radix = 4 if size // stride % 4 == 0 else 2
        masks = [step * stride ^ (stride > 1) for step in range(radix - 1, 0, -1)]
        parts = across(array, size, masks[-turn:] + masks[:-turn])
        stride *= radix
        if stride == size:
            return parts
        array = tree_sum(parts)
    return [array]


def send(array, groups, size, target):
    pairs = []
    for group in range(groups):
        for index in range(size):
            to_group, to_index = target(group, index)
            pairs.append((group * size + index, to_group * size + to_index))
    return lax.ppermute(array, ("walk", "param"), pairs)


def last_sums(array, groups, size):
    total = tree_sum(param_parts(array, size))
    hops = [
        send(total, groups, size, lambda group, index: ((group - hop) % groups, index ^ 1))
        for hop in range(1, groups)
    ]
    return [total] + hops


def body(jacobian, energies, shifts):
    rows, cols = jacobian.shape
    groups, shards = lax.axis_size("walk"), lax.axis_size("param")
    walkers, params = rows * groups, cols * shards
    vector, part, scalar = (1, cols), (2, LANES), (1, LANES)
    msg_shape = (1, cols + 2 * LANES)
    shift_rows = jnp.broadcast_to(shifts[:, None], (shifts.shape[0], LANES))

    jacobian, msg = call(
        first_kernel,
        [pltpu.VMEM((rows, cols), jnp.float32), (2, cols + LANES)],
        pltpu.with_memory_space_constraint(jacobian, pltpu.HBM),
        pltpu.with_memory_space_constraint(energies.reshape(1, rows), pltpu.HBM),
        spaces=[pl.BlockSpec(memory_space=pltpu.HBM)] * 2,
        scratch=[
            pltpu.VMEM((1, rows), jnp.float32),
            pltpu.SemaphoreType.DMA((CHUNKS,)),
            pltpu.SemaphoreType.DMA(()),
        ],
    )
    firsts = from_walk(msg, groups)
    vector0, sent = call(
        functools.partial(project_zero, walkers), [vector, part], jacobian, *firsts
    )
    parts = param_parts(sent, shards)
    msg, norm0 = call(back_kernel, [msg_shape, scalar], jacobian, *parts)
    msgs = from_walk(msg, groups)
    vector1, sent, state = call(
        functools.partial(project_one, groups, walkers),
        [vector, part, (2, LANES)],
        jacobian,
        *firsts,
        *msgs,
        norm0,
        vector0,
    )
    parts = param_parts(sent, shards, 1)
    msg, norm1 = call(back_kernel, [msg_shape, scalar], jacobian, *parts)
    msgs = from_walk(msg, groups)
    vector2, sent, alpha1 = call(
        functools.partial(project_two, groups),
        [vector, part, scalar],
        jacobian,
        *firsts,
        *msgs,
        state,
        norm0,
        norm1,
        vector0,
        vector1,
    )
    (update,) = call(
        functools.partial(final_kernel, params),
        [(shifts.shape[0], cols)],
        *last_sums(sent, groups, shards),
        shift_rows,
        state,
        alpha1,
        norm0,
        norm1,
        vector0,
        vector1,
        vector2,
        out_space=pltpu.HBM,
        scratch=[
            pltpu.VMEM((shifts.shape[0], cols), jnp.float32),
            pltpu.SemaphoreType.DMA((PIECES,)),
        ],
    )
    return update


def solution(mesh):
    return jax.shard_map(
        body,
        mesh=mesh,
        in_specs=(P("walk", "param"), P("walk"), P()),
        out_specs=P(None, "param"),
        check_vma=False,
    )
```

```python
import functools

import jax
import jax.numpy as jnp
from jax import lax
from jax.experimental import pallas as pl
from jax.experimental.pallas import tpu as pltpu
from jax.sharding import PartitionSpec as P

LANES = 128
TINY = 1e-37
CHUNKS = 8
PIECES = 3
GROUP = 8
epsilon = 1e-06


def tree_sum(terms):
    terms = list(terms)
    while len(terms) > 1:
        odd = terms[len(terms) // 2 * 2 :]
        terms = [a + b for a, b in zip(terms[0::2], terms[1::2])] + odd
    return terms[0]


def over_lanes(values):
    total = jnp.sum(values, axis=1, keepdims=True)
    return jnp.broadcast_to(total, (values.shape[0], LANES))


def over_rows(values):
    return jnp.sum(values, axis=0, keepdims=True)


def down_rows(row):
    return jnp.transpose(jnp.broadcast_to(row, (row.shape[1], row.shape[1])))


def centred_weight(row):
    weight = down_rows(row)
    mean = over_rows(weight) / row.shape[1]
    return weight - mean, mean


def each_tile(cols, step, carry):
    count = cols // LANES

    def run(number, carry):
        for part in range(GROUP):
            at = pl.multiple_of((number * GROUP + part) * LANES, LANES)
            carry = step(at, carry)
        return carry

    carry = lax.fori_loop(0, count // GROUP, run, carry)
    for number in range(count // GROUP * GROUP, count):
        carry = step(number * LANES, carry)
    return carry


def cut(count, pieces):
    edges = [count * number // pieces for number in range(pieces + 1)]
    return [(low * LANES, high * LANES) for low, high in zip(edges, edges[1:]) if high > low]


def load_tile(ref, row, at):
    return ref[row : row + 1, pl.ds(at, LANES)]


def first_kernel(jac_hbm, energy_hbm, jac_ref, msg_ref, energy_ref, sems, energy_sem):
    cols = jac_ref.shape[1]
    pieces = cut(cols // LANES, CHUNKS)
    energy_copy = pltpu.make_async_copy(energy_hbm, energy_ref, energy_sem)
    energy_copy.start()
    copies = [
        pltpu.make_async_copy(
            jac_hbm.at[:, low:high], jac_ref.at[:, low:high], sems.at[number]
        )
        for number, (low, high) in enumerate(pieces)
    ]
    for number, copy in enumerate(copies):
        copy.start(priority=number % 2)
    energy_copy.wait()
    weight, mean = centred_weight(energy_ref[...])
    msg_ref[0:1, cols : cols + LANES] = mean
    msg_ref[1:2, cols : cols + LANES] = mean
    for copy, (low, high) in zip(copies, pieces):
        copy.wait()
        for at in range(low, high, LANES):
            block = jac_ref[:, at : at + LANES]
            msg_ref[0:1, at : at + LANES] = over_rows(block * weight)
            msg_ref[1:2, at : at + LANES] = over_rows(block)


def back_kernel(jac_ref, *refs):
    part_refs, (msg_ref, norm_ref) = refs[:-2], refs[-2:]
    cols = jac_ref.shape[1]
    total = tree_sum([ref[...] for ref in part_refs])
    norm_ref[...] = total[1:2]
    weight, mean = centred_weight(total[0:1])

    def step(at, carry):
        msg_ref[:, pl.ds(at, LANES)] = over_rows(jac_ref[:, pl.ds(at, LANES)] * weight)
        return carry

    each_tile(cols, step, 0)
    msg_ref[:, cols : cols + LANES] = mean
    msg_ref[:, cols + LANES : cols + 2 * LANES] = over_rows(weight * weight)


def mean_offsets(means):
    centre = sum(means) / len(means)
    return [mean - centre for mean in means]


def square_total(offsets, squares, rows):
    return sum(squares) + rows * sum([offset * offset for offset in offsets])


def offset_term(offsets, sums):
    if len(sums) == 2:
        return offsets[0] * (sums[0] - sums[1])
    return sum([offset * term for offset, term in zip(offsets, sums)])


def project(jac_ref, firsts, msgs, offsets, scale, olds, vector_ref, part_ref):
    rows, cols = jac_ref.shape

    def step(at, carry):
        acc, square = carry
        value = sum([load_tile(ref, 0, at) for ref in msgs])
        value = value + offset_term(offsets, [load_tile(ref, 1, at) for ref in firsts])
        value = value * scale
        for factor, ref in olds:
            value = value - factor * load_tile(ref, 0, at)
        vector_ref[:, pl.ds(at, LANES)] = value
        return acc + jac_ref[:, pl.ds(at, LANES)] * value, square + value * value

    zeros = jnp.zeros((rows, LANES), jnp.float32), jnp.zeros((1, LANES), jnp.float32)
    acc, square = each_tile(cols, step, zeros)
    lines = jnp.concatenate([over_rows(jnp.transpose(acc)), over_lanes(square)], axis=0)
    part_ref[...] = jnp.broadcast_to(lines, part_ref.shape)


def project_zero(walkers, jac_ref, *refs):
    firsts, (vector_ref, part_ref) = refs[:-2], refs[-2:]
    cols = jac_ref.shape[1]
    offsets = mean_offsets([ref[0:1, cols : cols + LANES] for ref in firsts])
    scale = jnp.full((1, LANES), 1.0 / walkers, jnp.float32)
    project(jac_ref, firsts, firsts, offsets, scale, [], vector_ref, part_ref)


def message_scalars(msgs, rows, cols):
    offsets = mean_offsets([ref[:, cols : cols + LANES] for ref in msgs])
    squares = [ref[:, cols + LANES : cols + 2 * LANES] for ref in msgs]
    return offsets, square_total(offsets, squares, rows)


def project_one(groups, walkers, jac_ref, *refs):
    firsts, msgs, refs = refs[:groups], refs[groups : 2 * groups], refs[2 * groups :]
    norm_ref, old_ref, vector_ref, part_ref, state_ref = refs
    offsets, square = message_scalars(msgs, *jac_ref.shape)
    alpha = square / (walkers * jnp.maximum(norm_ref[...], TINY))
    scale = 1.0 / (walkers * jnp.maximum(alpha, TINY))
    state_ref[0:1] = alpha
    state_ref[1:2] = scale
    one = jnp.ones((1, LANES), jnp.float32)
    project(jac_ref, firsts, msgs, offsets, scale, [(one, old_ref)], vector_ref, part_ref)


def project_two(groups, jac_ref, *refs):
    firsts, msgs, refs = refs[:groups], refs[groups : 2 * groups], refs[2 * groups :]
    state_ref, norm_old, norm_now, older_ref, old_ref, vector_ref, part_ref, alpha_ref = refs
    offsets, square = message_scalars(msgs, *jac_ref.shape)
    scale = state_ref[1:2]
    alpha = square * scale / jnp.maximum(norm_now[...], TINY)
    alpha_ref[...] = alpha
    beta = norm_now[...] / jnp.maximum(norm_old[...], TINY)
    olds = [(alpha, old_ref), (beta, older_ref)]
    project(jac_ref, firsts, msgs, offsets, scale, olds, vector_ref, part_ref)


def final_kernel(groups, params, *refs):
    refs, vectors, (out_ref, held_ref, sems) = refs[:-6], refs[-6:-3], refs[-3:]
    sent_ref, (shift_ref, state_ref, alpha_ref, norm0_ref, norm1_ref) = refs[0], refs[1:]
    cols = out_ref.shape[1]
    shards = sent_ref.shape[0] // groups
    sums = [
        jnp.sum(sent_ref[at : at + shards], axis=0) for at in range(0, groups * shards, shards)
    ]
    lines = [total[0:1] for total in sums]
    rows = lines[0].shape[1]
    means = [over_lanes(line) / rows for line in lines]
    devs = [line - mean for line, mean in zip(lines, means)]
    squares = [over_lanes(dev * dev) for dev in devs]
    square = square_total(mean_offsets(means), squares, rows)
    norm0, norm1, norm2 = norm0_ref[...], norm1_ref[...], sums[0][1:2]
    alpha0, scale, alpha1 = state_ref[0:1], state_ref[1:2], alpha_ref[...]
    alpha2 = square * (scale / jnp.maximum(norm2, TINY))
    beta1 = norm1 / jnp.maximum(norm0, TINY)
    beta2 = norm2 / jnp.maximum(norm1, TINY)
    inverse = 1.0 / jnp.maximum(alpha0, TINY)
    shift = shift_ref[...] * inverse
    over0 = 1.0 / (1.0 + shift)
    over1 = 1.0 / ((alpha1 + shift) - beta1 * over0)
    over2 = 1.0 / ((alpha2 + shift) - beta2 * over1)
    coef2 = over0 * over1 * over2
    coef1 = -(over0 + beta2 * coef2) * over1
    coef0 = (1.0 - beta1 * coef1) * over0
    coefs = [coef0 * inverse, coef1 * inverse, coef2 * inverse]
    square = sum([coef * coef * norm for coef, norm in zip(coefs, (norm0, norm1, norm2))])
    factor = lax.rsqrt(square / params + epsilon)
    coefs = [coef * factor for coef in coefs]

    pieces = cut(cols // LANES, PIECES)
    copies = []
    for number, (low, high) in enumerate(pieces):
        for at in range(low, high, LANES):
            terms = [coef * load_tile(ref, 0, at) for coef, ref in zip(coefs, vectors)]
            held_ref[:, at : at + LANES] = terms[0] + terms[1] + terms[2]
        copies.append(
            pltpu.make_async_copy(
                held_ref.at[:, low:high], out_ref.at[:, low:high], sems.at[number]
            )
        )
        copies[-1].start()
    for copy in copies:
        copy.wait()


def call(kernel, outs, *args, spaces=None, out_space=pltpu.VMEM, scratch=()):
    shapes = [
        jax.ShapeDtypeStruct(out, jnp.float32) if isinstance(out, tuple) else out for out in outs
    ]
    space = pl.BlockSpec(memory_space=pltpu.VMEM)
    return pl.pallas_call(
        kernel,
        out_shape=shapes,
        in_specs=spaces or [space] * len(args),
        out_specs=[pl.BlockSpec(memory_space=out_space)] * len(shapes),
        scratch_shapes=scratch,
        compiler_params=pltpu.CompilerParams(vmem_limit_bytes=24 * 1024 * 1024),
    )(*args)


def from_walk(array, groups):
    others = []
    for hop in range(1, groups):
        pairs = [(index, (index - hop) % groups) for index in range(groups)]
        others.append(lax.ppermute(array, "walk", pairs))
    return [array] + others


def across(array, size, masks):
    out = [array]
    for mask in masks:
        pairs = [(index, index ^ mask) for index in range(size)]
        out.append(lax.ppermute(array, "param", pairs))
    return out


def masks_of(stride, radix, order):
    flip = 1 if stride > 1 else 0
    masks = [step * stride ^ flip for step in range(radix - 1, 0, -1)]
    return [masks[at] for at in order] if radix == 4 else masks


def param_parts(array, size, order=(0, 1, 2)):
    stride = 1
    while size > stride:
        radix = 4 if size // stride % 4 == 0 else 2
        parts = across(array, size, masks_of(stride, radix, order if stride == 1 else (0, 1, 2)))
        stride *= radix
        if stride == size:
            return parts
        array = tree_sum(parts)
    return [array]


def body(jacobian, energies, shifts):
    rows, cols = jacobian.shape
    groups, shards = lax.axis_size("walk"), lax.axis_size("param")
    walkers, params = rows * groups, cols * shards
    vector, part, scalar = (1, cols), (2, LANES), (1, LANES)
    msg_shape = (1, cols + 2 * LANES)
    shift_rows = jnp.broadcast_to(shifts[:, None], (shifts.shape[0], LANES))

    jacobian, msg = call(
        first_kernel,
        [pltpu.VMEM((rows, cols), jnp.float32), (2, cols + LANES)],
        pltpu.with_memory_space_constraint(jacobian, pltpu.HBM),
        pltpu.with_memory_space_constraint(energies.reshape(1, rows), pltpu.HBM),
        spaces=[pl.BlockSpec(memory_space=pltpu.HBM)] * 2,
        scratch=[
            pltpu.VMEM((1, rows), jnp.float32),
            pltpu.SemaphoreType.DMA((CHUNKS,)),
            pltpu.SemaphoreType.DMA(()),
        ],
    )
    firsts = from_walk(msg, groups)
    vector0, sent = call(
        functools.partial(project_zero, walkers), [vector, part], jacobian, *firsts
    )
    parts = param_parts(sent, shards)
    msg, norm0 = call(back_kernel, [msg_shape, scalar], jacobian, *parts)
    msgs = from_walk(msg, groups)
    vector1, sent, state = call(
        functools.partial(project_one, groups, walkers),
        [vector, part, (2, LANES)],
        jacobian,
        *firsts,
        *msgs,
        norm0,
        vector0,
    )
    parts = param_parts(sent, shards, (1, 2, 0))
    msg, norm1 = call(back_kernel, [msg_shape, scalar], jacobian, *parts)
    msgs = from_walk(msg, groups)
    vector2, sent, alpha1 = call(
        functools.partial(project_two, groups),
        [vector, (groups * shards,) + part, scalar],
        jacobian,
        *firsts,
        *msgs,
        state,
        norm0,
        norm1,
        vector0,
        vector1,
    )
    (update,) = call(
        functools.partial(final_kernel, groups, params),
        [(shifts.shape[0], cols)],
        lax.all_to_all(sent, ("walk", "param"), 0, 0, tiled=True),
        shift_rows,
        state,
        alpha1,
        norm0,
        norm1,
        vector0,
        vector1,
        vector2,
        out_space=pltpu.HBM,
        scratch=[
            pltpu.VMEM((shifts.shape[0], cols), jnp.float32),
            pltpu.SemaphoreType.DMA((PIECES,)),
        ],
    )
    return update


def solution(mesh):
    return jax.shard_map(
        body,
        mesh=mesh,
        in_specs=(P("walk", "param"), P("walk"), P()),
        out_specs=P(None, "param"),
        check_vma=False,
    )
```

```python
import functools

import jax
import jax.numpy as jnp
from jax import lax
from jax.experimental import pallas as pl
from jax.experimental.pallas import tpu as pltpu
from jax.sharding import PartitionSpec as P

LANES = 128
TINY = 1e-37
CHUNKS = 8
PIECES = 3
GROUP = 8
epsilon = 1e-06


def tree_sum(terms):
    terms = list(terms)
    while len(terms) > 1:
        odd = terms[len(terms) // 2 * 2 :]
        terms = [a + b for a, b in zip(terms[0::2], terms[1::2])] + odd
    return terms[0]


def over_lanes(values):
    total = jnp.sum(values, axis=1, keepdims=True)
    return jnp.broadcast_to(total, (values.shape[0], LANES))


def over_rows(values):
    return jnp.sum(values, axis=0, keepdims=True)


def down_rows(row):
    return jnp.transpose(jnp.broadcast_to(row, (row.shape[1], row.shape[1])))


def centred_weight(row):
    weight = down_rows(row)
    mean = over_rows(weight) / row.shape[1]
    return weight - mean, mean


def each_tile(cols, step, carry):
    count = cols // LANES

    def run(number, carry):
        for part in range(GROUP):
            at = pl.multiple_of((number * GROUP + part) * LANES, LANES)
            carry = step(at, carry)
        return carry

    carry = lax.fori_loop(0, count // GROUP, run, carry)
    for number in range(count // GROUP * GROUP, count):
        carry = step(number * LANES, carry)
    return carry


def cut(count, pieces):
    edges = [count * number // pieces for number in range(pieces + 1)]
    return [(low * LANES, high * LANES) for low, high in zip(edges, edges[1:]) if high > low]


def load_tile(ref, row, at):
    return ref[row : row + 1, pl.ds(at, LANES)]


def first_kernel(jac_hbm, energy_hbm, jac_ref, msg_ref, energy_ref, sems, energy_sem):
    cols = jac_ref.shape[1]
    pieces = cut(cols // LANES, CHUNKS)
    energy_copy = pltpu.make_async_copy(energy_hbm, energy_ref, energy_sem)
    energy_copy.start()
    rows = jac_ref.shape[0]
    halves = [(0, rows // 2), (rows // 2, rows)]
    copies = [
        [
            pltpu.make_async_copy(
                jac_hbm.at[top:end, low:high],
                jac_ref.at[top:end, low:high],
                sems.at[number, half],
            )
            for half, (top, end) in enumerate(halves)
        ]
        for number, (low, high) in enumerate(pieces)
    ]
    for pair in copies:
        for half, copy in enumerate(pair):
            copy.start(priority=half)
    energy_copy.wait()
    weight, mean = centred_weight(energy_ref[...])
    msg_ref[0:1, cols : cols + LANES] = mean
    msg_ref[1:2, cols : cols + LANES] = mean
    for pair, (low, high) in zip(copies, pieces):
        for copy in pair:
            copy.wait()
        for at in range(low, high, LANES):
            block = jac_ref[:, at : at + LANES]
            msg_ref[0:1, at : at + LANES] = over_rows(block * weight)
            msg_ref[1:2, at : at + LANES] = over_rows(block)


def back_kernel(jac_ref, *refs):
    part_refs, (msg_ref, norm_ref) = refs[:-2], refs[-2:]
    cols = jac_ref.shape[1]
    total = tree_sum([ref[...] for ref in part_refs])
    if total.ndim == 3:
        total = jnp.sum(total, axis=0)
    norm_ref[...] = total[1:2]
    weight, mean = centred_weight(total[0:1])

    def step(at, carry):
        msg_ref[:, pl.ds(at, LANES)] = over_rows(jac_ref[:, pl.ds(at, LANES)] * weight)
        return carry

    each_tile(cols, step, 0)
    msg_ref[:, cols : cols + LANES] = mean
    msg_ref[:, cols + LANES : cols + 2 * LANES] = over_rows(weight * weight)


def mean_offsets(means):
    centre = sum(means) / len(means)
    return [mean - centre for mean in means]


def square_total(offsets, squares, rows):
    return sum(squares) + rows * sum([offset * offset for offset in offsets])


def offset_term(offsets, sums):
    if len(sums) == 2:
        return offsets[0] * (sums[0] - sums[1])
    return sum([offset * term for offset, term in zip(offsets, sums)])


def project(jac_ref, firsts, msgs, offsets, scale, olds, vector_ref, part_ref):
    rows, cols = jac_ref.shape

    def step(at, carry):
        acc, square = carry
        value = sum([load_tile(ref, 0, at) for ref in msgs])
        value = value + offset_term(offsets, [load_tile(ref, 1, at) for ref in firsts])
        value = value * scale
        for factor, ref in olds:
            value = value - factor * load_tile(ref, 0, at)
        vector_ref[:, pl.ds(at, LANES)] = value
        return acc + jac_ref[:, pl.ds(at, LANES)] * value, square + value * value

    zeros = jnp.zeros((rows, LANES), jnp.float32), jnp.zeros((1, LANES), jnp.float32)
    acc, square = each_tile(cols, step, zeros)
    lines = jnp.concatenate([over_rows(jnp.transpose(acc)), over_lanes(square)], axis=0)
    part_ref[...] = jnp.broadcast_to(lines, part_ref.shape)


def project_zero(walkers, jac_ref, *refs):
    firsts, (vector_ref, part_ref) = refs[:-2], refs[-2:]
    cols = jac_ref.shape[1]
    offsets = mean_offsets([ref[0:1, cols : cols + LANES] for ref in firsts])
    scale = jnp.full((1, LANES), 1.0 / walkers, jnp.float32)
    project(jac_ref, firsts, firsts, offsets, scale, [], vector_ref, part_ref)


def message_scalars(msgs, rows, cols):
    offsets = mean_offsets([ref[:, cols : cols + LANES] for ref in msgs])
    squares = [ref[:, cols + LANES : cols + 2 * LANES] for ref in msgs]
    return offsets, square_total(offsets, squares, rows)


def project_one(groups, walkers, jac_ref, *refs):
    firsts, msgs, refs = refs[:groups], refs[groups : 2 * groups], refs[2 * groups :]
    norm_ref, old_ref, vector_ref, part_ref, state_ref = refs
    offsets, square = message_scalars(msgs, *jac_ref.shape)
    alpha = square / (walkers * jnp.maximum(norm_ref[...], TINY))
    scale = 1.0 / (walkers * jnp.maximum(alpha, TINY))
    state_ref[0:1] = alpha
    state_ref[1:2] = scale
    one = jnp.ones((1, LANES), jnp.float32)
    project(jac_ref, firsts, msgs, offsets, scale, [(one, old_ref)], vector_ref, part_ref)


def project_two(groups, jac_ref, *refs):
    firsts, msgs, refs = refs[:groups], refs[groups : 2 * groups], refs[2 * groups :]
    state_ref, norm_old, norm_now, older_ref, old_ref, vector_ref, part_ref, alpha_ref = refs
    offsets, square = message_scalars(msgs, *jac_ref.shape)
    scale = state_ref[1:2]
    alpha = square * scale / jnp.maximum(norm_now[...], TINY)
    alpha_ref[...] = alpha
    beta = norm_now[...] / jnp.maximum(norm_old[...], TINY)
    olds = [(alpha, old_ref), (beta, older_ref)]
    project(jac_ref, firsts, msgs, offsets, scale, olds, vector_ref, part_ref)


def final_kernel(groups, params, *refs):
    refs, vectors, (out_ref, held_ref, sems) = refs[:-6], refs[-6:-3], refs[-3:]
    sent_ref, (shift_ref, state_ref, alpha_ref, norm0_ref, norm1_ref) = refs[0], refs[1:]
    cols = out_ref.shape[1]
    shards = sent_ref.shape[0] // groups
    sums = [
        jnp.sum(sent_ref[at : at + shards], axis=0) for at in range(0, groups * shards, shards)
    ]
    lines = [total[0:1] for total in sums]
    rows = lines[0].shape[1]
    means = [over_lanes(line) / rows for line in lines]
    devs = [line - mean for line, mean in zip(lines, means)]
    squares = [over_lanes(dev * dev) for dev in devs]
    square = square_total(mean_offsets(means), squares, rows)
    norm0, norm1, norm2 = norm0_ref[...], norm1_ref[...], sums[0][1:2]
    alpha0, scale, alpha1 = state_ref[0:1], state_ref[1:2], alpha_ref[...]
    alpha2 = square * (scale / jnp.maximum(norm2, TINY))
    beta1 = norm1 / jnp.maximum(norm0, TINY)
    beta2 = norm2 / jnp.maximum(norm1, TINY)
    inverse = 1.0 / jnp.maximum(alpha0, TINY)
    shift = shift_ref[...] * inverse
    over0 = 1.0 / (1.0 + shift)
    over1 = 1.0 / ((alpha1 + shift) - beta1 * over0)
    over2 = 1.0 / ((alpha2 + shift) - beta2 * over1)
    coef2 = over0 * over1 * over2
    coef1 = -(over0 + beta2 * coef2) * over1
    coef0 = (1.0 - beta1 * coef1) * over0
    coefs = [coef0 * inverse, coef1 * inverse, coef2 * inverse]
    square = sum([coef * coef * norm for coef, norm in zip(coefs, (norm0, norm1, norm2))])
    factor = lax.rsqrt(square / params + epsilon)
    coefs = [coef * factor for coef in coefs]

    pieces = cut(cols // LANES, PIECES)
    copies = []
    for number, (low, high) in enumerate(pieces):
        for at in range(low, high, LANES):
            terms = [coef * load_tile(ref, 0, at) for coef, ref in zip(coefs, vectors)]
            held_ref[:, at : at + LANES] = terms[0] + terms[1] + terms[2]
        copies.append(
            pltpu.make_async_copy(
                held_ref.at[:, low:high], out_ref.at[:, low:high], sems.at[number]
            )
        )
        copies[-1].start()
    for copy in copies:
        copy.wait()


def call(kernel, outs, *args, spaces=None, out_space=pltpu.VMEM, scratch=()):
    shapes = [
        jax.ShapeDtypeStruct(out, jnp.float32) if isinstance(out, tuple) else out for out in outs
    ]
    space = pl.BlockSpec(memory_space=pltpu.VMEM)
    return pl.pallas_call(
        kernel,
        out_shape=shapes,
        in_specs=spaces or [space] * len(args),
        out_specs=[pl.BlockSpec(memory_space=out_space)] * len(shapes),
        scratch_shapes=scratch,
        compiler_params=pltpu.CompilerParams(vmem_limit_bytes=24 * 1024 * 1024),
    )(*args)


def from_walk(array, groups):
    others = []
    for hop in range(1, groups):
        pairs = [(index, (index - hop) % groups) for index in range(groups)]
        others.append(lax.ppermute(array, "walk", pairs))
    return [array] + others


def across(array, size, masks):
    out = [array]
    for mask in masks:
        pairs = [(index, index ^ mask) for index in range(size)]
        out.append(lax.ppermute(array, "param", pairs))
    return out


def masks_of(stride, radix, order):
    flip = 1 if stride > 1 else 0
    masks = [step * stride ^ flip for step in range(radix - 1, 0, -1)]
    return [masks[at] for at in order] if radix == 4 else masks


def param_parts(array, size, order=(0, 1, 2)):
    stride = 1
    while size > stride:
        radix = 4 if size // stride % 4 == 0 else 2
        parts = across(array, size, masks_of(stride, radix, order if stride == 1 else (0, 1, 2)))
        stride *= radix
        if stride == size:
            return parts
        array = tree_sum(parts)
    return [array]


def body(jacobian, energies, shifts):
    rows, cols = jacobian.shape
    groups, shards = lax.axis_size("walk"), lax.axis_size("param")
    walkers, params = rows * groups, cols * shards
    vector, part, scalar = (1, cols), (2, LANES), (1, LANES)
    msg_shape = (1, cols + 2 * LANES)
    shift_rows = jnp.broadcast_to(shifts[:, None], (shifts.shape[0], LANES))

    jacobian, msg = call(
        first_kernel,
        [pltpu.VMEM((rows, cols), jnp.float32), (2, cols + LANES)],
        pltpu.with_memory_space_constraint(jacobian, pltpu.HBM),
        pltpu.with_memory_space_constraint(energies.reshape(1, rows), pltpu.HBM),
        spaces=[pl.BlockSpec(memory_space=pltpu.HBM)] * 2,
        scratch=[
            pltpu.VMEM((1, rows), jnp.float32),
            pltpu.SemaphoreType.DMA((CHUNKS, 2)),
            pltpu.SemaphoreType.DMA(()),
        ],
    )
    firsts = from_walk(msg, groups)
    vector0, sent = call(
        functools.partial(project_zero, walkers), [vector, part], jacobian, *firsts
    )
    parts = param_parts(sent, shards)
    msg, norm0 = call(back_kernel, [msg_shape, scalar], jacobian, *parts)
    msgs = from_walk(msg, groups)
    vector1, sent, state = call(
        functools.partial(project_one, groups, walkers),
        [vector, (shards,) + part, (2, LANES)],
        jacobian,
        *firsts,
        *msgs,
        norm0,
        vector0,
    )
    parts = lax.all_to_all(sent, "param", 0, 0, tiled=True)
    msg, norm1 = call(back_kernel, [msg_shape, scalar], jacobian, parts)
    msgs = from_walk(msg, groups)
    vector2, sent, alpha1 = call(
        functools.partial(project_two, groups),
        [vector, (groups * shards,) + part, scalar],
        jacobian,
        *firsts,
        *msgs,
        state,
        norm0,
        norm1,
        vector0,
        vector1,
    )
    (update,) = call(
        functools.partial(final_kernel, groups, params),
        [(shifts.shape[0], cols)],
        lax.all_to_all(sent, ("walk", "param"), 0, 0, tiled=True),
        shift_rows,
        state,
        alpha1,
        norm0,
        norm1,
        vector0,
        vector1,
        vector2,
        out_space=pltpu.HBM,
        scratch=[
            pltpu.VMEM((shifts.shape[0], cols), jnp.float32),
            pltpu.SemaphoreType.DMA((PIECES,)),
        ],
    )
    return update


def solution(mesh):
    return jax.shard_map(
        body,
        mesh=mesh,
        in_specs=(P("walk", "param"), P("walk"), P()),
        out_specs=P(None, "param"),
        check_vma=False,
    )
```

```python
import functools

import jax
import jax.numpy as jnp
from jax import lax
from jax.experimental import pallas as pl
from jax.experimental.pallas import tpu as pltpu
from jax.sharding import PartitionSpec as P

LANES = 128
TINY = 1e-37
CHUNKS = 6
PIECES = 3
GROUP = 37
epsilon = 1e-06


def tree_sum(terms):
    terms = list(terms)
    while len(terms) > 1:
        odd = terms[len(terms) // 2 * 2 :]
        terms = [a + b for a, b in zip(terms[0::2], terms[1::2])] + odd
    return terms[0]


def over_lanes(values):
    total = jnp.sum(values, axis=1, keepdims=True)
    return jnp.broadcast_to(total, (values.shape[0], LANES))


def over_rows(values):
    return jnp.sum(values, axis=0, keepdims=True)


def down_rows(row):
    return jnp.transpose(jnp.broadcast_to(row, (row.shape[1], row.shape[1])))


def centred_weight(row):
    weight = down_rows(row)
    mean = over_rows(weight) / row.shape[1]
    return weight - mean, mean


def each_tile(cols, step, carry):
    count = cols // LANES

    def run(number, carry):
        for part in range(GROUP):
            at = pl.multiple_of((number * GROUP + part) * LANES, LANES)
            carry = step(at, carry)
        return carry

    carry = lax.fori_loop(0, count // GROUP, run, carry)
    for number in range(count // GROUP * GROUP, count):
        carry = step(number * LANES, carry)
    return carry


def cut(count, pieces):
    edges = [count * number // pieces for number in range(pieces + 1)]
    return [(low * LANES, high * LANES) for low, high in zip(edges, edges[1:]) if high > low]


def load_tile(ref, row, at):
    return ref[row : row + 1, pl.ds(at, LANES)]


def first_kernel(jac_hbm, energy_hbm, jac_ref, msg_ref, energy_ref, sems, energy_sem):
    cols = jac_ref.shape[1]
    pieces = cut(cols // LANES, CHUNKS)
    energy_copy = pltpu.make_async_copy(energy_hbm, energy_ref, energy_sem)
    energy_copy.start()
    rows = jac_ref.shape[0]
    halves = [(0, rows // 2), (rows // 2, rows)]
    copies = [
        [
            pltpu.make_async_copy(
                jac_hbm.at[top:end, low:high],
                jac_ref.at[top:end, low:high],
                sems.at[number, half],
            )
            for half, (top, end) in enumerate(halves)
        ]
        for number, (low, high) in enumerate(pieces)
    ]
    for pair in copies:
        for half, copy in enumerate(pair):
            copy.start(priority=half)
    energy_copy.wait()
    weight, mean = centred_weight(energy_ref[...])
    msg_ref[0:1, cols : cols + LANES] = mean
    msg_ref[1:2, cols : cols + LANES] = mean
    for pair, (low, high) in zip(copies, pieces):
        for copy in pair:
            copy.wait()
        for at in range(low, high, LANES):
            block = jac_ref[:, at : at + LANES]
            msg_ref[0:1, at : at + LANES] = over_rows(block * weight)
            msg_ref[1:2, at : at + LANES] = over_rows(block)


def back_kernel(jac_ref, *refs):
    part_refs, (msg_ref, norm_ref) = refs[:-2], refs[-2:]
    cols = jac_ref.shape[1]
    total = tree_sum([ref[...] for ref in part_refs])
    if total.ndim == 3:
        total = jnp.sum(total, axis=0)
    norm_ref[...] = total[1:2]
    weight, mean = centred_weight(total[0:1])

    def step(at, carry):
        msg_ref[:, pl.ds(at, LANES)] = over_rows(jac_ref[:, pl.ds(at, LANES)] * weight)
        return carry

    each_tile(cols, step, 0)
    msg_ref[:, cols : cols + LANES] = mean
    msg_ref[:, cols + LANES : cols + 2 * LANES] = over_rows(weight * weight)


def mean_offsets(means):
    centre = sum(means) / len(means)
    return [mean - centre for mean in means]


def square_total(offsets, squares, rows):
    return sum(squares) + rows * sum([offset * offset for offset in offsets])


def offset_term(offsets, sums):
    if len(sums) == 2:
        return offsets[0] * (sums[0] - sums[1])
    return sum([offset * term for offset, term in zip(offsets, sums)])


def project(jac_ref, firsts, msgs, offsets, scale, olds, vector_ref, part_ref):
    rows, cols = jac_ref.shape

    def step(at, carry):
        acc, square = carry
        value = sum([load_tile(ref, 0, at) for ref in msgs])
        value = value + offset_term(offsets, [load_tile(ref, 1, at) for ref in firsts])
        value = value * scale
        for factor, ref in olds:
            value = value - factor * load_tile(ref, 0, at)
        vector_ref[:, pl.ds(at, LANES)] = value
        return acc + jac_ref[:, pl.ds(at, LANES)] * value, square + value * value

    zeros = jnp.zeros((rows, LANES), jnp.float32), jnp.zeros((1, LANES), jnp.float32)
    acc, square = each_tile(cols, step, zeros)
    lines = jnp.concatenate([over_rows(jnp.transpose(acc)), over_lanes(square)], axis=0)
    part_ref[...] = jnp.broadcast_to(lines, part_ref.shape)


def project_zero(walkers, jac_ref, *refs):
    firsts, (vector_ref, part_ref) = refs[:-2], refs[-2:]
    cols = jac_ref.shape[1]
    offsets = mean_offsets([ref[0:1, cols : cols + LANES] for ref in firsts])
    scale = jnp.full((1, LANES), 1.0 / walkers, jnp.float32)
    project(jac_ref, firsts, firsts, offsets, scale, [], vector_ref, part_ref)


def message_scalars(msgs, rows, cols):
    offsets = mean_offsets([ref[:, cols : cols + LANES] for ref in msgs])
    squares = [ref[:, cols + LANES : cols + 2 * LANES] for ref in msgs]
    return offsets, square_total(offsets, squares, rows)


def project_one(groups, walkers, jac_ref, *refs):
    firsts, msgs, refs = refs[:groups], refs[groups : 2 * groups], refs[2 * groups :]
    norm_ref, old_ref, vector_ref, part_ref, state_ref = refs
    offsets, square = message_scalars(msgs, *jac_ref.shape)
    alpha = square / (walkers * jnp.maximum(norm_ref[...], TINY))
    scale = 1.0 / (walkers * jnp.maximum(alpha, TINY))
    state_ref[0:1] = alpha
    state_ref[1:2] = scale
    one = jnp.ones((1, LANES), jnp.float32)
    project(jac_ref, firsts, msgs, offsets, scale, [(one, old_ref)], vector_ref, part_ref)


def project_two(groups, jac_ref, *refs):
    firsts, msgs, refs = refs[:groups], refs[groups : 2 * groups], refs[2 * groups :]
    state_ref, norm_old, norm_now, older_ref, old_ref, vector_ref, part_ref, alpha_ref = refs
    offsets, square = message_scalars(msgs, *jac_ref.shape)
    scale = state_ref[1:2]
    alpha = square * scale / jnp.maximum(norm_now[...], TINY)
    alpha_ref[...] = alpha
    beta = norm_now[...] / jnp.maximum(norm_old[...], TINY)
    olds = [(alpha, old_ref), (beta, older_ref)]
    project(jac_ref, firsts, msgs, offsets, scale, olds, vector_ref, part_ref)


def final_kernel(groups, params, *refs):
    refs, vectors, (out_ref, held_ref, sems) = refs[:-6], refs[-6:-3], refs[-3:]
    sent_ref, (shift_ref, state_ref, alpha_ref, norm0_ref, norm1_ref) = refs[0], refs[1:]
    cols = out_ref.shape[1]
    shards = sent_ref.shape[0] // groups
    sums = [
        jnp.sum(sent_ref[at : at + shards], axis=0) for at in range(0, groups * shards, shards)
    ]
    lines = [total[0:1] for total in sums]
    rows = lines[0].shape[1]
    means = [over_lanes(line) / rows for line in lines]
    devs = [line - mean for line, mean in zip(lines, means)]
    squares = [over_lanes(dev * dev) for dev in devs]
    square = square_total(mean_offsets(means), squares, rows)
    norm0, norm1, norm2 = norm0_ref[...], norm1_ref[...], sums[0][1:2]
    alpha0, scale, alpha1 = state_ref[0:1], state_ref[1:2], alpha_ref[...]
    alpha2 = square * (scale / jnp.maximum(norm2, TINY))
    beta1 = norm1 / jnp.maximum(norm0, TINY)
    beta2 = norm2 / jnp.maximum(norm1, TINY)
    inverse = 1.0 / jnp.maximum(alpha0, TINY)
    shift = shift_ref[...] * inverse
    over0 = 1.0 / (1.0 + shift)
    over1 = 1.0 / ((alpha1 + shift) - beta1 * over0)
    over2 = 1.0 / ((alpha2 + shift) - beta2 * over1)
    coef2 = over0 * over1 * over2
    coef1 = -(over0 + beta2 * coef2) * over1
    coef0 = (1.0 - beta1 * coef1) * over0
    coefs = [coef0 * inverse, coef1 * inverse, coef2 * inverse]
    square = sum([coef * coef * norm for coef, norm in zip(coefs, (norm0, norm1, norm2))])
    factor = lax.rsqrt(square / params + epsilon)
    coefs = [coef * factor for coef in coefs]

    pieces = cut(cols // LANES, PIECES)
    copies = []
    for number, (low, high) in enumerate(pieces):
        for at in range(low, high, LANES):
            terms = [coef * load_tile(ref, 0, at) for coef, ref in zip(coefs, vectors)]
            held_ref[:, at : at + LANES] = terms[0] + terms[1] + terms[2]
        copies.append(
            pltpu.make_async_copy(
                held_ref.at[:, low:high], out_ref.at[:, low:high], sems.at[number]
            )
        )
        copies[-1].start()
    for copy in copies:
        copy.wait()


def call(kernel, outs, *args, spaces=None, out_space=pltpu.VMEM, scratch=()):
    shapes = [
        jax.ShapeDtypeStruct(out, jnp.float32) if isinstance(out, tuple) else out for out in outs
    ]
    space = pl.BlockSpec(memory_space=pltpu.VMEM)
    return pl.pallas_call(
        kernel,
        out_shape=shapes,
        in_specs=spaces or [space] * len(args),
        out_specs=[pl.BlockSpec(memory_space=out_space)] * len(shapes),
        scratch_shapes=scratch,
        compiler_params=pltpu.CompilerParams(vmem_limit_bytes=24 * 1024 * 1024),
    )(*args)


def from_walk(array, groups):
    others = []
    for hop in range(1, groups):
        pairs = [(index, (index - hop) % groups) for index in range(groups)]
        others.append(lax.ppermute(array, "walk", pairs))
    return [array] + others


def across(array, size, masks):
    out = [array]
    for mask in masks:
        pairs = [(index, index ^ mask) for index in range(size)]
        out.append(lax.ppermute(array, "param", pairs))
    return out


def masks_of(stride, radix, order):
    flip = 1 if stride > 1 else 0
    masks = [step * stride ^ flip for step in range(radix - 1, 0, -1)]
    return [masks[at] for at in order] if radix == 4 else masks


def param_parts(array, size, order=(0, 1, 2)):
    stride = 1
    while size > stride:
        radix = 4 if size // stride % 4 == 0 else 2
        parts = across(array, size, masks_of(stride, radix, order if stride == 1 else (0, 1, 2)))
        stride *= radix
        if stride == size:
            return parts
        array = tree_sum(parts)
    return [array]


def body(jacobian, energies, shifts):
    rows, cols = jacobian.shape
    groups, shards = lax.axis_size("walk"), lax.axis_size("param")
    walkers, params = rows * groups, cols * shards
    vector, part, scalar = (1, cols), (2, LANES), (1, LANES)
    msg_shape = (1, cols + 2 * LANES)
    shift_rows = jnp.broadcast_to(shifts[:, None], (shifts.shape[0], LANES))

    jacobian, msg = call(
        first_kernel,
        [pltpu.VMEM((rows, cols), jnp.float32), (2, cols + LANES)],
        pltpu.with_memory_space_constraint(jacobian, pltpu.HBM),
        pltpu.with_memory_space_constraint(energies.reshape(1, rows), pltpu.HBM),
        spaces=[pl.BlockSpec(memory_space=pltpu.HBM)] * 2,
        scratch=[
            pltpu.VMEM((1, rows), jnp.float32),
            pltpu.SemaphoreType.DMA((CHUNKS, 2)),
            pltpu.SemaphoreType.DMA(()),
        ],
    )
    firsts = from_walk(msg, groups)
    vector0, sent = call(
        functools.partial(project_zero, walkers), [vector, part], jacobian, *firsts
    )
    parts = param_parts(sent, shards)
    msg, norm0 = call(back_kernel, [msg_shape, scalar], jacobian, *parts)
    msgs = from_walk(msg, groups)
    vector1, sent, state = call(
        functools.partial(project_one, groups, walkers),
        [vector, (shards,) + part, (2, LANES)],
        jacobian,
        *firsts,
        *msgs,
        norm0,
        vector0,
    )
    parts = lax.all_to_all(sent, "param", 0, 0, tiled=True)
    msg, norm1 = call(back_kernel, [msg_shape, scalar], jacobian, parts)
    msgs = from_walk(msg, groups)
    vector2, sent, alpha1 = call(
        functools.partial(project_two, groups),
        [vector, (groups * shards,) + part, scalar],
        jacobian,
        *firsts,
        *msgs,
        state,
        norm0,
        norm1,
        vector0,
        vector1,
    )
    (update,) = call(
        functools.partial(final_kernel, groups, params),
        [(shifts.shape[0], cols)],
        lax.all_to_all(sent, ("walk", "param"), 0, 0, tiled=True),
        shift_rows,
        state,
        alpha1,
        norm0,
        norm1,
        vector0,
        vector1,
        vector2,
        out_space=pltpu.HBM,
        scratch=[
            pltpu.VMEM((shifts.shape[0], cols), jnp.float32),
            pltpu.SemaphoreType.DMA((PIECES,)),
        ],
    )
    return update


def solution(mesh):
    return jax.shard_map(
        body,
        mesh=mesh,
        in_specs=(P("walk", "param"), P("walk"), P()),
        out_specs=P(None, "param"),
        check_vma=False,
    )
```

```python
import functools

import jax
import jax.numpy as jnp
from jax import lax
from jax.experimental import pallas as pl
from jax.experimental.pallas import tpu as pltpu
from jax.sharding import PartitionSpec as P

LANES = 128
TINY = 1e-37
CHUNKS = 6
PIECES = 3
epsilon = 1e-06


def tree_sum(terms):
    terms = list(terms)
    while len(terms) > 1:
        odd = terms[len(terms) // 2 * 2 :]
        terms = [a + b for a, b in zip(terms[0::2], terms[1::2])] + odd
    return terms[0]


def over_lanes(values):
    total = jnp.sum(values, axis=1, keepdims=True)
    return jnp.broadcast_to(total, (values.shape[0], LANES))


def over_rows(values):
    return jnp.sum(values, axis=0, keepdims=True)


def down_rows(row):
    return jnp.transpose(jnp.broadcast_to(row, (row.shape[1], row.shape[1])))


def centred_weight(row):
    weight = down_rows(row)
    mean = over_rows(weight) / row.shape[1]
    return weight - mean, mean


def block_rows(cols):
    return -(-(cols // LANES + 2) // 8) * 8


def cut(count, pieces):
    edges = [count * number // pieces for number in range(pieces + 1)]
    return [(low * LANES, high * LANES) for low, high in zip(edges, edges[1:]) if high > low]


def first_kernel(jac_hbm, energy_hbm, jac_ref, msg_ref, energy_ref, sems, energy_sem):
    cols = jac_ref.shape[1]
    pieces = cut(cols // LANES, CHUNKS)
    energy_copy = pltpu.make_async_copy(energy_hbm, energy_ref, energy_sem)
    energy_copy.start()
    rows = jac_ref.shape[0]
    halves = [(0, rows // 2), (rows // 2, rows)]
    copies = [
        [
            pltpu.make_async_copy(
                jac_hbm.at[top:end, low:high],
                jac_ref.at[top:end, low:high],
                sems.at[number, half],
            )
            for half, (top, end) in enumerate(halves)
        ]
        for number, (low, high) in enumerate(pieces)
    ]
    for pair in copies:
        for half, copy in enumerate(pair):
            copy.start(priority=half)
    energy_copy.wait()
    weight, mean = centred_weight(energy_ref[...])
    tiles, below = cols // LANES, block_rows(cols)
    msg_ref[tiles : tiles + 1] = mean
    for pair, (low, high) in zip(copies, pieces):
        for copy in pair:
            copy.wait()
        for at in range(low, high, LANES):
            block = jac_ref[:, at : at + LANES]
            tile = at // LANES
            msg_ref[tile : tile + 1] = over_rows(block * weight)
            msg_ref[below + tile : below + tile + 1] = over_rows(block)


def back_kernel(jac_ref, *refs):
    part_refs, (msg_ref, norm_ref) = refs[:-2], refs[-2:]
    cols = jac_ref.shape[1]
    total = tree_sum([ref[...] for ref in part_refs])
    if total.ndim == 3:
        total = jnp.sum(total, axis=0)
    norm_ref[...] = total[1:2]
    weight, mean = centred_weight(total[0:1])

    tiles = cols // LANES
    for tile in range(tiles):
        block = jac_ref[:, tile * LANES : (tile + 1) * LANES]
        msg_ref[tile : tile + 1] = over_rows(block * weight)
    msg_ref[tiles : tiles + 1] = mean
    msg_ref[tiles + 1 : tiles + 2] = over_rows(weight * weight)


def mean_offsets(means):
    centre = sum(means) / len(means)
    return [mean - centre for mean in means]


def square_total(offsets, squares, rows):
    return sum(squares) + rows * sum([offset * offset for offset in offsets])


def offset_term(offsets, sums):
    if len(sums) == 2:
        return offsets[0] * (sums[0] - sums[1])
    return sum([offset * term for offset, term in zip(offsets, sums)])


def project(jac_ref, firsts, msgs, offsets, scale, olds, vector_ref, part_ref):
    rows, cols = jac_ref.shape
    tiles, below = cols // LANES, block_rows(cols)
    acc, square = jnp.zeros((rows, LANES), jnp.float32), jnp.zeros((1, LANES), jnp.float32)
    for low in range(0, tiles, 8):
        high = min(low + 8, tiles)
        value = sum([ref[low:high] for ref in msgs])
        sums = [ref[below + low : below + high] for ref in firsts]
        value = (value + offset_term(offsets, sums)) * scale
        for factor, ref in olds:
            value = value - factor * ref[low:high]
        vector_ref[low:high] = value
        square = square + over_rows(value * value)
        for tile in range(low, high):
            block = jac_ref[:, tile * LANES : (tile + 1) * LANES]
            acc = acc + block * value[tile - low : tile - low + 1]
    lines = jnp.concatenate([over_rows(jnp.transpose(acc)), over_lanes(square)], axis=0)
    part_ref[...] = jnp.broadcast_to(lines, part_ref.shape)


def project_zero(walkers, jac_ref, *refs):
    firsts, (vector_ref, part_ref) = refs[:-2], refs[-2:]
    tiles = jac_ref.shape[1] // LANES
    offsets = mean_offsets([ref[tiles : tiles + 1] for ref in firsts])
    scale = jnp.full((1, LANES), 1.0 / walkers, jnp.float32)
    project(jac_ref, firsts, firsts, offsets, scale, [], vector_ref, part_ref)


def message_scalars(msgs, rows, cols):
    tiles = cols // LANES
    offsets = mean_offsets([ref[tiles : tiles + 1] for ref in msgs])
    squares = [ref[tiles + 1 : tiles + 2] for ref in msgs]
    return offsets, square_total(offsets, squares, rows)


def project_one(groups, walkers, jac_ref, *refs):
    firsts, msgs, refs = refs[:groups], refs[groups : 2 * groups], refs[2 * groups :]
    norm_ref, old_ref, vector_ref, part_ref, state_ref = refs
    offsets, square = message_scalars(msgs, *jac_ref.shape)
    alpha = square / (walkers * jnp.maximum(norm_ref[...], TINY))
    scale = 1.0 / (walkers * jnp.maximum(alpha, TINY))
    state_ref[0:1] = alpha
    state_ref[1:2] = scale
    one = jnp.ones((1, LANES), jnp.float32)
    project(jac_ref, firsts, msgs, offsets, scale, [(one, old_ref)], vector_ref, part_ref)


def project_two(groups, jac_ref, *refs):
    firsts, msgs, refs = refs[:groups], refs[groups : 2 * groups], refs[2 * groups :]
    state_ref, norm_old, norm_now, older_ref, old_ref, vector_ref, part_ref, alpha_ref = refs
    offsets, square = message_scalars(msgs, *jac_ref.shape)
    scale = state_ref[1:2]
    alpha = square * scale / jnp.maximum(norm_now[...], TINY)
    alpha_ref[...] = alpha
    beta = norm_now[...] / jnp.maximum(norm_old[...], TINY)
    olds = [(alpha, old_ref), (beta, older_ref)]
    project(jac_ref, firsts, msgs, offsets, scale, olds, vector_ref, part_ref)


def final_kernel(groups, params, *refs):
    refs, vectors, (out_ref, held_ref, sems) = refs[:-6], refs[-6:-3], refs[-3:]
    sent_ref, (shift_ref, state_ref, alpha_ref, norm0_ref, norm1_ref) = refs[0], refs[1:]
    cols = out_ref.shape[1]
    shards = sent_ref.shape[0] // groups
    sums = [
        jnp.sum(sent_ref[at : at + shards], axis=0) for at in range(0, groups * shards, shards)
    ]
    lines = [total[0:1] for total in sums]
    rows = lines[0].shape[1]
    means = [over_lanes(line) / rows for line in lines]
    devs = [line - mean for line, mean in zip(lines, means)]
    squares = [over_lanes(dev * dev) for dev in devs]
    square = square_total(mean_offsets(means), squares, rows)
    norm0, norm1, norm2 = norm0_ref[...], norm1_ref[...], sums[0][1:2]
    alpha0, scale, alpha1 = state_ref[0:1], state_ref[1:2], alpha_ref[...]
    alpha2 = square * (scale / jnp.maximum(norm2, TINY))
    beta1 = norm1 / jnp.maximum(norm0, TINY)
    beta2 = norm2 / jnp.maximum(norm1, TINY)
    inverse = 1.0 / jnp.maximum(alpha0, TINY)
    shift = shift_ref[...] * inverse
    over0 = 1.0 / (1.0 + shift)
    over1 = 1.0 / ((alpha1 + shift) - beta1 * over0)
    over2 = 1.0 / ((alpha2 + shift) - beta2 * over1)
    coef2 = over0 * over1 * over2
    coef1 = -(over0 + beta2 * coef2) * over1
    coef0 = (1.0 - beta1 * coef1) * over0
    coefs = [coef0 * inverse, coef1 * inverse, coef2 * inverse]
    square = sum([coef * coef * norm for coef, norm in zip(coefs, (norm0, norm1, norm2))])
    factor = lax.rsqrt(square / params + epsilon)
    coefs = [coef * factor for coef in coefs]

    pieces = cut(cols // LANES, PIECES)
    copies = []
    for number, (low, high) in enumerate(pieces):
        for at in range(low, high, LANES):
            tile = at // LANES
            terms = [coef * ref[tile : tile + 1] for coef, ref in zip(coefs, vectors)]
            held_ref[:, at : at + LANES] = terms[0] + terms[1] + terms[2]
        copies.append(
            pltpu.make_async_copy(
                held_ref.at[:, low:high], out_ref.at[:, low:high], sems.at[number]
            )
        )
        copies[-1].start()
    for copy in copies:
        copy.wait()


def call(kernel, outs, *args, spaces=None, out_space=pltpu.VMEM, scratch=()):
    shapes = [
        jax.ShapeDtypeStruct(out, jnp.float32) if isinstance(out, tuple) else out for out in outs
    ]
    space = pl.BlockSpec(memory_space=pltpu.VMEM)
    return pl.pallas_call(
        kernel,
        out_shape=shapes,
        in_specs=spaces or [space] * len(args),
        out_specs=[pl.BlockSpec(memory_space=out_space)] * len(shapes),
        scratch_shapes=scratch,
        compiler_params=pltpu.CompilerParams(vmem_limit_bytes=24 * 1024 * 1024),
    )(*args)


def from_walk(array, groups):
    others = []
    for hop in range(1, groups):
        pairs = [(index, (index - hop) % groups) for index in range(groups)]
        others.append(lax.ppermute(array, "walk", pairs))
    return [array] + others


def across(array, size, masks):
    out = [array]
    for mask in masks:
        pairs = [(index, index ^ mask) for index in range(size)]
        out.append(lax.ppermute(array, "param", pairs))
    return out


def masks_of(stride, radix, order):
    flip = 1 if stride > 1 else 0
    masks = [step * stride ^ flip for step in range(radix - 1, 0, -1)]
    return [masks[at] for at in order] if radix == 4 else masks


def param_parts(array, size, order=(0, 1, 2)):
    stride = 1
    while size > stride:
        radix = 4 if size // stride % 4 == 0 else 2
        parts = across(array, size, masks_of(stride, radix, order if stride == 1 else (0, 1, 2)))
        stride *= radix
        if stride == size:
            return parts
        array = tree_sum(parts)
    return [array]


def body(jacobian, energies, shifts):
    rows, cols = jacobian.shape
    groups, shards = lax.axis_size("walk"), lax.axis_size("param")
    walkers, params = rows * groups, cols * shards
    height = block_rows(cols)
    vector, part, scalar = (height, LANES), (2, LANES), (1, LANES)
    msg_shape = (height, LANES)
    shift_rows = jnp.broadcast_to(shifts[:, None], (shifts.shape[0], LANES))

    jacobian, msg = call(
        first_kernel,
        [pltpu.VMEM((rows, cols), jnp.float32), (2 * height, LANES)],
        pltpu.with_memory_space_constraint(jacobian, pltpu.HBM),
        pltpu.with_memory_space_constraint(energies.reshape(1, rows), pltpu.HBM),
        spaces=[pl.BlockSpec(memory_space=pltpu.HBM)] * 2,
        scratch=[
            pltpu.VMEM((1, rows), jnp.float32),
            pltpu.SemaphoreType.DMA((CHUNKS, 2)),
            pltpu.SemaphoreType.DMA(()),
        ],
    )
    firsts = from_walk(msg, groups)
    vector0, sent = call(
        functools.partial(project_zero, walkers), [vector, part], jacobian, *firsts
    )
    parts = param_parts(sent, shards)
    msg, norm0 = call(back_kernel, [msg_shape, scalar], jacobian, *parts)
    msgs = from_walk(msg, groups)
    vector1, sent, state = call(
        functools.partial(project_one, groups, walkers),
        [vector, (shards,) + part, (2, LANES)],
        jacobian,
        *firsts,
        *msgs,
        norm0,
        vector0,
    )
    parts = lax.all_to_all(sent, "param", 0, 0, tiled=True)
    msg, norm1 = call(back_kernel, [msg_shape, scalar], jacobian, parts)
    msgs = from_walk(msg, groups)
    vector2, sent, alpha1 = call(
        functools.partial(project_two, groups),
        [vector, (groups * shards,) + part, scalar],
        jacobian,
        *firsts,
        *msgs,
        state,
        norm0,
        norm1,
        vector0,
        vector1,
    )
    (update,) = call(
        functools.partial(final_kernel, groups, params),
        [(shifts.shape[0], cols)],
        lax.all_to_all(sent, ("walk", "param"), 0, 0, tiled=True),
        shift_rows,
        state,
        alpha1,
        norm0,
        norm1,
        vector0,
        vector1,
        vector2,
        out_space=pltpu.HBM,
        scratch=[
            pltpu.VMEM((shifts.shape[0], cols), jnp.float32),
            pltpu.SemaphoreType.DMA((PIECES,)),
        ],
    )
    return update


def solution(mesh):
    return jax.shard_map(
        body,
        mesh=mesh,
        in_specs=(P("walk", "param"), P("walk"), P()),
        out_specs=P(None, "param"),
        check_vma=False,
    )
```

```python
import functools

import jax
import jax.numpy as jnp
from jax import lax
from jax.experimental import pallas as pl
from jax.experimental.pallas import tpu as pltpu
from jax.sharding import PartitionSpec as P

LANES = 128
TINY = 1e-37
CHUNKS = 6
PIECES = 3
epsilon = 1e-06


def tree_sum(terms):
    terms = list(terms)
    while len(terms) > 1:
        odd = terms[len(terms) // 2 * 2 :]
        terms = [a + b for a, b in zip(terms[0::2], terms[1::2])] + odd
    return terms[0]


def over_lanes(values):
    total = jnp.sum(values, axis=1, keepdims=True)
    return jnp.broadcast_to(total, (values.shape[0], LANES))


def over_rows(values):
    return jnp.sum(values, axis=0, keepdims=True)


def down_rows(row):
    return jnp.transpose(jnp.broadcast_to(row, (row.shape[1], row.shape[1])))


def centred_weight(row):
    weight = down_rows(row)
    mean = over_rows(weight) / row.shape[1]
    return weight - mean, mean


def each_tile(cols, step, carry):
    for at in range(0, cols, LANES):
        carry = step(at, carry)
    return carry


def cut(count, pieces):
    edges = [count * number // pieces for number in range(pieces + 1)]
    return [(low * LANES, high * LANES) for low, high in zip(edges, edges[1:]) if high > low]


def load_tile(ref, row, at):
    return ref[row : row + 1, pl.ds(at, LANES)]


def first_kernel(jac_hbm, energy_hbm, jac_ref, msg_ref, energy_ref, sems, energy_sem):
    cols = jac_ref.shape[1]
    pieces = cut(cols // LANES, CHUNKS)
    energy_copy = pltpu.make_async_copy(energy_hbm, energy_ref, energy_sem)
    energy_copy.start()
    rows = jac_ref.shape[0]
    halves = [(0, rows // 2), (rows // 2, rows)]
    copies = [
        [
            pltpu.make_async_copy(
                jac_hbm.at[top:end, low:high],
                jac_ref.at[top:end, low:high],
                sems.at[number, half],
            )
            for half, (top, end) in enumerate(halves)
        ]
        for number, (low, high) in enumerate(pieces)
    ]
    for pair in copies:
        for half, copy in enumerate(pair):
            copy.start(priority=half)
    energy_copy.wait()
    weight, mean = centred_weight(energy_ref[...])
    msg_ref[0:1, cols : cols + LANES] = mean
    msg_ref[1:2, cols : cols + LANES] = mean
    for pair, (low, high) in zip(copies, pieces):
        for copy in pair:
            copy.wait()
        for at in range(low, high, LANES):
            block = jac_ref[:, at : at + LANES]
            msg_ref[0:1, at : at + LANES] = over_rows(block * weight)
            msg_ref[1:2, at : at + LANES] = over_rows(block)


def back_kernel(jac_ref, *refs):
    part_refs, (msg_ref, norm_ref) = refs[:-2], refs[-2:]
    cols = jac_ref.shape[1]
    total = tree_sum([ref[...] for ref in part_refs])
    if total.ndim == 3:
        total = jnp.sum(total, axis=0)
    norm_ref[...] = total[1:2]
    weight, mean = centred_weight(total[0:1])

    def step(at, carry):
        msg_ref[:, pl.ds(at, LANES)] = over_rows(jac_ref[:, pl.ds(at, LANES)] * weight)
        return carry

    each_tile(cols, step, 0)
    msg_ref[:, cols : cols + LANES] = mean
    msg_ref[:, cols + LANES : cols + 2 * LANES] = over_rows(weight * weight)


def mean_offsets(means):
    centre = sum(means) / len(means)
    return [mean - centre for mean in means]


def square_total(offsets, squares, rows):
    return sum(squares) + rows * sum([offset * offset for offset in offsets])


def offset_term(offsets, sums):
    if len(sums) == 2:
        return offsets[0] * (sums[0] - sums[1])
    return sum([offset * term for offset, term in zip(offsets, sums)])


def project(jac_ref, firsts, msgs, offsets, scale, olds, vector_ref, part_ref):
    rows, cols = jac_ref.shape

    def step(at, carry):
        acc, square = carry
        value = sum([load_tile(ref, 0, at) for ref in msgs])
        value = value + offset_term(offsets, [load_tile(ref, 1, at) for ref in firsts])
        value = value * scale
        for factor, ref in olds:
            value = value - factor * load_tile(ref, 0, at)
        vector_ref[:, pl.ds(at, LANES)] = value
        return acc + jac_ref[:, pl.ds(at, LANES)] * value, square + value * value

    zeros = jnp.zeros((rows, LANES), jnp.float32), jnp.zeros((1, LANES), jnp.float32)
    acc, square = each_tile(cols, step, zeros)
    lines = jnp.concatenate([over_rows(jnp.transpose(acc)), over_lanes(square)], axis=0)
    part_ref[...] = jnp.broadcast_to(lines, part_ref.shape)


def project_zero(walkers, jac_ref, *refs):
    firsts, (vector_ref, part_ref) = refs[:-2], refs[-2:]
    cols = jac_ref.shape[1]
    offsets = mean_offsets([ref[0:1, cols : cols + LANES] for ref in firsts])
    scale = jnp.full((1, LANES), 1.0 / walkers, jnp.float32)
    project(jac_ref, firsts, firsts, offsets, scale, [], vector_ref, part_ref)


def message_scalars(msgs, rows, cols):
    offsets = mean_offsets([ref[:, cols : cols + LANES] for ref in msgs])
    squares = [ref[:, cols + LANES : cols + 2 * LANES] for ref in msgs]
    return offsets, square_total(offsets, squares, rows)


def project_one(groups, walkers, jac_ref, *refs):
    firsts, msgs, refs = refs[:groups], refs[groups : 2 * groups], refs[2 * groups :]
    norm_ref, old_ref, vector_ref, part_ref, state_ref = refs
    offsets, square = message_scalars(msgs, *jac_ref.shape)
    alpha = square / (walkers * jnp.maximum(norm_ref[...], TINY))
    scale = 1.0 / (walkers * jnp.maximum(alpha, TINY))
    state_ref[0:1] = alpha
    state_ref[1:2] = scale
    one = jnp.ones((1, LANES), jnp.float32)
    project(jac_ref, firsts, msgs, offsets, scale, [(one, old_ref)], vector_ref, part_ref)


def project_two(groups, jac_ref, *refs):
    firsts, msgs, refs = refs[:groups], refs[groups : 2 * groups], refs[2 * groups :]
    state_ref, norm_old, norm_now, older_ref, old_ref, vector_ref, part_ref, alpha_ref = refs
    offsets, square = message_scalars(msgs, *jac_ref.shape)
    scale = state_ref[1:2]
    alpha = square * scale / jnp.maximum(norm_now[...], TINY)
    alpha_ref[...] = alpha
    beta = norm_now[...] / jnp.maximum(norm_old[...], TINY)
    olds = [(alpha, old_ref), (beta, older_ref)]
    project(jac_ref, firsts, msgs, offsets, scale, olds, vector_ref, part_ref)


def final_kernel(groups, params, *refs):
    refs, vectors, (out_ref, held_ref, sems) = refs[:-6], refs[-6:-3], refs[-3:]
    sent_ref, (shift_ref, state_ref, alpha_ref, norm0_ref, norm1_ref) = refs[0], refs[1:]
    cols = out_ref.shape[1]
    shards = sent_ref.shape[0] // groups
    sums = [
        jnp.sum(sent_ref[at : at + shards], axis=0) for at in range(0, groups * shards, shards)
    ]
    lines = [total[0:1] for total in sums]
    rows = lines[0].shape[1]
    means = [over_lanes(line) / rows for line in lines]
    devs = [line - mean for line, mean in zip(lines, means)]
    squares = [over_lanes(dev * dev) for dev in devs]
    square = square_total(mean_offsets(means), squares, rows)
    norm0, norm1, norm2 = norm0_ref[...], norm1_ref[...], sums[0][1:2]
    alpha0, scale, alpha1 = state_ref[0:1], state_ref[1:2], alpha_ref[...]
    alpha2 = square * (scale / jnp.maximum(norm2, TINY))
    beta1 = norm1 / jnp.maximum(norm0, TINY)
    beta2 = norm2 / jnp.maximum(norm1, TINY)
    inverse = 1.0 / jnp.maximum(alpha0, TINY)
    shift = shift_ref[...] * inverse
    over0 = 1.0 / (1.0 + shift)
    over1 = 1.0 / ((alpha1 + shift) - beta1 * over0)
    over2 = 1.0 / ((alpha2 + shift) - beta2 * over1)
    coef2 = over0 * over1 * over2
    coef1 = -(over0 + beta2 * coef2) * over1
    coef0 = (1.0 - beta1 * coef1) * over0
    coefs = [coef0 * inverse, coef1 * inverse, coef2 * inverse]
    square = sum([coef * coef * norm for coef, norm in zip(coefs, (norm0, norm1, norm2))])
    factor = lax.rsqrt(square / params + epsilon)
    coefs = [coef * factor for coef in coefs]

    pieces = cut(cols // LANES, PIECES)
    copies = []
    for number, (low, high) in enumerate(pieces):
        for at in range(low, high, LANES):
            terms = [coef * load_tile(ref, 0, at) for coef, ref in zip(coefs, vectors)]
            held_ref[:, at : at + LANES] = terms[0] + terms[1] + terms[2]
        copies.append(
            pltpu.make_async_copy(
                held_ref.at[:, low:high], out_ref.at[:, low:high], sems.at[number]
            )
        )
        copies[-1].start()
    for copy in copies:
        copy.wait()


def call(kernel, outs, *args, spaces=None, out_space=pltpu.VMEM, scratch=()):
    shapes = [
        jax.ShapeDtypeStruct(out, jnp.float32) if isinstance(out, tuple) else out for out in outs
    ]
    space = pl.BlockSpec(memory_space=pltpu.VMEM)
    return pl.pallas_call(
        kernel,
        out_shape=shapes,
        in_specs=spaces or [space] * len(args),
        out_specs=[pl.BlockSpec(memory_space=out_space)] * len(shapes),
        scratch_shapes=scratch,
        compiler_params=pltpu.CompilerParams(vmem_limit_bytes=24 * 1024 * 1024),
    )(*args)


def from_walk(array, groups):
    others = []
    for hop in range(1, groups):
        pairs = [(index, (index - hop) % groups) for index in range(groups)]
        others.append(lax.ppermute(array, "walk", pairs))
    return [array] + others


def across(array, size, masks):
    out = [array]
    for mask in masks:
        pairs = [(index, index ^ mask) for index in range(size)]
        out.append(lax.ppermute(array, "param", pairs))
    return out


def masks_of(stride, radix, order):
    flip = 1 if stride > 1 else 0
    masks = [step * stride ^ flip for step in range(radix - 1, 0, -1)]
    return [masks[at] for at in order] if radix == 4 else masks


def param_parts(array, size, order=(0, 1, 2)):
    stride = 1
    while size > stride:
        radix = 4 if size // stride % 4 == 0 else 2
        parts = across(array, size, masks_of(stride, radix, order if stride == 1 else (0, 1, 2)))
        stride *= radix
        if stride == size:
            return parts
        array = tree_sum(parts)
    return [array]


def body(jacobian, energies, shifts):
    rows, cols = jacobian.shape
    groups, shards = lax.axis_size("walk"), lax.axis_size("param")
    walkers, params = rows * groups, cols * shards
    vector, part, scalar = (1, cols), (2, LANES), (1, LANES)
    msg_shape = (1, cols + 2 * LANES)
    shift_rows = jnp.broadcast_to(shifts[:, None], (shifts.shape[0], LANES))

    jacobian, msg = call(
        first_kernel,
        [pltpu.VMEM((rows, cols), jnp.float32), (2, cols + LANES)],
        pltpu.with_memory_space_constraint(jacobian, pltpu.HBM),
        pltpu.with_memory_space_constraint(energies.reshape(1, rows), pltpu.HBM),
        spaces=[pl.BlockSpec(memory_space=pltpu.HBM)] * 2,
        scratch=[
            pltpu.VMEM((1, rows), jnp.float32),
            pltpu.SemaphoreType.DMA((CHUNKS, 2)),
            pltpu.SemaphoreType.DMA(()),
        ],
    )
    firsts = from_walk(msg, groups)
    vector0, sent = call(
        functools.partial(project_zero, walkers), [vector, part], jacobian, *firsts
    )
    parts = param_parts(sent, shards)
    msg, norm0 = call(back_kernel, [msg_shape, scalar], jacobian, *parts)
    msgs = from_walk(msg, groups)
    vector1, sent, state = call(
        functools.partial(project_one, groups, walkers),
        [vector, (shards,) + part, (2, LANES)],
        jacobian,
        *firsts,
        *msgs,
        norm0,
        vector0,
    )
    parts = lax.all_to_all(sent, "param", 0, 0, tiled=True)
    msg, norm1 = call(back_kernel, [msg_shape, scalar], jacobian, parts)
    msgs = from_walk(msg, groups)
    vector2, sent, alpha1 = call(
        functools.partial(project_two, groups),
        [vector, (groups * shards,) + part, scalar],
        jacobian,
        *firsts,
        *msgs,
        state,
        norm0,
        norm1,
        vector0,
        vector1,
    )
    (update,) = call(
        functools.partial(final_kernel, groups, params),
        [(shifts.shape[0], cols)],
        lax.all_to_all(sent, ("walk", "param"), 0, 0, tiled=True),
        shift_rows,
        state,
        alpha1,
        norm0,
        norm1,
        vector0,
        vector1,
        vector2,
        out_space=pltpu.HBM,
        scratch=[
            pltpu.VMEM((shifts.shape[0], cols), jnp.float32),
            pltpu.SemaphoreType.DMA((PIECES,)),
        ],
    )
    return update


def solution(mesh):
    return jax.shard_map(
        body,
        mesh=mesh,
        in_specs=(P("walk", "param"), P("walk"), P()),
        out_specs=P(None, "param"),
        check_vma=False,
    )
```

```python
import functools

import jax
import jax.numpy as jnp
from jax import lax
from jax.experimental import pallas as pl
from jax.experimental.pallas import tpu as pltpu
from jax.sharding import PartitionSpec as P

LANES = 128
TINY = 1e-37
CHUNKS = 6
PIECES = 3
GROUP = 37
epsilon = 1e-06


def tree_sum(terms):
    terms = list(terms)
    while len(terms) > 1:
        odd = terms[len(terms) // 2 * 2 :]
        terms = [a + b for a, b in zip(terms[0::2], terms[1::2])] + odd
    return terms[0]


def over_lanes(values):
    total = jnp.sum(values, axis=1, keepdims=True)
    return jnp.broadcast_to(total, (values.shape[0], LANES))


def over_rows(values):
    return jnp.sum(values, axis=0, keepdims=True)


def down_rows(row):
    return jnp.transpose(jnp.broadcast_to(row, (row.shape[1], row.shape[1])))


def centred_weight(row):
    weight = down_rows(row)
    mean = over_rows(weight) / row.shape[1]
    return weight - mean, mean


def each_tile(cols, step, carry):
    count = cols // LANES

    def run(number, carry):
        for part in range(GROUP):
            at = pl.multiple_of((number * GROUP + part) * LANES, LANES)
            carry = step(at, carry)
        return carry

    carry = lax.fori_loop(0, count // GROUP, run, carry)
    for number in range(count // GROUP * GROUP, count):
        carry = step(number * LANES, carry)
    return carry


def cut(count, pieces):
    edges = [count * number // pieces for number in range(pieces + 1)]
    return [(low * LANES, high * LANES) for low, high in zip(edges, edges[1:]) if high > low]


def load_tile(ref, row, at):
    return ref[row : row + 1, pl.ds(at, LANES)]


def first_kernel(
    jac_hbm, energy_hbm, shift_hbm, jac_ref, msg_ref, rows_ref, energy_ref, shift_ref, sems, small_sems
):
    cols = jac_ref.shape[1]
    pieces = cut(cols // LANES, CHUNKS)
    energy_copy = pltpu.make_async_copy(energy_hbm, energy_ref, small_sems.at[0])
    shift_copy = pltpu.make_async_copy(shift_hbm, shift_ref, small_sems.at[1])
    energy_copy.start()
    shift_copy.start()
    rows = jac_ref.shape[0]
    halves = [(0, rows // 2), (rows // 2, rows)]
    copies = [
        [
            pltpu.make_async_copy(
                jac_hbm.at[top:end, low:high],
                jac_ref.at[top:end, low:high],
                sems.at[number, half],
            )
            for half, (top, end) in enumerate(halves)
        ]
        for number, (low, high) in enumerate(pieces)
    ]
    for pair in copies:
        for half, copy in enumerate(pair):
            copy.start(priority=half)
    energy_copy.wait()
    shift_copy.wait()
    rows_ref[...] = jnp.transpose(
        jnp.broadcast_to(shift_ref[...], (LANES, rows_ref.shape[0]))
    )
    weight, mean = centred_weight(energy_ref[...])
    msg_ref[0:1, cols : cols + LANES] = mean
    msg_ref[1:2, cols : cols + LANES] = mean
    for pair, (low, high) in zip(copies, pieces):
        for copy in pair:
            copy.wait()
        for at in range(low, high, LANES):
            block = jac_ref[:, at : at + LANES]
            msg_ref[0:1, at : at + LANES] = over_rows(block * weight)
            msg_ref[1:2, at : at + LANES] = over_rows(block)


def back_kernel(jac_ref, *refs):
    part_refs, (msg_ref, norm_ref) = refs[:-2], refs[-2:]
    cols = jac_ref.shape[1]
    total = tree_sum([ref[...] for ref in part_refs])
    if total.ndim == 3:
        total = jnp.sum(total, axis=0)
    norm_ref[...] = total[1:2]
    weight, mean = centred_weight(total[0:1])

    def step(at, carry):
        msg_ref[:, pl.ds(at, LANES)] = over_rows(jac_ref[:, pl.ds(at, LANES)] * weight)
        return carry

    for at in range(0, cols, LANES):
        step(at, 0)
    msg_ref[:, cols : cols + LANES] = mean
    msg_ref[:, cols + LANES : cols + 2 * LANES] = over_rows(weight * weight)


def mean_offsets(means):
    centre = sum(means) / len(means)
    return [mean - centre for mean in means]


def square_total(offsets, squares, rows):
    return sum(squares) + rows * sum([offset * offset for offset in offsets])


def offset_term(offsets, sums):
    if len(sums) == 2:
        return offsets[0] * (sums[0] - sums[1])
    return sum([offset * term for offset, term in zip(offsets, sums)])


def project(jac_ref, firsts, msgs, offsets, scale, olds, vector_ref, part_ref):
    rows, cols = jac_ref.shape

    def step(at, carry):
        acc, square = carry
        value = sum([load_tile(ref, 0, at) for ref in msgs])
        value = value + offset_term(offsets, [load_tile(ref, 1, at) for ref in firsts])
        value = value * scale
        for factor, ref in olds:
            value = value - factor * load_tile(ref, 0, at)
        vector_ref[:, pl.ds(at, LANES)] = value
        return acc + jac_ref[:, pl.ds(at, LANES)] * value, square + value * value

    zeros = jnp.zeros((rows, LANES), jnp.float32), jnp.zeros((1, LANES), jnp.float32)
    acc, square = each_tile(cols, step, zeros)
    lines = jnp.concatenate([over_rows(jnp.transpose(acc)), over_lanes(square)], axis=0)
    part_ref[...] = jnp.broadcast_to(lines, part_ref.shape)


def project_zero(walkers, jac_ref, *refs):
    firsts, (vector_ref, part_ref) = refs[:-2], refs[-2:]
    cols = jac_ref.shape[1]
    offsets = mean_offsets([ref[0:1, cols : cols + LANES] for ref in firsts])
    scale = jnp.full((1, LANES), 1.0 / walkers, jnp.float32)
    project(jac_ref, firsts, firsts, offsets, scale, [], vector_ref, part_ref)


def message_scalars(msgs, rows, cols):
    offsets = mean_offsets([ref[:, cols : cols + LANES] for ref in msgs])
    squares = [ref[:, cols + LANES : cols + 2 * LANES] for ref in msgs]
    return offsets, square_total(offsets, squares, rows)


def project_one(groups, walkers, jac_ref, *refs):
    firsts, msgs, refs = refs[:groups], refs[groups : 2 * groups], refs[2 * groups :]
    norm_ref, old_ref, vector_ref, part_ref, state_ref = refs
    offsets, square = message_scalars(msgs, *jac_ref.shape)
    alpha = square / (walkers * jnp.maximum(norm_ref[...], TINY))
    scale = 1.0 / (walkers * jnp.maximum(alpha, TINY))
    state_ref[0:1] = alpha
    state_ref[1:2] = scale
    one = jnp.ones((1, LANES), jnp.float32)
    project(jac_ref, firsts, msgs, offsets, scale, [(one, old_ref)], vector_ref, part_ref)


def project_two(groups, jac_ref, *refs):
    firsts, msgs, refs = refs[:groups], refs[groups : 2 * groups], refs[2 * groups :]
    state_ref, norm_old, norm_now, older_ref, old_ref, vector_ref, part_ref, alpha_ref = refs
    offsets, square = message_scalars(msgs, *jac_ref.shape)
    scale = state_ref[1:2]
    alpha = square * scale / jnp.maximum(norm_now[...], TINY)
    alpha_ref[...] = alpha
    beta = norm_now[...] / jnp.maximum(norm_old[...], TINY)
    olds = [(alpha, old_ref), (beta, older_ref)]
    project(jac_ref, firsts, msgs, offsets, scale, olds, vector_ref, part_ref)


def final_kernel(groups, params, *refs):
    refs, vectors, (out_ref, held_ref, sems) = refs[:-6], refs[-6:-3], refs[-3:]
    sent_ref, (shift_ref, state_ref, alpha_ref, norm0_ref, norm1_ref) = refs[0], refs[1:]
    cols = out_ref.shape[1]
    shards = sent_ref.shape[0] // groups
    sums = [
        jnp.sum(sent_ref[at : at + shards], axis=0) for at in range(0, groups * shards, shards)
    ]
    lines = [total[0:1] for total in sums]
    rows = lines[0].shape[1]
    means = [over_lanes(line) / rows for line in lines]
    devs = [line - mean for line, mean in zip(lines, means)]
    squares = [over_lanes(dev * dev) for dev in devs]
    square = square_total(mean_offsets(means), squares, rows)
    norm0, norm1, norm2 = norm0_ref[...], norm1_ref[...], sums[0][1:2]
    alpha0, scale, alpha1 = state_ref[0:1], state_ref[1:2], alpha_ref[...]
    alpha2 = square * (scale / jnp.maximum(norm2, TINY))
    beta1 = norm1 / jnp.maximum(norm0, TINY)
    beta2 = norm2 / jnp.maximum(norm1, TINY)
    inverse = 1.0 / jnp.maximum(alpha0, TINY)
    shift = shift_ref[...] * inverse
    over0 = 1.0 / (1.0 + shift)
    over1 = 1.0 / ((alpha1 + shift) - beta1 * over0)
    over2 = 1.0 / ((alpha2 + shift) - beta2 * over1)
    coef2 = over0 * over1 * over2
    coef1 = -(over0 + beta2 * coef2) * over1
    coef0 = (1.0 - beta1 * coef1) * over0
    coefs = [coef0 * inverse, coef1 * inverse, coef2 * inverse]
    square = sum([coef * coef * norm for coef, norm in zip(coefs, (norm0, norm1, norm2))])
    factor = lax.rsqrt(square / params + epsilon)
    coefs = [coef * factor for coef in coefs]

    pieces = cut(cols // LANES, PIECES)
    copies = []
    for number, (low, high) in enumerate(pieces):
        for at in range(low, high, LANES):
            terms = [coef * load_tile(ref, 0, at) for coef, ref in zip(coefs, vectors)]
            held_ref[:, at : at + LANES] = terms[0] + terms[1] + terms[2]
        copies.append(
            pltpu.make_async_copy(
                held_ref.at[:, low:high], out_ref.at[:, low:high], sems.at[number]
            )
        )
        copies[-1].start()
    for copy in copies:
        copy.wait()


def call(kernel, outs, *args, spaces=None, out_space=pltpu.VMEM, scratch=()):
    shapes = [
        jax.ShapeDtypeStruct(out, jnp.float32) if isinstance(out, tuple) else out for out in outs
    ]
    space = pl.BlockSpec(memory_space=pltpu.VMEM)
    return pl.pallas_call(
        kernel,
        out_shape=shapes,
        in_specs=spaces or [space] * len(args),
        out_specs=[pl.BlockSpec(memory_space=out_space)] * len(shapes),
        scratch_shapes=scratch,
        compiler_params=pltpu.CompilerParams(vmem_limit_bytes=24 * 1024 * 1024),
    )(*args)


def from_walk(array, groups):
    others = []
    for hop in range(1, groups):
        pairs = [(index, (index - hop) % groups) for index in range(groups)]
        others.append(lax.ppermute(array, "walk", pairs))
    return [array] + others


def across(array, size, masks):
    out = [array]
    for mask in masks:
        pairs = [(index, index ^ mask) for index in range(size)]
        out.append(lax.ppermute(array, "param", pairs))
    return out


def masks_of(stride, radix, order):
    flip = 1 if stride > 1 else 0
    masks = [step * stride ^ flip for step in range(radix - 1, 0, -1)]
    return [masks[at] for at in order] if radix == 4 else masks


def param_parts(array, size, order=(0, 1, 2)):
    stride = 1
    while size > stride:
        radix = 4 if size // stride % 4 == 0 else 2
        parts = across(array, size, masks_of(stride, radix, order if stride == 1 else (0, 1, 2)))
        stride *= radix
        if stride == size:
            return parts
        array = tree_sum(parts)
    return [array]


def body(jacobian, energies, shifts):
    rows, cols = jacobian.shape
    groups, shards = lax.axis_size("walk"), lax.axis_size("param")
    walkers, params = rows * groups, cols * shards
    vector, part, scalar = (1, cols), (2, LANES), (1, LANES)
    msg_shape = (1, cols + 2 * LANES)
    trials = shifts.shape[0]

    jacobian, msg, shift_rows = call(
        first_kernel,
        [pltpu.VMEM((rows, cols), jnp.float32), (2, cols + LANES), (trials, LANES)],
        pltpu.with_memory_space_constraint(jacobian, pltpu.HBM),
        pltpu.with_memory_space_constraint(energies.reshape(1, rows), pltpu.HBM),
        pltpu.with_memory_space_constraint(shifts.reshape(1, trials), pltpu.HBM),
        spaces=[pl.BlockSpec(memory_space=pltpu.HBM)] * 3,
        scratch=[
            pltpu.VMEM((1, rows), jnp.float32),
            pltpu.VMEM((1, trials), jnp.float32),
            pltpu.SemaphoreType.DMA((CHUNKS, 2)),
            pltpu.SemaphoreType.DMA((2,)),
        ],
    )
    firsts = from_walk(msg, groups)
    vector0, sent = call(
        functools.partial(project_zero, walkers), [vector, part], jacobian, *firsts
    )
    parts = param_parts(sent, shards)
    msg, norm0 = call(back_kernel, [msg_shape, scalar], jacobian, *parts)
    msgs = from_walk(msg, groups)
    vector1, sent, state = call(
        functools.partial(project_one, groups, walkers),
        [vector, (shards,) + part, (2, LANES)],
        jacobian,
        *firsts,
        *msgs,
        norm0,
        vector0,
    )
    parts = lax.all_to_all(sent, "param", 0, 0, tiled=True)
    msg, norm1 = call(back_kernel, [msg_shape, scalar], jacobian, parts)
    msgs = from_walk(msg, groups)
    vector2, sent, alpha1 = call(
        functools.partial(project_two, groups),
        [vector, (groups * shards,) + part, scalar],
        jacobian,
        *firsts,
        *msgs,
        state,
        norm0,
        norm1,
        vector0,
        vector1,
    )
    (update,) = call(
        functools.partial(final_kernel, groups, params),
        [(shifts.shape[0], cols)],
        lax.all_to_all(sent, ("walk", "param"), 0, 0, tiled=True),
        shift_rows,
        state,
        alpha1,
        norm0,
        norm1,
        vector0,
        vector1,
        vector2,
        out_space=pltpu.HBM,
        scratch=[
            pltpu.VMEM((shifts.shape[0], cols), jnp.float32),
            pltpu.SemaphoreType.DMA((PIECES,)),
        ],
    )
    return update


def solution(mesh):
    return jax.shard_map(
        body,
        mesh=mesh,
        in_specs=(P("walk", "param"), P("walk"), P()),
        out_specs=P(None, "param"),
        check_vma=False,
    )
```

```python
import functools

import jax
import jax.numpy as jnp
from jax import lax
from jax.experimental import pallas as pl
from jax.experimental.pallas import tpu as pltpu
from jax.sharding import PartitionSpec as P

LANES = 128
TINY = 1e-37
CHUNKS = 6
PIECES = 3
GROUP = 37
epsilon = 1e-06


def tree_sum(terms):
    terms = list(terms)
    while len(terms) > 1:
        odd = terms[len(terms) // 2 * 2 :]
        terms = [a + b for a, b in zip(terms[0::2], terms[1::2])] + odd
    return terms[0]


def over_lanes(values):
    total = jnp.sum(values, axis=1, keepdims=True)
    return jnp.broadcast_to(total, (values.shape[0], LANES))


def over_rows(values):
    return jnp.sum(values, axis=0, keepdims=True)


def down_rows(row):
    return jnp.transpose(jnp.broadcast_to(row, (row.shape[1], row.shape[1])))


def centred_weight(row):
    weight = down_rows(row)
    mean = over_rows(weight) / row.shape[1]
    return weight - mean, mean


def each_tile(cols, step, carry):
    count = cols // LANES

    def run(number, carry):
        for part in range(GROUP):
            at = pl.multiple_of((number * GROUP + part) * LANES, LANES)
            carry = step(at, carry)
        return carry

    carry = lax.fori_loop(0, count // GROUP, run, carry)
    for number in range(count // GROUP * GROUP, count):
        carry = step(number * LANES, carry)
    return carry


def cut(count, pieces):
    edges = [count * number // pieces for number in range(pieces + 1)]
    return [(low * LANES, high * LANES) for low, high in zip(edges, edges[1:]) if high > low]


def load_tile(ref, row, at):
    return ref[row : row + 1, pl.ds(at, LANES)]


def first_kernel(jac_hbm, energy_hbm, jac_ref, msg_ref, energy_ref, sems, energy_sem):
    cols = jac_ref.shape[1]
    pieces = cut(cols // LANES, CHUNKS)
    energy_copy = pltpu.make_async_copy(energy_hbm, energy_ref, energy_sem)
    energy_copy.start()
    rows = jac_ref.shape[0]
    halves = [(0, rows // 2), (rows // 2, rows)]
    copies = [
        [
            pltpu.make_async_copy(
                jac_hbm.at[top:end, low:high],
                jac_ref.at[top:end, low:high],
                sems.at[number, half],
            )
            for half, (top, end) in enumerate(halves)
        ]
        for number, (low, high) in enumerate(pieces)
    ]
    for pair in copies:
        for half, copy in enumerate(pair):
            copy.start(priority=half)
    energy_copy.wait()
    weight, mean = centred_weight(energy_ref[...])
    msg_ref[0:1, cols : cols + LANES] = mean
    msg_ref[1:2, cols : cols + LANES] = mean
    for pair, (low, high) in zip(copies, pieces):
        for copy in pair:
            copy.wait()
        for at in range(low, high, LANES):
            block = jac_ref[:, at : at + LANES]
            msg_ref[0:1, at : at + LANES] = over_rows(block * weight)
            msg_ref[1:2, at : at + LANES] = over_rows(block)


def back_kernel(jac_ref, *refs):
    part_refs, (msg_ref, norm_ref) = refs[:-2], refs[-2:]
    cols = jac_ref.shape[1]
    total = tree_sum([ref[...] for ref in part_refs])
    if total.ndim == 3:
        total = jnp.sum(total, axis=0)
    norm_ref[...] = total[1:2]
    weight, mean = centred_weight(total[0:1])

    def step(at, carry):
        msg_ref[:, pl.ds(at, LANES)] = over_rows(jac_ref[:, pl.ds(at, LANES)] * weight)
        return carry

    for at in range(0, cols, LANES):
        step(at, 0)
    msg_ref[:, cols : cols + LANES] = mean
    msg_ref[:, cols + LANES : cols + 2 * LANES] = over_rows(weight * weight)


def mean_offsets(means):
    centre = sum(means) / len(means)
    return [mean - centre for mean in means]


def square_total(offsets, squares, rows):
    return sum(squares) + rows * sum([offset * offset for offset in offsets])


def offset_term(offsets, sums):
    if len(sums) == 2:
        return offsets[0] * (sums[0] - sums[1])
    return sum([offset * term for offset, term in zip(offsets, sums)])


def project(jac_ref, firsts, msgs, offsets, scale, olds, vector_ref, part_ref):
    rows, cols = jac_ref.shape

    def step(at, carry):
        acc, square = carry
        value = sum([load_tile(ref, 0, at) for ref in msgs])
        value = value + offset_term(offsets, [load_tile(ref, 1, at) for ref in firsts])
        value = value * scale
        for factor, ref in olds:
            value = value - factor * load_tile(ref, 0, at)
        vector_ref[:, pl.ds(at, LANES)] = value
        return acc + jac_ref[:, pl.ds(at, LANES)] * value, square + value * value

    zeros = jnp.zeros((rows, LANES), jnp.float32), jnp.zeros((1, LANES), jnp.float32)
    acc, square = each_tile(cols, step, zeros)
    lines = jnp.concatenate([over_rows(jnp.transpose(acc)), over_lanes(square)], axis=0)
    part_ref[...] = jnp.broadcast_to(lines, part_ref.shape)


def project_zero(walkers, jac_ref, *refs):
    firsts, (vector_ref, part_ref) = refs[:-2], refs[-2:]
    cols = jac_ref.shape[1]
    offsets = mean_offsets([ref[0:1, cols : cols + LANES] for ref in firsts])
    scale = jnp.full((1, LANES), 1.0 / walkers, jnp.float32)
    project(jac_ref, firsts, firsts, offsets, scale, [], vector_ref, part_ref)


def message_scalars(msgs, rows, cols):
    offsets = mean_offsets([ref[:, cols : cols + LANES] for ref in msgs])
    squares = [ref[:, cols + LANES : cols + 2 * LANES] for ref in msgs]
    return offsets, square_total(offsets, squares, rows)


def project_one(groups, walkers, jac_ref, *refs):
    firsts, msgs, refs = refs[:groups], refs[groups : 2 * groups], refs[2 * groups :]
    norm_ref, old_ref, vector_ref, part_ref, state_ref = refs
    offsets, square = message_scalars(msgs, *jac_ref.shape)
    alpha = square / (walkers * jnp.maximum(norm_ref[...], TINY))
    scale = 1.0 / (walkers * jnp.maximum(alpha, TINY))
    state_ref[0:1] = alpha
    state_ref[1:2] = scale
    one = jnp.ones((1, LANES), jnp.float32)
    project(jac_ref, firsts, msgs, offsets, scale, [(one, old_ref)], vector_ref, part_ref)


def project_two(groups, jac_ref, *refs):
    firsts, msgs, refs = refs[:groups], refs[groups : 2 * groups], refs[2 * groups :]
    state_ref, norm_old, norm_now, older_ref, old_ref, vector_ref, part_ref, alpha_ref = refs
    offsets, square = message_scalars(msgs, *jac_ref.shape)
    scale = state_ref[1:2]
    alpha = square * scale / jnp.maximum(norm_now[...], TINY)
    alpha_ref[...] = alpha
    beta = norm_now[...] / jnp.maximum(norm_old[...], TINY)
    olds = [(alpha, old_ref), (beta, older_ref)]
    project(jac_ref, firsts, msgs, offsets, scale, olds, vector_ref, part_ref)


def final_kernel(groups, params, *refs):
    refs, vectors, (out_ref, held_ref, sems) = refs[:-6], refs[-6:-3], refs[-3:]
    sent_ref, (shift_ref, state_ref, alpha_ref, norm0_ref, norm1_ref) = refs[0], refs[1:]
    cols = out_ref.shape[1]
    shards = sent_ref.shape[0] // groups
    sums = [
        jnp.sum(sent_ref[at : at + shards], axis=0) for at in range(0, groups * shards, shards)
    ]
    lines = [total[0:1] for total in sums]
    rows = lines[0].shape[1]
    means = [over_lanes(line) / rows for line in lines]
    devs = [line - mean for line, mean in zip(lines, means)]
    squares = [over_lanes(dev * dev) for dev in devs]
    square = square_total(mean_offsets(means), squares, rows)
    norm0, norm1, norm2 = norm0_ref[...], norm1_ref[...], sums[0][1:2]
    alpha0, scale, alpha1 = state_ref[0:1], state_ref[1:2], alpha_ref[...]
    alpha2 = square * (scale / jnp.maximum(norm2, TINY))
    beta1 = norm1 / jnp.maximum(norm0, TINY)
    beta2 = norm2 / jnp.maximum(norm1, TINY)
    inverse = 1.0 / jnp.maximum(alpha0, TINY)
    shift = shift_ref[...] * inverse
    over0 = 1.0 / (1.0 + shift)
    over1 = 1.0 / ((alpha1 + shift) - beta1 * over0)
    over2 = 1.0 / ((alpha2 + shift) - beta2 * over1)
    coef2 = over0 * over1 * over2
    coef1 = -(over0 + beta2 * coef2) * over1
    coef0 = (1.0 - beta1 * coef1) * over0
    coefs = [coef0 * inverse, coef1 * inverse, coef2 * inverse]
    square = sum([coef * coef * norm for coef, norm in zip(coefs, (norm0, norm1, norm2))])
    factor = lax.rsqrt(square / params + epsilon)
    coefs = [coef * factor for coef in coefs]

    pieces = cut(cols // LANES, PIECES)
    copies = []
    for number, (low, high) in enumerate(pieces):
        for at in range(low, high, LANES):
            terms = [coef * load_tile(ref, 0, at) for coef, ref in zip(coefs, vectors)]
            held_ref[:, at : at + LANES] = terms[0] + terms[1] + terms[2]
        copies.append(
            pltpu.make_async_copy(
                held_ref.at[:, low:high], out_ref.at[:, low:high], sems.at[number]
            )
        )
        copies[-1].start()
    for copy in copies:
        copy.wait()


def call(kernel, outs, *args, spaces=None, out_space=pltpu.VMEM, scratch=()):
    shapes = [
        jax.ShapeDtypeStruct(out, jnp.float32) if isinstance(out, tuple) else out for out in outs
    ]
    space = pl.BlockSpec(memory_space=pltpu.VMEM)
    return pl.pallas_call(
        kernel,
        out_shape=shapes,
        in_specs=spaces or [space] * len(args),
        out_specs=[pl.BlockSpec(memory_space=out_space)] * len(shapes),
        scratch_shapes=scratch,
        compiler_params=pltpu.CompilerParams(vmem_limit_bytes=24 * 1024 * 1024),
    )(*args)


def from_walk(array, groups):
    others = []
    for hop in range(1, groups):
        pairs = [(index, (index - hop) % groups) for index in range(groups)]
        others.append(lax.ppermute(array, "walk", pairs))
    return [array] + others


def across(array, size, masks):
    out = [array]
    for mask in masks:
        pairs = [(index, index ^ mask) for index in range(size)]
        out.append(lax.ppermute(array, "param", pairs))
    return out


def masks_of(stride, radix, order):
    flip = 1 if stride > 1 else 0
    masks = [step * stride ^ flip for step in range(radix - 1, 0, -1)]
    return [masks[at] for at in order] if radix == 4 else masks


def param_parts(array, size, order=(0, 1, 2)):
    stride = 1
    while size > stride:
        radix = 4 if size // stride % 4 == 0 else 2
        parts = across(array, size, masks_of(stride, radix, order if stride == 1 else (0, 1, 2)))
        stride *= radix
        if stride == size:
            return parts
        array = tree_sum(parts)
    return [array]


def body(jacobian, energies, shifts):
    rows, cols = jacobian.shape
    groups, shards = lax.axis_size("walk"), lax.axis_size("param")
    walkers, params = rows * groups, cols * shards
    vector, part, scalar = (1, cols), (2, LANES), (1, LANES)
    msg_shape = (1, cols + 2 * LANES)
    shift_rows = jnp.broadcast_to(shifts[:, None], (shifts.shape[0], LANES))

    jacobian, msg = call(
        first_kernel,
        [pltpu.VMEM((rows, cols), jnp.float32), (2, cols + LANES)],
        pltpu.with_memory_space_constraint(jacobian, pltpu.HBM),
        pltpu.with_memory_space_constraint(energies.reshape(1, rows), pltpu.HBM),
        spaces=[pl.BlockSpec(memory_space=pltpu.HBM)] * 2,
        scratch=[
            pltpu.VMEM((1, rows), jnp.float32),
            pltpu.SemaphoreType.DMA((CHUNKS, 2)),
            pltpu.SemaphoreType.DMA(()),
        ],
    )
    firsts = from_walk(msg, groups)
    vector0, sent = call(
        functools.partial(project_zero, walkers), [vector, part], jacobian, *firsts
    )
    parts = param_parts(sent, shards)
    msg, norm0 = call(back_kernel, [msg_shape, scalar], jacobian, *parts)
    msgs = from_walk(msg, groups)
    vector1, sent, state = call(
        functools.partial(project_one, groups, walkers),
        [vector, (shards,) + part, (2, LANES)],
        jacobian,
        *firsts,
        *msgs,
        norm0,
        vector0,
    )
    parts = lax.all_to_all(sent, "param", 0, 0, tiled=True)
    msg, norm1 = call(back_kernel, [msg_shape, scalar], jacobian, parts)
    msgs = from_walk(msg, groups)
    vector2, sent, alpha1 = call(
        functools.partial(project_two, groups),
        [vector, (groups * shards,) + part, scalar],
        jacobian,
        *firsts,
        *msgs,
        state,
        norm0,
        norm1,
        vector0,
        vector1,
    )
    (update,) = call(
        functools.partial(final_kernel, groups, params),
        [(shifts.shape[0], cols)],
        lax.all_to_all(sent, ("walk", "param"), 0, 0, tiled=True),
        shift_rows,
        state,
        alpha1,
        norm0,
        norm1,
        vector0,
        vector1,
        vector2,
        out_space=pltpu.HBM,
        scratch=[
            pltpu.VMEM((shifts.shape[0], cols), jnp.float32),
            pltpu.SemaphoreType.DMA((PIECES,)),
        ],
    )
    return update


def solution(mesh):
    return jax.shard_map(
        body,
        mesh=mesh,
        in_specs=(P("walk", "param"), P("walk"), P()),
        out_specs=P(None, "param"),
        check_vma=False,
    )
```
